32 devices in a mesh: seq: 4 (over y, x), batch: 8 (over z, core).
Axes of the slice: x: 2, y: 2, z: 4, core: 2. Of those that a mesh axis runs over, the one named last changes fastest.
Arguments:
- tokens: bfloat16 [8, 2048, 768], P('batch', 'seq'), may hold values from -6 to 6
- segment_ids: int32 [8, 2048], P('batch', 'seq'), may hold values from 0 to 10, as said below
- span_starts: int32 [8, 32], P('batch', 'seq'), may hold values from 0 to 1, as said below
- first_gain: float32 [768], replicated, may hold values from 0.5 to 1.5
- first_shift: float32 [768], replicated, may hold values from -3 to 3
- second_gain: float32 [768], replicated, may hold values from 0.5 to 1.5
- second_shift: float32 [768], replicated, may hold values from -3 to 3
- input_weight: bfloat16 [768, 2304], replicated, may hold values from -0.21875 to 0.21875
- input_bias: float32 [2304], replicated, may hold values from -3 to 3
- feature_freq: float32 [64, 64], replicated, may hold values from -4 to 4
- feature_weight: float32 [12, 64], replicated, may hold values from 0.5 to 2
- output_weight: bfloat16 [768, 768], replicated, may hold values from -1.75 to 1.75
- output_bias: float32 [768], replicated, may hold values from -3 to 3
- up_weight: bfloat16 [768, 3072], replicated, may hold values from -0.21875 to 0.21875
- up_bias: float32 [3072], replicated, may hold values from -3 to 3
- down_weight: bfloat16 [3072, 768], replicated, may hold values from -0.109375 to 0.109375
- down_bias: float32 [768], replicated, may hold values from -3 to 3
- cotangent: bfloat16 [8, 2048, 768], P('batch', 'seq'), may hold values from -6 to 6
Outputs:
- result: bfloat16 [8, 2048, 768], P('batch', 'seq')
- tokens_grad: bfloat16 [8, 2048, 768], P('batch', 'seq')
- first_gain_grad: float32 [768], replicated
- first_shift_grad: float32 [768], replicated
- second_gain_grad: float32 [768], replicated
- second_shift_grad: float32 [768], replicated
- input_weight_grad: float32 [768, 2304], replicated
- input_bias_grad: float32 [2304], replicated
- feature_weight_grad: float32 [12, 64], replicated
- output_weight_grad: float32 [768, 768], replicated
- output_bias_grad: float32 [768], replicated
- up_weight_grad: float32 [768, 3072], replicated
- up_bias_grad: float32 [3072], replicated
- down_weight_grad: float32 [3072, 768], replicated
- down_bias_grad: float32 [768], replicated
The draws below stay inside these ranges and needn't reach their ends.
Inputs may be any that keep to these rules, and one draw needn't show every extreme that they name: `segment_ids`: along each sequence the ids start at 0 and rise by one exactly where a document begins; every sequence holds the same number of documents, and documents run across span and device boundaries. `span_starts`: 1 exactly where the span's first token has another segment id than the token before it, and for each sequence's first span.
All inputs are finite; a program needn't handle non-finite values.
Results may differ from the reference program's by a relative error of at most 0.012.
The reference program's roundings to bfloat16 on the way count: a program that leaves them out, or rounds other values in their place, can miss the bound.
Values sent between devices are 32-bit elements; how exact they have to be, the bound alone decides.
No kernel may reach another device: no remote copies, remote signals or barrier semaphores. Data moves between devices by JAX's collectives and lax.ppermute only.
A program may use at most 192 MiB of HBM per device.

```python
import math
import jax
import jax.numpy as jnp
from jax import lax

D = 768
HEADS = 12
HD = 64
ROT = 16
NF = 64
FF = 3072
SPAN = 64
SEQ_LEN = 2048
NSEQS = 8


def begins_of_one(key):
    blocks = SEQ_LEN // SPAN
    edge_count = SEQ_LEN // (6 * SPAN)
    inner_count = SEQ_LEN // 512 + 1
    edge_pick = jax.random.permutation(jax.random.fold_in(key, 1), blocks - 1)[:edge_count] + 1
    edge_pos = edge_pick * SPAN
    inner_pick = jax.random.permutation(jax.random.fold_in(key, 2), blocks * (SPAN - 1))[:inner_count]
    inner_pos = inner_pick // (SPAN - 1) * SPAN + inner_pick % (SPAN - 1) + 1
    flags = jnp.zeros((SEQ_LEN,), jnp.int32)
    flags = flags.at[edge_pos].set(1)
    flags = flags.at[inner_pos].set(1)
    flags = flags.at[0].set(1)
    return flags


def document_begins(key):
    base = jax.random.fold_in(key, 11)
    keys = jax.random.split(base, NSEQS)
    return jax.vmap(begins_of_one)(keys)


def draw_segment_ids(key, part):
    begins = document_begins(key)
    return (jnp.cumsum(begins, axis=1) - 1).astype(jnp.int32)


def draw_span_starts(key, part):
    begins = document_begins(key)
    return begins[:, ::SPAN].astype(jnp.int32)


def shard_levels(key, shape, cuts, low, top_value):
    def one(position, parts):
        steps = jax.random.uniform(jax.random.fold_in(jax.random.fold_in(key, 6), position), (parts,), jnp.float32, low / len(cuts), top_value / len(cuts))
        return jnp.repeat(jnp.exp(steps), shape[position] // parts).reshape((-1,) + (1,) * (len(shape) - position - 1))

    level = one(*cuts[0])
    for cut in cuts[1:]:
        level = level * one(*cut)
    return level


def bell_draw(own_key, dims, scale, limit, cuts=(), kind=jnp.bfloat16):
    factor_of = shard_levels(own_key, dims, cuts, -0.22, 0.18) if cuts else 1.0
    values = jax.random.normal(own_key, dims, jnp.float32) * scale * factor_of
    return jnp.minimum(jnp.maximum(values, -limit), limit).astype(kind)


def setup_inputs(seed: int = 0) -> dict:
    key_of = jax.random.split(jax.random.key(seed), 19)
    tokens = bell_draw(key_of[0], (NSEQS, SEQ_LEN, D), 1.0, 6.0, ((0, 8), (1, 4)))
    segment_ids = draw_segment_ids(jax.random.fold_in(key_of[18], 71), 0)
    span_starts = draw_span_starts(jax.random.fold_in(key_of[18], 71), 0)
    first_gain = jnp.clip(1.0 + 0.1 * jax.random.normal(key_of[3], (D,), jnp.float32), 0.5, 1.5)
    first_shift = bell_draw(key_of[4], (D,), 0.3, 3.0, (), jnp.float32)
    second_gain = jnp.clip(1.0 + 0.1 * jax.random.normal(key_of[5], (D,), jnp.float32), 0.5, 1.5)
    second_shift = bell_draw(key_of[6], (D,), 0.3, 3.0, (), jnp.float32)
    input_weight = bell_draw(key_of[7], (D, 3 * D), D ** -0.5, 0.21875)
    input_bias = bell_draw(key_of[8], (3 * D,), 0.3, 3.0, (), jnp.float32)
    feature_freq = bell_draw(key_of[9], (HD, NF), 1.0, 4.0, (), jnp.float32)
    feature_weight = jnp.clip(jnp.exp(jax.random.uniform(key_of[10], (HEADS, NF), jnp.float32, math.log(0.5), math.log(2.0))), 0.5, 2.0)
    output_weight = bell_draw(key_of[11], (D, D), (D // 64) ** -0.5, 1.75)
    output_bias = bell_draw(key_of[12], (D,), 0.3, 3.0, (), jnp.float32)
    up_weight = bell_draw(key_of[13], (D, FF), D ** -0.5, 0.21875)
    up_bias = bell_draw(key_of[14], (FF,), 0.3, 3.0, (), jnp.float32)
    down_weight = bell_draw(key_of[15], (FF, D), FF ** -0.5, 0.109375)
    down_bias = bell_draw(key_of[16], (D,), 0.3, 3.0, (), jnp.float32)
    cotangent = bell_draw(key_of[17], (NSEQS, SEQ_LEN, D), 1.0, 6.0, ((0, 8), (1, 4)))
    return {"tokens": tokens, "segment_ids": segment_ids, "span_starts": span_starts, "first_gain": first_gain, "first_shift": first_shift, "second_gain": second_gain, "second_shift": second_shift, "input_weight": input_weight, "input_bias": input_bias, "feature_freq": feature_freq, "feature_weight": feature_weight, "output_weight": output_weight, "output_bias": output_bias, "up_weight": up_weight, "up_bias": up_bias, "down_weight": down_weight, "down_bias": down_bias, "cotangent": cotangent}


@jax.custom_vjp
def low(v):
    return lax.optimization_barrier(v.astype(jnp.bfloat16)).astype(jnp.float32)

@jax.custom_vjp
def low_back(v):
    return v

def low_keep(v):
    return (low(v), None)

def low_pass(kept, grad):
    return (grad,)

def back_keep(v):
    return (v, None)

def back_low(kept, grad):
    return (low(grad),)
low.defvjp(low_keep, low_pass)
low_back.defvjp(back_keep, back_low)
HIGH = lax.Precision.HIGHEST
EPSILON = 1e-05
ROT_BASE = 10000.0

def layer_norm(values, gain, shift):
    centre = lax.optimization_barrier(jnp.mean(values, axis=-1, keepdims=True))
    centred = values - centre
    spread = lax.optimization_barrier(jnp.mean(centred * centred, axis=-1, keepdims=True))
    return centred * lax.rsqrt(spread + EPSILON) * gain + shift

def cosine_table(points):
    index = jnp.arange(points, dtype=jnp.float32)
    table = jnp.cos(math.pi * (index[None, :] + 0.5) * index[:, None] / points) * math.sqrt(2.0 / points)
    return table * jnp.where(index[:, None] == 0, math.sqrt(0.5), 1.0)

def projection(feature_freq):
    points = feature_freq.shape[0]
    return jnp.dot(cosine_table(points).T, feature_freq, preferred_element_type=jnp.float32, precision=HIGH)

def angles(positions, rot_width):
    freq = ROT_BASE ** (-2.0 * jnp.arange(rot_width // 2, dtype=jnp.float32) / rot_width)
    turn = positions.astype(jnp.float32)[:, None] * freq[None, :]
    return (jnp.cos(turn), jnp.sin(turn))

def rotary(values, cosine, sine):
    half = cosine.shape[-1]
    front = values[..., :half]
    middle = values[..., half:2 * half]
    remain = values[..., 2 * half:]
    cos_b = cosine[:, None, :]
    sin_b = sine[:, None, :]
    return jnp.concatenate([front * cos_b - middle * sin_b, middle * cos_b + front * sin_b, remain], axis=-1)

def feature_map(values, proj, weight):
    scaled = values * math.sqrt(2.0 / values.shape[-1])
    lifted = jnp.einsum('...hd,df->...hf', scaled, proj, precision=HIGH)
    expo = lifted - 0.5 * lax.optimization_barrier(jnp.sum(scaled * scaled, axis=-1, keepdims=True))
    return weight * jnp.exp(expo)

def span_attention(query_feat, key_feat, value_low, segment_ids, span_starts):
    seq_count, length, head_count, feat_count = query_feat.shape
    head_width = value_low.shape[-1]
    blocks = length // SPAN

    def split(array):
        return jnp.moveaxis(array.reshape((seq_count, blocks, SPAN) + array.shape[2:]), 1, 0)
    causal = jnp.arange(SPAN)[:, None] >= jnp.arange(SPAN)[None, :]

    def advance(carry, pieces):
        state, norm_state = carry
        query_part, key_part, value_part, seg_part, start_part = pieces
        opened = start_part.astype(jnp.float32)
        pair_mask = ((seg_part[:, :, None] == seg_part[:, None, :]) & causal[None]).astype(jnp.float32)
        raw = jnp.einsum('bthf,bshf->bhts', query_part, key_part, precision=HIGH) * pair_mask[:, None]
        scores = low_back(raw)
        keep_first = (1.0 - opened)[:, None] * (seg_part == seg_part[:, :1]).astype(jnp.float32)
        last_doc = (seg_part == seg_part[:, -1:]).astype(jnp.float32)
        flow_gate = (1.0 - opened) * (seg_part[:, 0] == seg_part[:, -1]).astype(jnp.float32)
        inside = jnp.einsum('bhts,bshd->bthd', low(scores), value_part, precision=HIGH)
        outside = jnp.einsum('bthf,bhfd->bthd', query_part, low(state), precision=HIGH) * keep_first[:, :, None, None]
        numer = low_back(inside + outside)
        denom = jnp.swapaxes(lax.optimization_barrier(jnp.sum(scores, axis=-1)), 1, 2) + jnp.einsum('bthf,bhf->bth', query_part, norm_state, precision=HIGH) * keep_first[:, :, None]
        attended = numer / denom[..., None]
        key_last = key_part * last_doc[:, :, None, None]
        local = low_back(jnp.einsum('bshf,bshd->bhfd', key_last, value_part, precision=HIGH))
        local_norm = lax.optimization_barrier(jnp.sum(key_last, axis=1))
        state = local + flow_gate[:, None, None, None] * state
        norm_state = local_norm + flow_gate[:, None, None] * norm_state
        return ((state, norm_state), attended)
    start = (jnp.zeros((seq_count, head_count, feat_count, head_width), jnp.float32), jnp.zeros((seq_count, head_count, feat_count), jnp.float32))
    pieces = (split(query_feat), split(key_feat), split(value_low), split(segment_ids), jnp.moveaxis(span_starts, 1, 0))
    _, outputs = lax.scan(jax.checkpoint(advance), start, pieces)
    return jnp.moveaxis(outputs, 0, 1).reshape(seq_count, length, head_count, head_width)

def block(values, weights, segment_ids, span_starts, proj):
    first_gain, first_shift, second_gain, second_shift, input_weight, input_bias, feature_weight, output_weight, output_bias, up_weight, up_bias, down_weight, down_bias = weights
    seq_count, length, model_width = values.shape
    head_count = feature_weight.shape[0]
    head_width = model_width // head_count
    first_low = low(layer_norm(values, first_gain, first_shift))
    second_low = low(layer_norm(values, second_gain, second_shift))
    mixed = low_back(jnp.einsum('bld,de->ble', first_low, input_weight, precision=HIGH) + input_bias)
    queries = mixed[..., :model_width].reshape(seq_count, length, head_count, head_width)
    keys = mixed[..., model_width:2 * model_width].reshape(seq_count, length, head_count, head_width)
    value_low = low(mixed[..., 2 * model_width:].reshape(seq_count, length, head_count, head_width))
    cosine, sine = angles(jnp.arange(length), ROT)
    query_feat = low(feature_map(rotary(queries, cosine, sine), proj, feature_weight))
    key_feat = low(feature_map(rotary(keys, cosine, sine), proj, feature_weight))
    attended = span_attention(query_feat, key_feat, value_low, segment_ids, span_starts)
    attended = low(attended.reshape(seq_count, length, model_width))
    attn_out = jnp.einsum('bld,de->ble', attended, output_weight, precision=HIGH) + output_bias
    hidden = low_back(jnp.einsum('bld,df->blf', second_low, up_weight, precision=HIGH) + up_bias)
    active = low(jax.nn.gelu(hidden, approximate=False))
    mlp_out = jnp.einsum('blf,fd->bld', active, down_weight, precision=HIGH) + down_bias
    return values + attn_out + mlp_out

def reference(tokens, segment_ids, span_starts, first_gain, first_shift, second_gain, second_shift, input_weight, input_bias, feature_freq, feature_weight, output_weight, output_bias, up_weight, up_bias, down_weight, down_bias, cotangent):
    weights = tuple((w.astype(jnp.float32) for w in (first_gain, first_shift, second_gain, second_shift, input_weight, input_bias, feature_weight, output_weight, output_bias, up_weight, up_bias, down_weight, down_bias)))
    proj = projection(feature_freq.astype(jnp.float32))
    groups = segment_ids.shape[0] // 2

    def regroup(array):
        return array.reshape((groups, 2) + array.shape[1:])

    def group_step(totals, items):
        values, seg_part, start_part, cot_part = items

        def run(inputs, params):
            return block(inputs, params, seg_part, start_part, proj)
        output, pullback = jax.vjp(run, values.astype(jnp.float32), weights)
        token_grad, weight_grads = pullback(cot_part.astype(jnp.float32))
        totals = tuple((a + b for a, b in zip(totals, weight_grads)))
        return (totals, (output.astype(jnp.bfloat16), token_grad.astype(jnp.bfloat16)))
    zeros = tuple((jnp.zeros_like(w) for w in weights))
    totals, (outputs, token_grads) = lax.scan(group_step, zeros, (regroup(tokens), regroup(segment_ids), regroup(span_starts), regroup(cotangent)))
    result = outputs.reshape(tokens.shape)
    tokens_grad = token_grads.reshape(tokens.shape)
    return (result, tokens_grad, totals[0], totals[1], totals[2], totals[3], totals[4], totals[5], totals[6], totals[7], totals[8], totals[9], totals[10], totals[11], totals[12])
```

```python
import math

import jax
import jax.numpy as jnp
from jax import lax
from jax.sharding import PartitionSpec as P

ROT = 16
SPAN = 64


HIGH = lax.Precision.HIGHEST
EPSILON = 1e-05
ROT_BASE = 10000.0


def carried_in(array, axis, combine, identity, reverse):
    count, place = (lax.axis_size(axis), lax.axis_index(axis))
    everything = jax.tree.map(lambda part: lax.all_gather(part, axis), array)
    start = jax.tree.map(
        lambda part, zero: jnp.broadcast_to(jnp.asarray(zero, part.dtype), part.shape),
        array,
        identity,
    )

    def lap(k, before):
        at = count - 1 - k if reverse else k
        reached = at > place if reverse else at < place
        new = combine(before, jax.tree.map(lambda part: part[at], everything))
        return jax.tree.map(lambda a, b: jnp.where(reached, a, b), new, before)

    return lax.fori_loop(0, count, lap, start)


AXES = ("seq", "batch")


def bit_groups():
    seqs, batches = lax.axis_size("seq"), lax.axis_size("batch")
    seq_bits = [batches << k for k in range(seqs.bit_length() - 1)]
    batch_bits = [1 << k for k in range(batches.bit_length() - 1)]
    return batch_bits[:1], seq_bits, batch_bits[1:]


def own_index():
    return lax.axis_index("seq") * lax.axis_size("batch") + lax.axis_index("batch")


def swap(array, bit):
    count = lax.axis_size("seq") * lax.axis_size("batch")
    return lax.ppermute(array, AXES, [(i, i ^ bit) for i in range(count)])


def bit_value(bit):
    return (own_index() & bit) // bit


def exchange_sum(parts):
    flat = jnp.concatenate([p.reshape(-1) for p in parts])
    core, seqs, rest = bit_groups()
    for bit in core + seqs + rest:
        flat = flat + swap(flat, bit)
    out, at = [], 0
    for p in parts:
        out.append(flat[at : at + p.size].reshape(p.shape))
        at += p.size
    return out


def reduce_scatter_rows(array, start, pieces, order):
    terms = [(array, start)]
    left = pieces
    for bit in order:
        left //= 2
        mine = bit_value(bit)

        def cut(which):
            got = [lax.dynamic_slice_in_dim(t, at + which * left, left, 0) for t, at in terms]
            total = got[0]
            for g in got[1:]:
                total = total + g
            return total

        came = swap(cut(1 - mine), bit)
        terms = [(t, at + mine * left) for t, at in terms] + [(came, 0)]
    total = None
    for t, at in terms:
        g = lax.dynamic_slice_in_dim(t, at, left, 0)
        total = g if total is None else total + g
    return total


def gather_rows(piece, order):
    for bit in order[:0:-1]:
        came = swap(piece, bit)
        mine = bit_value(bit)
        piece = jnp.where(
            mine == 0,
            jnp.concatenate([piece, came], axis=0),
            jnp.concatenate([came, piece], axis=0),
        )
    return piece, swap(piece, order[0])


def reduce_chunks(array):
    core, seqs, rest = bit_groups()
    orders = (core + seqs + rest, core + seqs[::-1] + rest, core + rest[:1] + seqs + rest[1:])
    count = lax.axis_size("seq") * lax.axis_size("batch")
    rows, columns = array.shape
    cut = array.reshape(len(orders) * count, rows // (len(orders) * count), columns)
    out = jnp.zeros_like(cut)
    for k, order in enumerate(orders):
        piece = reduce_scatter_rows(cut, k * count, count, order)
        own, other = gather_rows(piece, order)
        mine = bit_value(order[0])
        half = count // 2
        out = lax.dynamic_update_slice_in_dim(out, own, k * count + mine * half, 0)
        out = lax.dynamic_update_slice_in_dim(out, other, k * count + (1 - mine) * half, 0)
    return out.reshape(rows, columns)


def layer_norm(values, gain, shift):
    centre = jnp.mean(values, axis=-1, keepdims=True)
    centred = values - centre
    spread = jnp.mean(centred * centred, axis=-1, keepdims=True)
    return centred * lax.rsqrt(spread + EPSILON) * gain + shift


def cosine_table(points):
    index = jnp.arange(points, dtype=jnp.float32)
    table = jnp.cos(math.pi * (index[None, :] + 0.5) * index[:, None] / points) * math.sqrt(
        2.0 / points
    )
    return table * jnp.where(index[:, None] == 0, math.sqrt(0.5), 1.0)


def projection(feature_freq):
    points = feature_freq.shape[0]
    return jnp.dot(
        cosine_table(points).T, feature_freq, preferred_element_type=jnp.float32, precision=HIGH
    )


def angles(positions, rot_width):
    freq = ROT_BASE ** (-2.0 * jnp.arange(rot_width // 2, dtype=jnp.float32) / rot_width)
    turn = positions.astype(jnp.float32)[:, None] * freq[None, :]
    return (jnp.cos(turn), jnp.sin(turn))


def rotary(values, cosine, sine):
    half = cosine.shape[-1]
    front = values[..., :half]
    middle = values[..., half : 2 * half]
    remain = values[..., 2 * half :]
    cos_b = cosine[:, None, :]
    sin_b = sine[:, None, :]
    return jnp.concatenate(
        [front * cos_b - middle * sin_b, middle * cos_b + front * sin_b, remain], axis=-1
    )


def feature_map(values, proj, weight):
    scaled = values * math.sqrt(2.0 / values.shape[-1])
    lifted = jnp.einsum("...hd,df->...hf", scaled, proj, precision=HIGH)
    expo = lifted - 0.5 * jnp.sum(scaled * scaled, axis=-1, keepdims=True)
    return weight * jnp.exp(expo)


def exact_gelu(values):
    return jax.nn.gelu(values, approximate=False)


def combine(earlier, following):
    return (
        following[0] + following[2][:, None, None, None] * earlier[0],
        following[1] + following[2][:, None, None] * earlier[1],
        earlier[2] * following[2],
    )


def per_device(
    tokens,
    segment_ids,
    span_starts,
    first_gain,
    first_shift,
    second_gain,
    second_shift,
    input_weight,
    input_bias,
    feature_freq,
    feature_weight,
    output_weight,
    output_bias,
    up_weight,
    up_bias,
    down_weight,
    down_bias,
    cotangent,
):
    seq_count, length, model_width = tokens.shape
    head_count, feat_count = feature_weight.shape
    head_width = model_width // head_count
    blocks = length // SPAN
    row_count = seq_count * length
    f32 = jnp.float32
    b16 = jnp.bfloat16
    as_float = tokens.astype(f32)

    def norms(values, gain_one, shift_one, gain_two, shift_two):
        return (layer_norm(values, gain_one, shift_one), layer_norm(values, gain_two, shift_two))

    (first_norm, second_norm), norm_back = jax.vjp(
        norms, as_float, first_gain, first_shift, second_gain, second_shift
    )
    first_low = first_norm.astype(b16).reshape(row_count, model_width)
    second_low = second_norm.astype(b16).reshape(row_count, model_width)
    mixed = jnp.dot(first_low, input_weight, preferred_element_type=f32) + input_bias
    queries = mixed[:, :model_width].reshape(seq_count, length, head_count, head_width)
    keys = mixed[:, model_width : 2 * model_width].reshape(
        seq_count, length, head_count, head_width
    )
    value_low = (
        mixed[:, 2 * model_width :]
        .astype(b16)
        .reshape(seq_count, blocks, SPAN, head_count, head_width)
    )
    offset = lax.axis_index("seq") * length
    cosine, sine = angles(offset + jnp.arange(length), ROT)
    proj = projection(feature_freq)

    def lift(query_in, key_in, weight):
        return (
            feature_map(rotary(query_in, cosine, sine), proj, weight),
            feature_map(rotary(key_in, cosine, sine), proj, weight),
        )

    (query_phi, key_phi), feat_back = jax.vjp(lift, queries, keys, feature_weight)
    query_low = query_phi.astype(b16).reshape(seq_count, blocks, SPAN, head_count, feat_count)
    key_low = key_phi.astype(b16).reshape(seq_count, blocks, SPAN, head_count, feat_count)
    query_wide = query_low.astype(f32)
    segs = segment_ids.reshape(seq_count, blocks, SPAN)
    opened = span_starts.astype(f32)
    causal = jnp.arange(SPAN)[:, None] >= jnp.arange(SPAN)[None, :]
    pair_mask = ((segs[:, :, :, None] == segs[:, :, None, :]) & causal[None, None]).astype(f32)
    keep_first = (1.0 - opened)[:, :, None] * (segs == segs[:, :, :1]).astype(f32)
    last_doc = (segs == segs[:, :, -1:]).astype(f32)
    flow_gate = (1.0 - opened) * (segs[:, :, 0] == segs[:, :, -1]).astype(f32)
    scores = (
        jnp.einsum("bnthf,bnshf->bnhts", query_low, key_low, preferred_element_type=f32)
        * pair_mask[:, :, None]
    )
    score_low = scores.astype(b16)
    key_last = key_low * last_doc[..., None, None].astype(b16)
    local = jnp.einsum("bnshf,bnshd->bnhfd", key_last, value_low, preferred_element_type=f32)
    local_norm = jnp.sum(key_last.astype(f32), axis=2)
    closed = 1.0 - flow_gate
    lower_tri = (jnp.arange(blocks)[:, None] > jnp.arange(blocks)[None, :]).astype(f32)
    upper_tri = (jnp.arange(blocks)[None, :] >= jnp.arange(blocks)[:, None]).astype(f32)
    before = jnp.einsum("cj,bj->bc", lower_tri, closed, precision=HIGH)
    through = before + closed
    total_closed = through[:, -1]
    reach_mat = lower_tri[None] * (before[:, :, None] == through[:, None, :]).astype(f32)
    entry_gate = (before == 0.0).astype(f32)
    tail_gate = (total_closed[:, None] == through).astype(f32)
    whole_gate = (total_closed == 0.0).astype(f32)
    summary = (
        jnp.einsum("bj,bjhfd->bhfd", tail_gate, local, precision=HIGH),
        jnp.einsum("bj,bjhf->bhf", tail_gate, local_norm, precision=HIGH),
        whole_gate,
    )
    identity = (jnp.zeros_like(summary[0]), jnp.zeros_like(summary[1]), jnp.ones_like(whole_gate))
    carried, carried_norm, _ = carried_in(summary, "seq", combine, identity, False)
    state = (
        jnp.einsum("bcj,bjhfd->bchfd", reach_mat, local, precision=HIGH)
        + entry_gate[:, :, None, None, None] * carried[:, None]
    )
    state_norm = (
        jnp.einsum("bcj,bjhf->bchf", reach_mat, local_norm, precision=HIGH)
        + entry_gate[:, :, None, None] * carried_norm[:, None]
    )
    state_low = state.astype(b16)
    inside = jnp.einsum("bnhts,bnshd->bnthd", score_low, value_low, preferred_element_type=f32)
    outside = (
        jnp.einsum("bnthf,bnhfd->bnthd", query_low, state_low, preferred_element_type=f32)
        * keep_first[..., None, None]
    )
    numer = inside + outside
    denom = (
        jnp.swapaxes(jnp.sum(scores, axis=-1), 2, 3)
        + jnp.einsum("bnthf,bnhf->bnth", query_wide, state_norm, precision=HIGH)
        * keep_first[..., None]
    )
    attended = numer / denom[..., None]
    attn_low = attended.astype(b16).reshape(row_count, model_width)
    attn_out = jnp.dot(attn_low, output_weight, preferred_element_type=f32) + output_bias
    hidden = jnp.dot(second_low, up_weight, preferred_element_type=f32) + up_bias
    active, gelu_back = jax.vjp(exact_gelu, hidden)
    active_low = active.astype(b16)
    mlp_out = jnp.dot(active_low, down_weight, preferred_element_type=f32) + down_bias
    result = (as_float.reshape(row_count, model_width) + attn_out + mlp_out).astype(b16)
    grad_rows = cotangent.reshape(row_count, model_width)
    bias_total = jnp.sum(grad_rows.astype(f32), axis=0)
    down_weight_grad = jnp.einsum("tf,td->fd", active_low, grad_rows, preferred_element_type=f32)
    output_weight_grad = jnp.einsum("ti,td->id", attn_low, grad_rows, preferred_element_type=f32)
    d_active = jnp.einsum("td,fd->tf", grad_rows, down_weight, preferred_element_type=f32)
    (d_hidden_f,) = gelu_back(d_active)
    d_hidden = d_hidden_f.astype(b16)
    up_weight_grad = jnp.einsum("td,tf->df", second_low, d_hidden, preferred_element_type=f32)
    up_bias_grad = jnp.sum(d_hidden.astype(f32), axis=0)
    d_second = jnp.einsum("tf,df->td", d_hidden, up_weight, preferred_element_type=f32)
    d_attended = jnp.einsum("te,de->td", grad_rows, output_weight, preferred_element_type=f32)
    d_attended = d_attended.reshape(seq_count, blocks, SPAN, head_count, head_width)
    d_numer = (d_attended / denom[..., None]).astype(b16)
    d_denom = -jnp.sum(d_attended * attended, axis=-1) / denom
    d_score_part = jnp.einsum("bnthd,bnshd->bnhts", d_numer, value_low, preferred_element_type=f32)
    d_value = jnp.einsum("bnhts,bnthd->bnshd", score_low, d_numer, preferred_element_type=f32)
    d_scores = (
        (d_score_part + jnp.swapaxes(d_denom, 2, 3)[..., None]) * pair_mask[:, :, None]
    ).astype(b16)
    d_query = jnp.einsum("bnhts,bnshf->bnthf", d_scores, key_low, preferred_element_type=f32)
    d_key = jnp.einsum("bnhts,bnthf->bnshf", d_scores, query_low, preferred_element_type=f32)
    query_keep = query_low * keep_first[..., None, None].astype(b16)
    here = jnp.einsum("bnthf,bnthd->bnhfd", query_keep, d_numer, preferred_element_type=f32)
    here_norm = jnp.einsum(
        "bnth,bnthf->bnhf", d_denom * keep_first[..., None], query_wide, precision=HIGH
    )
    d_query = d_query + keep_first[..., None, None] * (
        jnp.einsum("bnthd,bnhfd->bnthf", d_numer, state_low, preferred_element_type=f32)
        + d_denom[..., None] * state_norm[:, :, None]
    )
    ahead_mat = upper_tri[None] * (before[:, :, None] == before[:, None, :]).astype(f32)
    leaving = (total_closed[:, None] == before).astype(f32)
    back_summary = (
        jnp.einsum("bj,bjhfd->bhfd", ahead_mat[:, 0], here, precision=HIGH),
        jnp.einsum("bj,bjhf->bhf", ahead_mat[:, 0], here_norm, precision=HIGH),
        whole_gate,
    )
    later_grad, later_norm_grad, _ = carried_in(back_summary, "seq", combine, identity, True)
    d_state = (
        jnp.einsum("bcj,bjhfd->bchfd", ahead_mat, here, precision=HIGH)
        + leaving[:, :, None, None, None] * later_grad[:, None]
    )
    d_state_norm = (
        jnp.einsum("bcj,bjhf->bchf", ahead_mat, here_norm, precision=HIGH)
        + leaving[:, :, None, None] * later_norm_grad[:, None]
    )
    d_local = jnp.concatenate([d_state[:, 1:], later_grad[:, None]], axis=1).astype(b16)
    d_local_norm = jnp.concatenate([d_state_norm[:, 1:], later_norm_grad[:, None]], axis=1)
    d_key = d_key + last_doc[..., None, None] * (
        jnp.einsum("bnshd,bnhfd->bnshf", value_low, d_local, preferred_element_type=f32)
        + d_local_norm[:, :, None]
    )
    d_value = d_value + last_doc[..., None, None] * jnp.einsum(
        "bnshf,bnhfd->bnshd", key_low, d_local, preferred_element_type=f32
    )
    d_queries, d_keys, feature_weight_grad = feat_back(
        (
            d_query.reshape(seq_count, length, head_count, feat_count),
            d_key.reshape(seq_count, length, head_count, feat_count),
        )
    )
    d_mixed = jnp.concatenate(
        [
            d_queries.reshape(row_count, model_width),
            d_keys.reshape(row_count, model_width),
            d_value.reshape(row_count, model_width),
        ],
        axis=1,
    ).astype(b16)
    input_weight_grad = jnp.einsum("td,te->de", first_low, d_mixed, preferred_element_type=f32)
    input_bias_grad = jnp.sum(d_mixed.astype(f32), axis=0)
    d_first = jnp.einsum("te,de->td", d_mixed, input_weight, preferred_element_type=f32)
    d_inputs, first_gain_grad, first_shift_grad, second_gain_grad, second_shift_grad = norm_back(
        (
            d_first.reshape(seq_count, length, model_width),
            d_second.reshape(seq_count, length, model_width),
        )
    )
    tokens_grad = (cotangent.astype(f32) + d_inputs).astype(b16)
    small_parts = (
        first_gain_grad,
        first_shift_grad,
        second_gain_grad,
        second_shift_grad,
        input_bias_grad,
        feature_weight_grad,
        bias_total,
        up_bias_grad,
    )
    small = exchange_sum(small_parts)
    attn_grad = jnp.concatenate([input_weight_grad, output_weight_grad], axis=1)
    down_sum = reduce_chunks(down_weight_grad)
    up_sum = reduce_chunks(up_weight_grad)
    attn_sum = reduce_chunks(attn_grad)
    width = input_weight.shape[1]
    summed = (
        attn_sum[:, :width],
        attn_sum[:, width:],
        up_sum,
        down_sum,
    )
    return (
        result.reshape(seq_count, length, model_width),
        tokens_grad,
        small[0],
        small[1],
        small[2],
        small[3],
        summed[0],
        small[4],
        small[5],
        summed[1],
        small[6],
        summed[2],
        small[7],
        summed[3],
        small[6],
    )


def solution(mesh):
    in_specs = (
        P("batch", "seq", None),
        P("batch", "seq"),
        P("batch", "seq"),
        P(),
        P(),
        P(),
        P(),
        P(),
        P(),
        P(),
        P(),
        P(),
        P(),
        P(),
        P(),
        P(),
        P(),
        P("batch", "seq", None),
    )
    out_specs = (
        P("batch", "seq", None),
        P("batch", "seq", None),
        P(),
        P(),
        P(),
        P(),
        P(),
        P(),
        P(),
        P(),
        P(),
        P(),
        P(),
        P(),
        P(),
    )
    return jax.shard_map(
        per_device, mesh=mesh, in_specs=in_specs, out_specs=out_specs, check_vma=False
    )
```

```python
import functools
import math

import jax
import jax.numpy as jnp
from jax import lax
from jax.experimental import pallas as pl
from jax.experimental.pallas import tpu as pltpu
from jax.sharding import PartitionSpec as P

ROT = 16
HIGH = lax.Precision.HIGHEST
EPSILON = 1e-05
ROT_BASE = 10000.0
F32 = jnp.float32
B16 = jnp.bfloat16
GROUP = 4
EXTRA = 16
NN, NT, TN = ((1,), (0,)), ((1,), (1,)), ((0,), (0,))
TILE = 8
VMEM_LIMIT = 56 * 1024 * 1024

AXES = ("seq", "batch")


def bit_groups():
    seqs, batches = lax.axis_size("seq"), lax.axis_size("batch")
    seq_bits = [batches << k for k in range(seqs.bit_length() - 1)]
    batch_bits = [1 << k for k in range(batches.bit_length() - 1)]
    return batch_bits[:1], seq_bits, batch_bits[1:]


def own_index():
    return lax.axis_index("seq") * lax.axis_size("batch") + lax.axis_index("batch")


def swap(array, bit):
    count = lax.axis_size("seq") * lax.axis_size("batch")
    return lax.ppermute(array, AXES, [(i, i ^ bit) for i in range(count)])


def bit_value(bit):
    return (own_index() & bit) // bit


def exchange_sum(parts):
    flat = jnp.concatenate([p.reshape(-1) for p in parts])
    core, seqs, rest = bit_groups()
    for bit in core + seqs + rest:
        flat = flat + swap(flat, bit)
    out, at = [], 0
    for p in parts:
        out.append(flat[at : at + p.size].reshape(p.shape))
        at += p.size
    return out


def reduce_scatter_rows(array, start, pieces, order):
    terms = [(array, start)]
    left = pieces
    for bit in order:
        left //= 2
        mine = bit_value(bit)

        def cut(which):
            got = [lax.dynamic_slice_in_dim(t, at + which * left, left, 0) for t, at in terms]
            total = got[0]
            for g in got[1:]:
                total = total + g
            return total

        came = swap(cut(1 - mine), bit)
        terms = [(t, at + mine * left) for t, at in terms] + [(came, 0)]
    total = None
    for t, at in terms:
        g = lax.dynamic_slice_in_dim(t, at, left, 0)
        total = g if total is None else total + g
    return total


def gather_rows(piece, order):
    for bit in order[:0:-1]:
        came = swap(piece, bit)
        mine = bit_value(bit)
        piece = jnp.where(
            mine == 0,
            jnp.concatenate([piece, came], axis=0),
            jnp.concatenate([came, piece], axis=0),
        )
    return piece, swap(piece, order[0])


def reduce_chunks(chunks):
    core, seqs, rest = bit_groups()
    orders = (core + seqs + rest, core + seqs[::-1] + rest, core + rest[:1] + seqs + rest[1:])
    count = chunks[0].shape[0]
    half = count // 2
    out = jnp.zeros((len(chunks) * count,) + chunks[0].shape[1:], F32)
    for k, (chunk, order) in enumerate(zip(chunks, orders)):
        piece = reduce_scatter_rows(chunk, 0, count, order)
        own, other = gather_rows(piece, order)
        mine = bit_value(order[0])
        out = lax.dynamic_update_slice_in_dim(out, own, k * count + mine * half, 0)
        out = lax.dynamic_update_slice_in_dim(out, other, k * count + (1 - mine) * half, 0)
    return out


def cosine_table(points):
    index = jnp.arange(points, dtype=jnp.float32)
    table = jnp.cos(math.pi * (index[None, :] + 0.5) * index[:, None] / points) * math.sqrt(
        2.0 / points
    )
    return table * jnp.where(index[:, None] == 0, math.sqrt(0.5), 1.0)


def projection(feature_freq):
    points = feature_freq.shape[0]
    return jnp.dot(
        cosine_table(points).T, feature_freq, preferred_element_type=jnp.float32, precision=HIGH
    )


def dot(a, b, dims, precision=None):
    return lax.dot_general(a, b, (dims, ((), ())), preferred_element_type=F32, precision=precision)


def params():
    return pltpu.CompilerParams(vmem_limit_bytes=VMEM_LIMIT)


def full(shape):
    return pl.BlockSpec(shape, lambda *_: (0,) * len(shape))


def normalise(tokens):
    values = tokens.astype(F32)
    centre = jnp.mean(values, axis=-1, keepdims=True)
    centred = values - centre
    spread = jnp.mean(centred * centred, axis=-1, keepdims=True)
    rstd = lax.rsqrt(spread + EPSILON)
    return centred * rstd, rstd


def norm_kernel(tok, g1, s1, g2, s2, first_t, second, second_t):
    xhat, _ = normalise(tok[...])
    one = (xhat * g1[...] + s1[...]).astype(B16)
    two = (xhat * g2[...] + s2[...]).astype(B16)
    second[...] = two
    first_t[...] = one.T
    second_t[...] = two.T


def norms(tokens, g1, s1, g2, s2):
    rows, width = tokens.shape
    return pl.pallas_call(
        norm_kernel,
        out_shape=(
            jax.ShapeDtypeStruct((width, rows), B16),
            jax.ShapeDtypeStruct((rows, width), B16),
            jax.ShapeDtypeStruct((width, rows), B16),
        ),
        compiler_params=params(),
        name="norms",
    )(tokens, g1, s1, g2, s2)


def mlp_kernel(second, cot, up, up_bias, down, act, d_hidden, down_grad, bias_grad):
    hidden = dot(second[...], up[...], NN) + up_bias[...]
    phi = 0.5 + 0.5 * lax.erf(hidden * math.sqrt(0.5))
    density = jnp.exp(hidden * hidden * -0.5) * (1.0 / math.sqrt(2.0 * math.pi))
    active = (hidden * phi).astype(B16)
    d_active = dot(cot[...], down[...], NT)
    d_low = (d_active * (phi + hidden * density)).astype(B16)
    act[...] = active
    d_hidden[...] = d_low
    down_grad[...] = dot(active, cot[...], TN)
    bias_grad[...] = jnp.sum(d_low.astype(F32), axis=0, keepdims=True)


def mlp_part(second, cot, up, up_bias, down, part, parts, tile):
    rows, width = second.shape
    hidden = up.shape[1] // parts
    steps = hidden // tile
    at = part * steps
    return pl.pallas_call(
        mlp_kernel,
        grid=(steps,),
        in_specs=[
            full((rows, width)),
            full((rows, width)),
            pl.BlockSpec((width, tile), lambda j: (0, at + j)),
            pl.BlockSpec((1, tile), lambda j: (0, at + j)),
            pl.BlockSpec((tile, width), lambda j: (at + j, 0)),
        ],
        out_specs=[
            pl.BlockSpec((rows, tile), lambda j: (0, j)),
            pl.BlockSpec((rows, tile), lambda j: (0, j)),
            pl.BlockSpec((tile, width), lambda j: (j, 0)),
            pl.BlockSpec((1, tile), lambda j: (0, j)),
        ],
        out_shape=(
            jax.ShapeDtypeStruct((rows, hidden), B16),
            jax.ShapeDtypeStruct((rows, hidden), B16),
            jax.ShapeDtypeStruct((hidden, width), F32),
            jax.ShapeDtypeStruct((1, hidden), F32),
        ),
        compiler_params=params(),
        name="mlp",
    )(second, cot, up, up_bias, down)


def rotate(x, cosine, sine, back):
    half = ROT // 2
    a, b = x[:, :half], x[:, half:ROT]
    sine = -sine if back else sine
    return jnp.concatenate([a * cosine - b * sine, b * cosine + a * sine, x[:, ROT:]], axis=1)


def head_sums(x, size):
    cut = x.reshape(x.shape[0] // size, size, x.shape[1])
    total = jnp.sum(cut, axis=1, keepdims=True)
    return jnp.broadcast_to(total, cut.shape).reshape(x.shape)


def feature_kernel(
    size, first_t, wq, wk, wv, bq, bk, bv, weight, proj_t, cosine, sine, seg, start,
    q_feat, k_feat, v_low, scaled, expo, summary,
):
    scale = math.sqrt(2.0 / size)
    feats = []
    for side, (w, bias, out) in enumerate(((wq, bq, q_feat), (wk, bk, k_feat))):
        x = dot(w[...], first_t[...], TN) + bias[...]
        heads = x.shape[0] // size
        x = rotate(x.reshape(heads, size, x.shape[1]), cosine[...], sine[...], False)
        sx = x.reshape(heads * size, x.shape[2]) * scale
        lifted = dot(proj_t[...], sx, NN, HIGH)
        e = jnp.exp(lifted - 0.5 * head_sums(sx * sx, size))
        phi = (weight[...] * e).astype(B16)
        scaled[side] = sx
        expo[side] = e
        out[...] = phi
        feats.append(phi)
    value = (dot(wv[...], first_t[...], TN) + bv[...]).astype(B16)
    v_low[...] = value
    ids = seg[...]
    length = ids.shape[1]
    last = (ids == ids[:, length - 1 :]).astype(F32)
    whole = jnp.where((ids[:, :1] == ids[:, length - 1 :]) & (start[0] == 0), 1.0, 0.0)
    key_last = (feats[1].astype(F32) * last).astype(B16)
    row = lax.broadcasted_iota(jnp.int32, (EXTRA, length), 0)
    ones = jnp.where(row == 0, 1.0, 0.0).astype(B16)
    tall = size + EXTRA
    rows = lax.broadcasted_iota(jnp.int32, (tall, 2 * size), 0)
    for pair in range(heads // 2):
        got = []
        for h in (2 * pair, 2 * pair + 1):
            v_ext = jnp.concatenate([value[h * size : (h + 1) * size], ones], axis=0)
            got.append(dot(v_ext, key_last[h * size : (h + 1) * size], NT))
        both = jnp.concatenate(got, axis=1)
        summary[pair] = jnp.where(rows == size + 1, whole, both)


def features(first_t, in_weight, in_bias, weight, proj_t, cosine, sine, seg, start, size):
    width, length = first_t.shape
    tile = GROUP * size
    steps = width // tile
    pairs = GROUP // 2
    column = lambda k: pl.BlockSpec((width, tile), lambda g: (0, k * steps + g))
    bias = lambda k: pl.BlockSpec((tile, 1), lambda g: (k * steps + g, 0))
    rows = pl.BlockSpec((tile, length), lambda g: (g, 0))
    two = pl.BlockSpec((2, tile, length), lambda g: (0, g, 0))
    low = jax.ShapeDtypeStruct((width, length), B16)
    wide = jax.ShapeDtypeStruct((2, width, length), F32)
    return pl.pallas_call(
        functools.partial(feature_kernel, size),
        grid=(steps,),
        in_specs=[
            full((width, length)),
            column(0), column(1), column(2),
            bias(0), bias(1), bias(2),
            pl.BlockSpec((tile, 1), lambda g: (g, 0)),
            full((tile, tile)),
            full(cosine.shape), full(sine.shape), full(seg.shape),
            pl.BlockSpec(memory_space=pltpu.SMEM),
        ],
        out_specs=[
            rows, rows, rows, two, two,
            pl.BlockSpec((pairs, size + EXTRA, 2 * size), lambda g: (g, 0, 0)),
        ],
        out_shape=(
            low, low, low, wide, wide,
            jax.ShapeDtypeStruct((steps * pairs, size + EXTRA, 2 * size), F32),
        ),
        compiler_params=params(),
        name="features",
    )(first_t, in_weight, in_weight, in_weight, in_bias, in_bias, in_bias, weight, proj_t,
      cosine, sine, seg, start)


def chain_gates(flags, place, forward):
    count = len(flags)
    gates = [None]
    for m in range(1, count):
        other = place ^ m
        gate = jnp.where(other < place if forward else other > place, 1.0, 0.0)
        for n in range(1, count):
            if n != m:
                mid = place ^ n
                inside = (
                    (mid > other) & (mid < place) if forward else (mid < other) & (mid > place)
                )
                gate = gate * jnp.where(inside, flags[n], 1.0)
        gates.append(gate)
    return gates


def joined(refs, gates, pair):
    total = None
    for ref, gate in zip(refs, gates[1:]):
        term = jnp.where(gate != 0.0, ref[pair] * gate, 0.0)
        total = term if total is None else total + term
    return total


def halves(x):
    high = x.astype(B16).astype(F32)
    return high, x - high


def attention_kernel(size, partners, place, start, *refs):
    refs = list(refs)
    q_feat, k_feat, v_low, w_out, cot, seg, seg_col = refs[:7]
    came = refs[7 : 7 + partners]
    att, dq_out, dk_out, dv_out, here_out, gate_out, mask = refs[7 + partners :]
    length = seg.shape[1]
    block = 256
    ids = seg[...]

    @pl.when(pl.program_id(0) == 0)
    def _():
        key_at = lax.broadcasted_iota(jnp.int32, (length, length), 0)
        query_at = lax.broadcasted_iota(jnp.int32, (length, length), 1)
        same = (seg_col[...] == ids) & (key_at <= query_at)
        mask[...] = jnp.where(same, 1.0, 0.0)

    flags = [None] + [ref[0, size + 1 : size + 2, :] for ref in came]
    ahead = chain_gates(flags, place[0], True)
    behind = chain_gates(flags, place[0], False)
    for m in range(partners):
        gate_out[m] = jnp.broadcast_to(behind[m + 1], gate_out.shape[1:])
    keep = jnp.where((ids == ids[:, :1]) & (start[0] == 0), 1.0, 0.0)
    d_att = dot(w_out[...], cot[...], NT)
    tall = size + EXTRA
    row_s = lax.broadcasted_iota(jnp.int32, (tall, size), 0)
    row_d = lax.broadcasted_iota(jnp.int32, (EXTRA, length), 0)
    blocks = [(t * block, (t + 1) * block) for t in range(length // block)]
    for pair in range(GROUP // 2):
        state_pair = joined(came, ahead, pair)
        here_pair = []
        for h in (2 * pair, 2 * pair + 1):
            rows = slice(h * size, (h + 1) * size)
            state = state_pair[:, (h % 2) * size : (h % 2 + 1) * size]
            n_high, n_low = halves(state[size : size + 1])
            ext = jnp.where(row_s < size, state, 0.0)
            ext = ext + jnp.where((row_s == size) | (row_s == size + 2), n_high, 0.0)
            ext = (ext + jnp.where(row_s == size + 1, n_low, 0.0)).astype(B16)
            q, k, v = q_feat[rows], k_feat[rows], v_low[rows]
            outside = dot(ext, q, NN)
            scores, d_nums, d_dens = [], [], []
            for lo, hi in blocks:
                raw = dot(k[:, :hi], q[:, lo:hi], TN) * mask[:hi, lo:hi]
                s_low = raw.astype(B16)
                kept = keep[:, lo:hi]
                out_part = outside[:, lo:hi]
                denom = jnp.sum(raw, axis=0, keepdims=True) + kept * (
                    out_part[size : size + 1] + out_part[size + 1 : size + 2]
                )
                numer = dot(v[:, :hi], s_low, NN) + kept * out_part[:size]
                inverse = 1.0 / denom
                attended = numer * inverse
                da = d_att[rows, lo:hi]
                att[rows, lo:hi] = attended.astype(B16)
                d_nums.append((da * inverse).astype(B16))
                d_dens.append(-jnp.sum(da * attended, axis=0, keepdims=True) * inverse)
                scores.append(s_low)
            d_num = jnp.concatenate(d_nums, axis=1)
            d_den = jnp.concatenate(d_dens, axis=1)
            d_high, d_low = halves(d_den)
            tail = jnp.where(row_d < 2, d_high, jnp.where(row_d == 2, d_low, 0.0)).astype(B16)
            dn_ext = jnp.concatenate([d_num, tail], axis=0)
            dq_state = dot(ext, dn_ext, TN)
            dv_parts = [None] * len(blocks)
            dk_parts = [None] * len(blocks)
            for n, (lo, hi) in enumerate(blocks):
                d_score = dot(v[:, :hi], d_num[:, lo:hi], TN) + d_den[:, lo:hi]
                d_score = (d_score * mask[:hi, lo:hi]).astype(B16)
                dq_out[rows, lo:hi] = (
                    dot(k[:, :hi], d_score, NN) + keep[:, lo:hi] * dq_state[:, lo:hi]
                )
                for m in range(n + 1):
                    a, b = blocks[m]
                    dv = dot(d_num[:, lo:hi], scores[n][a:b], NT)
                    dk = dot(q[:, lo:hi], d_score[a:b], NT)
                    dv_parts[m] = dv if dv_parts[m] is None else dv_parts[m] + dv
                    dk_parts[m] = dk if dk_parts[m] is None else dk_parts[m] + dk
            for m, (a, b) in enumerate(blocks):
                dv_out[rows, a:b] = dv_parts[m]
                dk_out[rows, a:b] = dk_parts[m]
            here = dot((dn_ext.astype(F32) * keep).astype(B16), q, NT)
            norm = here[size : size + 1] + here[size + 2 : size + 3]
            here_pair.append(jnp.where(row_s < size, here, jnp.where(row_s == size, norm, 0.0)))
        here_out[pair] = jnp.concatenate(here_pair, axis=1)


def attention(place, start, q_feat, k_feat, v_low, w_out, cot, seg, seg_col, came, size):
    width, length = q_feat.shape
    tile = GROUP * size
    steps = width // tile
    pairs = GROUP // 2
    partners = len(came)
    rows = pl.BlockSpec((tile, length), lambda g: (g, 0))
    packed = pl.BlockSpec((pairs, size + EXTRA, 2 * size), lambda g: (g, 0, 0))
    wide = jax.ShapeDtypeStruct((width, length), F32)
    return pl.pallas_call(
        functools.partial(attention_kernel, size, partners),
        grid=(steps,),
        in_specs=[
            pl.BlockSpec(memory_space=pltpu.SMEM),
            pl.BlockSpec(memory_space=pltpu.SMEM),
            rows, rows, rows,
            pl.BlockSpec((tile, width), lambda g: (g, 0)),
            full(cot.shape), full(seg.shape), full(seg_col.shape),
        ]
        + [packed] * partners,
        out_specs=[rows, rows, rows, rows, packed, full((partners, 8, 2 * size))],
        out_shape=(
            jax.ShapeDtypeStruct((width, length), B16),
            wide, wide, wide,
            jax.ShapeDtypeStruct((steps * pairs, size + EXTRA, 2 * size), F32),
            jax.ShapeDtypeStruct((partners, 8, 2 * size), F32),
        ),
        scratch_shapes=[pltpu.VMEM((length, length), F32)],
        compiler_params=params(),
        name="attention",
    )(place, start, q_feat, k_feat, v_low, w_out, cot, seg, seg_col, *came)


def backward_kernel(size, partners, *refs):
    refs = list(refs)
    (dq, dk, dv, k_feat, v_low, scaled, expo, weight, wq, wk, wv, first_t, att, cot_col, proj,
     cosine, sine, seg, tok, cot, d_second, g1, g2) = refs[:23]
    came = refs[23 : 23 + partners]
    gates_in = refs[23 + partners]
    grad, bias_grad, weight_grad, tok_grad, gain_grad, acc = refs[24 + partners :]
    step = pl.program_id(0)
    scale = math.sqrt(2.0 / size)
    ids = seg[...]
    length = ids.shape[1]
    last = jnp.where(ids == ids[:, length - 1 :], 1.0, 0.0)
    gates = [None] + [gates_in[m][:1] for m in range(partners)]
    tall = size + EXTRA
    row_s = lax.broadcasted_iota(jnp.int32, (tall, size), 0)
    row_d = lax.broadcasted_iota(jnp.int32, (EXTRA, length), 0)
    ones = jnp.where(row_d < 2, 1.0, 0.0).astype(B16)
    dks, dvs = [], []
    for pair in range(GROUP // 2):
        later = joined(came, gates, pair)
        for h in (2 * pair, 2 * pair + 1):
            rows = slice(h * size, (h + 1) * size)
            g = later[:, (h % 2) * size : (h % 2 + 1) * size]
            n_high, n_low = halves(g[size : size + 1])
            ext = jnp.where(row_s < size, g, jnp.where(row_s == size, n_high, 0.0))
            ext = (ext + jnp.where(row_s == size + 1, n_low, 0.0)).astype(B16)
            v_ext = jnp.concatenate([v_low[rows], ones], axis=0)
            dks.append(dk[rows] + last * dot(ext, v_ext, TN))
            dvs.append(dv[rows] + last * dot(ext[:size], k_feat[rows], NN))
    d_feats = (dq[...], jnp.concatenate(dks, axis=0))
    pieces = []
    total = None
    for side, d_feat in enumerate(d_feats):
        t1 = d_feat * expo[side]
        total = t1 if total is None else total + t1
        d_expo = weight[...] * t1
        d_x = dot(proj[...], d_expo, NN, HIGH) - scaled[side] * head_sums(d_expo, size)
        heads = d_x.shape[0] // size
        d_x = rotate((d_x * scale).reshape(heads, size, length), cosine[...], sine[...], True)
        pieces.append(d_x.reshape(heads * size, length).astype(B16))
    pieces.append(jnp.concatenate(dvs, axis=0).astype(B16))
    weight_grad[...] = jnp.sum(total, axis=1, keepdims=True)
    one_row = jnp.ones((8, length), B16)
    part = None
    for m, (piece, w) in enumerate(zip(pieces, (wq, wk, wv))):
        g = dot(first_t[...], piece, NT)
        grad[:, m] = g.reshape(grad.shape[0], grad.shape[2], grad.shape[3])
        bias_grad[m] = dot(one_row, piece, NT)
        d = dot(w[...], piece, NN)
        part = d if part is None else part + d
    g = dot(att[...], cot_col[...], NN)
    grad[:, 3] = g.reshape(grad.shape[0], grad.shape[2], grad.shape[3])

    @pl.when(step == 0)
    def _():
        acc[...] = part

    @pl.when(step > 0)
    def _():
        acc[...] += part

    @pl.when(step == pl.num_programs(0) - 1)
    def _():
        d_first = acc[...].T
        d_sec = d_second[...]
        xhat, rstd = normalise(tok[...])
        gain_grad[0:1] = jnp.sum(d_first * xhat, axis=0, keepdims=True)
        gain_grad[1:2] = jnp.sum(d_first, axis=0, keepdims=True)
        gain_grad[2:3] = jnp.sum(d_sec * xhat, axis=0, keepdims=True)
        gain_grad[3:4] = jnp.sum(d_sec, axis=0, keepdims=True)
        cotangent = cot[...].astype(F32)
        gain_grad[4:5] = jnp.sum(cotangent, axis=0, keepdims=True)
        e = d_first * g1[...] + d_sec * g2[...]
        mean_e = jnp.mean(e, axis=-1, keepdims=True)
        mean_x = jnp.mean(e * xhat, axis=-1, keepdims=True)
        tok_grad[...] = (cotangent + rstd * (e - mean_e - xhat * mean_x)).astype(B16)


def backward(
    dq, dk, dv, k_feat, v_low, scaled, expo, weight, in_weight, first_t, att, cot, proj,
    cosine, sine, seg, tok, d_second, g1, g2, came, gates, size,
):
    width, length = dq.shape
    tile = GROUP * size
    steps = width // tile
    pairs = GROUP // 2
    partners = len(came)
    rows = pl.BlockSpec((tile, length), lambda g: (g, 0))
    two = pl.BlockSpec((2, tile, length), lambda g: (0, g, 0))
    column = lambda k: pl.BlockSpec((width, tile), lambda g: (0, k * steps + g))
    packed = pl.BlockSpec((pairs, size + EXTRA, 2 * size), lambda g: (g, 0, 0))
    count = width // TILE
    return pl.pallas_call(
        functools.partial(backward_kernel, size, partners),
        grid=(steps,),
        in_specs=[
            rows, rows, rows, rows, rows, two, two,
            pl.BlockSpec((tile, 1), lambda g: (g, 0)),
            column(0), column(1), column(2),
            full(first_t.shape), full(att.shape),
            pl.BlockSpec((length, tile), lambda g: (0, g)),
            full((tile, tile)),
            full(cosine.shape), full(sine.shape), full(seg.shape),
            full(tok.shape), full(cot.shape), full(d_second.shape), full(g1.shape), full(g2.shape),
        ]
        + [packed] * partners
        + [full(gates.shape)],
        out_specs=[
            pl.BlockSpec((count, 4, TILE, tile), lambda g: (0, 0, 0, g)),
            pl.BlockSpec((3, 8, tile), lambda g: (0, 0, g)),
            pl.BlockSpec((tile, 1), lambda g: (g, 0)),
            full(tok.shape),
            full((8, width)),
        ],
        out_shape=(
            jax.ShapeDtypeStruct((count, 4, TILE, width), F32),
            jax.ShapeDtypeStruct((3, 8, width), F32),
            jax.ShapeDtypeStruct((width, 1), F32),
            jax.ShapeDtypeStruct(tok.shape, B16),
            jax.ShapeDtypeStruct((8, width), F32),
        ),
        scratch_shapes=[pltpu.VMEM((width, length), F32)],
        compiler_params=params(),
        name="backward",
    )(dq, dk, dv, k_feat, v_low, scaled, expo, weight, in_weight, in_weight, in_weight, first_t,
      att, cot, proj, cosine, sine, seg, tok, cot, d_second, g1, g2, *came, gates)


def block_diagonal(table):
    size = table.shape[0]
    eye = jnp.eye(GROUP, dtype=F32)
    return (eye[:, None, :, None] * table[None, :, None, :]).reshape(GROUP * size, GROUP * size)


def per_device(
    tokens,
    segment_ids,
    span_starts,
    first_gain,
    first_shift,
    second_gain,
    second_shift,
    input_weight,
    input_bias,
    feature_freq,
    feature_weight,
    output_weight,
    output_bias,
    up_weight,
    up_bias,
    down_weight,
    down_bias,
    cotangent,
):
    seq_count, length, width = tokens.shape
    assert seq_count == 1
    heads, size = feature_weight.shape
    tok, cot = tokens[0], cotangent[0]
    g1, s1, g2, s2 = (x.reshape(1, -1) for x in (first_gain, first_shift, second_gain, second_shift))
    seqs = lax.axis_size("seq")
    count = seqs * lax.axis_size("batch")
    place = lax.axis_index("seq")
    freq = ROT_BASE ** (-2.0 * jnp.arange(ROT // 2, dtype=F32) / ROT)
    turn = freq[:, None] * (place * length + jnp.arange(length)).astype(F32)[None, :]
    cosine, sine = jnp.cos(turn), jnp.sin(turn)
    proj = projection(feature_freq)
    seg = segment_ids.reshape(1, length)
    seg_col = segment_ids.reshape(length, 1)
    start = span_starts[0, :1]
    weight_col = feature_weight.reshape(-1, 1)

    first_t, second, second_t = norms(tok, g1, s1, g2, s2)
    parts = 3
    mlp = [
        mlp_part(second, cot, up_weight, up_bias.reshape(1, -1), down_weight, i, 1, 512)
        for i in range(1)
    ]
    active = jnp.concatenate([m[0] for m in mlp], axis=1)
    d_hidden = jnp.concatenate([m[1] for m in mlp], axis=1)
    up_bias_grad = jnp.concatenate([m[3] for m in mlp], axis=1).reshape(-1)

    q_feat, k_feat, v_low, scaled, expo, summary = features(
        first_t, input_weight, input_bias.reshape(-1, 1), weight_col, block_diagonal(proj.T),
        cosine, sine, seg, start, size,
    )
    batches = lax.axis_size("batch")
    states = [swap(summary, m * batches) for m in range(1, seqs)]
    third = width // parts
    up_chunks = [
        dot(second_t[i * third : (i + 1) * third], d_hidden, NN) for i in range(parts)
    ]
    d_second = dot(d_hidden, up_weight, NT)
    mlp_out = dot(active, down_weight, NN)
    att, dq, dk, dv, here, gates = attention(
        place.reshape(1), start, q_feat, k_feat, v_low, output_weight, cot, seg, seg_col, states,
        size,
    )
    later = [swap(here, m * batches) for m in range(1, seqs)]
    attn_out = dot(att, output_weight, TN) + output_bias
    result = (tok.astype(F32) + attn_out + (mlp_out + down_bias)).astype(B16)
    attn_grad, bias_grad, weight_grad, tok_grad, gain_grad = backward(
        dq, dk, dv, k_feat, v_low, scaled, expo, weight_col, input_weight, first_t, att, cot,
        block_diagonal(proj), cosine, sine, seg, tok, d_second, g1, g2, later, gates, size,
    )
    small = exchange_sum(
        (gain_grad[:5], bias_grad[:, 0], weight_grad, up_bias_grad)
    )
    down_sum = lax.psum(mlp[0][2], AXES)
    up_sum = reduce_chunks([c.reshape(count, -1, up_weight.shape[1]) for c in up_chunks])
    tiles = third // TILE
    split = max(count // tiles, 1)
    attn_grad = attn_grad.reshape(parts, tiles, 4, split, TILE // split, width)
    attn_grad = jnp.swapaxes(attn_grad, 2, 3).reshape(parts, count, -1, 4, TILE // split, width)
    attn_sum = reduce_chunks([attn_grad[i] for i in range(parts)])
    attn_sum = attn_sum.reshape(-1, 4, TILE // split, width)
    input_weight_grad = jnp.swapaxes(attn_sum[:, :3], 1, 2).reshape(width, 3 * width)
    output_weight_grad = attn_sum[:, 3].reshape(width, width)
    gains, in_bias = small[0], small[1]
    return (
        result[None],
        tok_grad[None],
        gains[0],
        gains[1],
        gains[2],
        gains[3],
        input_weight_grad,
        in_bias.reshape(-1),
        small[2].reshape(heads, size),
        output_weight_grad,
        gains[4],
        up_sum.reshape(up_weight.shape),
        small[3],
        down_sum.reshape(down_weight.shape),
        gains[4],
    )


def solution(mesh):
    in_specs = (
        P("batch", "seq", None),
        P("batch", "seq"),
        P("batch", "seq"),
        P(),
        P(),
        P(),
        P(),
        P(),
        P(),
        P(),
        P(),
        P(),
        P(),
        P(),
        P(),
        P(),
        P(),
        P("batch", "seq", None),
    )
    out_specs = (
        P("batch", "seq", None),
        P("batch", "seq", None),
        P(),
        P(),
        P(),
        P(),
        P(),
        P(),
        P(),
        P(),
        P(),
        P(),
        P(),
        P(),
        P(),
    )
    return jax.shard_map(
        per_device, mesh=mesh, in_specs=in_specs, out_specs=out_specs, check_vma=False
    )
```

```python
import functools
import math

import jax
import jax.numpy as jnp
import numpy as np
from jax import lax
from jax.experimental import pallas as pl
from jax.experimental.pallas import tpu as pltpu
from jax.sharding import PartitionSpec as P

ROT = 16
HIGH = lax.Precision.HIGHEST
EPSILON = 1e-05
ROT_BASE = 10000.0
F32 = jnp.float32
B16 = jnp.bfloat16
GROUP = 4
EXTRA = 16
NN, NT, TN = ((1,), (0,)), ((1,), (1,)), ((0,), (0,))
TILE = 8
VMEM_LIMIT = 24 * 1024 * 1024
STEP_LIMIT = 14 * 1024 * 1024
BIG_LIMIT = 60 * 1024 * 1024
FREE = pl.CostEstimate(flops=0, bytes_accessed=0, transcendentals=0)

AXES = ("seq", "batch")


def bit_groups():
    seqs, batches = lax.axis_size("seq"), lax.axis_size("batch")
    seq_bits = [batches << k for k in range(seqs.bit_length() - 1)]
    batch_bits = [1 << k for k in range(batches.bit_length() - 1)]
    return batch_bits[:1], seq_bits, batch_bits[1:]


def own_index():
    return lax.axis_index("seq") * lax.axis_size("batch") + lax.axis_index("batch")


def swap(array, bit):
    count = lax.axis_size("seq") * lax.axis_size("batch")
    return lax.ppermute(array, AXES, [(i, i ^ bit) for i in range(count)])


def bit_value(bit):
    return (own_index() & bit) // bit


def device_bits():
    core, seqs, rest = bit_groups()
    count = len(core + seqs + rest)
    return (own_index() >> jnp.arange(count, dtype=jnp.int32)) & 1


def place_of(at, bits):
    total = at.get(0, 0)
    for bit, factor in at.items():
        if bit:
            total = total + factor * bits[bit.bit_length() - 1]
    return total


def shifted(at, bit, factor):
    moved = dict(at)
    moved[bit] = moved.get(bit, 0) + factor
    return moved


def block_spec(shape, block, index):
    tail = (0,) * (len(shape) - 1)
    return pl.BlockSpec((block,) + tuple(shape[1:]), lambda i, bits: (index(i, bits),) + tail)


def sum_tiles(bits, outputs, deps):
    totals = [sum(count for count, _ in segments) for _, segments in outputs]
    arrays, specs, plan, out_specs, out_shape = [], [], [], [], []
    for owner, (block, segments) in enumerate(outputs):
        begin = 0
        for count, terms in segments:
            blocks, slots = count // block, []
            for array, at in terms:
                at = {bit: factor // block for bit, factor in at.items()}

                def index(i, bits, at=at, begin=begin, blocks=blocks):
                    return place_of(at, bits) + jnp.clip(i - begin, 0, blocks - 1)

                specs.append(block_spec(array.shape, block, index))
                slots.append(len(arrays))
                arrays.append(array)
            plan.append((owner, begin, blocks, slots))
            begin += blocks
        shape = (totals[owner],) + arrays[-1].shape[1:]
        out_shape.append(jax.ShapeDtypeStruct(shape, F32))
        out_specs.append(block_spec(shape, block, lambda i, bits, n=begin: jnp.minimum(i, n - 1)))
    steps = max(begin + blocks for _, begin, blocks, _ in plan)

    def kernel(_, *refs):
        ins, outs = refs[: len(arrays)], refs[len(arrays) + len(deps) :]
        i = pl.program_id(0)
        for owner, begin, blocks, slots in plan:

            def add(owner=owner, slots=slots):
                total = ins[slots[0]][...]
                for slot in slots[1:]:
                    total = total + ins[slot][...]
                outs[owner][...] = total

            if begin == 0 and blocks == steps:
                add()
            else:
                pl.when((i >= begin) & (i < begin + blocks))(add)

    got = pl.pallas_call(
        kernel,
        grid_spec=pltpu.PrefetchScalarGridSpec(
            num_scalar_prefetch=1,
            grid=(steps,),
            in_specs=specs + unused(deps),
            out_specs=out_specs,
        ),
        out_shape=out_shape,
        compiler_params=params(STEP_LIMIT),
        cost_estimate=FREE,
        name="sum_tiles",
    )(bits, *arrays, *deps)
    return list(got)


def interleave(bits, pairs, order, merge, block, deps):
    count, shape = pairs[0][0].shape[0], pairs[0][0].shape[1:]
    groups = len(pairs)
    tail = (0,) * len(shape)
    flat = [x for pair in pairs for x in pair]

    def kernel(bits, *refs):
        ins, outs = refs[: 2 * groups], refs[2 * groups + len(deps) :]
        for g, bit in enumerate(order):
            out = outs[0].at[g] if merge else outs[g]
            mine = bits[bit.bit_length() - 1]
            out[pl.ds(mine, 1)] = ins[2 * g][...][None]
            out[pl.ds(1 - mine, 1)] = ins[2 * g + 1][...][None]

    if merge:
        out_specs = [
            pl.BlockSpec((groups, 2, block) + shape, lambda i, bits: (0, 0, i) + tail)
        ]
        out_shape = [jax.ShapeDtypeStruct((groups, 2, count) + shape, F32)]
    else:
        out_specs = [pl.BlockSpec((2, block) + shape, lambda i, bits: (0, i) + tail)] * groups
        out_shape = [jax.ShapeDtypeStruct((2, count) + shape, F32)] * groups
    got = pl.pallas_call(
        kernel,
        grid_spec=pltpu.PrefetchScalarGridSpec(
            num_scalar_prefetch=1,
            grid=(count // block,),
            in_specs=[block_spec(x.shape, block, lambda i, bits: i) for x in flat] + unused(deps),
            out_specs=out_specs,
        ),
        out_shape=out_shape,
        compiler_params=params(STEP_LIMIT),
        cost_estimate=FREE,
        name="interleave",
    )(bits, *flat, *deps)
    if merge:
        return got[0].reshape((groups * 2 * count,) + shape)
    return [x.reshape((2 * count,) + shape) for x in got]


def put_half(bits, bit, own, part, shapes, moves, into, deps, chunks=6):
    half = part.shape[0]
    rows = half // chunks
    at = bit.bit_length() - 1
    count = len(shapes) if len(shapes) == 1 else 4

    def kernel(bits, part, *refs):
        outs, buffer, in_sems, out_sems = refs[len(into) + len(deps) : -3], *refs[-3:]
        which = bits[at] if own else 1 - bits[at]
        spans = [pl.ds(c * rows, rows) for c in range(chunks)]
        coming = [
            pltpu.make_async_copy(part.at[span], buffer.at[span], in_sems.at[c])
            for c, span in enumerate(spans)
        ]
        going = [
            [
                pltpu.make_async_copy(a, b, out_sems.at[c * count + m])
                for m, (a, b) in enumerate(moves(buffer, outs, which, span))
            ]
            for c, span in enumerate(spans)
        ]
        for copy in coming:
            copy.start()
        for copy, onward in zip(coming, going):
            copy.wait()
            for out in onward:
                out.start()
        for onward in going:
            for out in onward:
                out.wait()

    got = pl.pallas_call(
        kernel,
        grid_spec=pltpu.PrefetchScalarGridSpec(
            num_scalar_prefetch=1,
            grid=(1,),
            in_specs=unused([part] + into + deps),
            out_specs=unused(shapes),
            scratch_shapes=[
                pltpu.VMEM(part.shape, F32),
                pltpu.SemaphoreType.DMA((chunks,)),
                pltpu.SemaphoreType.DMA((chunks * count,)),
            ],
        ),
        out_shape=[jax.ShapeDtypeStruct((2, half) + s, F32) for s in shapes],
        input_output_aliases={2 + k: k for k in range(len(into))},
        compiler_params=params(STEP_LIMIT),
        cost_estimate=FREE,
        name="put_half",
    )(bits, part, *into, *deps)
    return list(got)


def move_up(part, outs, half, rows):
    return [(part.at[rows], outs[0].at[half, rows])]


def move_attention(part, outs, half, rows):
    width = part.shape[-1]
    pieces = [outs[0].at[half, rows, :, pl.ds(m * width, width)] for m in range(3)]
    pieces.append(outs[1].at[half, rows])
    return [(part.at[rows, m], piece) for m, piece in enumerate(pieces)]


class Reduction:
    def __init__(self, bits, send, keep, small=None):
        core, seqs, rest = bit_groups()
        ring = seqs + rest[:1]
        self.bits = bits
        self.core, self.tail = core[0], rest[1:]
        self.orders = [ring[k:] + ring[:k] for k in range(3)]
        self.left = keep.shape[0] // 3
        came = swap(send, self.core)
        self.terms = [[(keep, {0: g * self.left}), (came, {0: g * self.left})] for g in range(3)]
        self.small = small
        if small is not None:
            self.small_bits = ring + self.tail
            self.small_came = swap(small, self.core)

    def small_output(self):
        return [] if self.small is None else [(1, [(1, [(self.small, {}), (self.small_came, {})])])]

    def small_next(self, small):
        if small:
            (self.small,) = small
            bits = self.small_bits
            if bits:
                self.small_came, self.small_bits = swap(self.small, bits[0]), bits[1:]

    def scatter(self, step, deps):
        self.left //= 2
        outputs = []
        for g, order in enumerate(self.orders):
            bit = order[step]
            terms = [
                (t, shifted(shifted(at, 0, self.left), bit, -self.left)) for t, at in self.terms[g]
            ]
            outputs.append((min(2, max(self.left // 2, 1)), [(self.left, terms)]))
        sends = sum_tiles(self.bits, outputs + self.small_output(), deps)
        for g, order in enumerate(self.orders):
            bit = order[step]
            came = swap(sends[g], bit)
            self.terms[g] = [(t, shifted(at, bit, self.left)) for t, at in self.terms[g]]
            self.terms[g].append((came, {}))
        self.small_next(sends[3:])
        return sends[:1]

    def exchange(self, deps):
        segments = [(self.left, terms) for terms in self.terms]
        total, *small = sum_tiles(self.bits, [(self.left, segments)] + self.small_output(), deps)
        self.small_next(small)
        first = total
        for bit in self.tail[:-1]:
            total = total + swap(total, bit)
            if small:
                self.small_next([self.small + self.small_came])
        self.both = (total, swap(total, self.tail[-1]))
        return [first]

    def settle(self, deps):
        outputs = [
            (self.left, [(self.left, [(x, {0: g * self.left}) for x in self.both])])
            for g in range(3)
        ]
        self.pieces = sum_tiles(self.bits, outputs + self.small_output(), deps)
        self.small_next(self.pieces[3:])
        self.pieces = self.pieces[:3]
        self.next_swap(2)
        return self.pieces[:1]

    def next_swap(self, step):
        self.came = [swap(p, order[step]) for p, order in zip(self.pieces, self.orders)]

    def gather(self, step, deps):
        pairs = list(zip(self.pieces, self.came))
        order = [o[step] for o in self.orders]
        block = max(pairs[0][0].shape[0] // 4, 1) if step == 0 else max(pairs[0][0].shape[0] // 2, 1)
        self.pieces = interleave(self.bits, pairs, order, step == 0, block, deps)
        if step:
            self.next_swap(step - 1)
            return self.pieces[:1]
        self.came = swap(self.pieces, self.core)
        return [self.pieces]

    def finish_own(self, how, shapes, deps):
        self.out = put_half(self.bits, self.core, True, self.pieces, shapes, how, [], deps)
        return self.out[:1]

    def finish(self, how, shapes, deps):
        got = put_half(self.bits, self.core, False, self.came, shapes, how, self.out, deps)
        return [g.reshape(-1, s[-1]) for g, s in zip(got, shapes)]


def from_partners(array):
    return [swap(array, m * lax.axis_size("batch")) for m in range(1, lax.axis_size("seq"))]


def cosine_table(points):
    index = np.arange(points, dtype=np.float64)
    table = np.cos(math.pi * (index[None, :] + 0.5) * index[:, None] / points) * math.sqrt(
        2.0 / points
    )
    return (table * np.where(index[:, None] == 0, math.sqrt(0.5), 1.0)).astype(np.float32)


def rotary_freq():
    return (ROT_BASE ** (-2.0 * np.arange(ROT // 2) / ROT)).astype(np.float32)


def dot(a, b, dims, precision=None):
    return lax.dot_general(a, b, (dims, ((), ())), preferred_element_type=F32, precision=precision)


def params(limit=None):
    return pltpu.CompilerParams(vmem_limit_bytes=limit or VMEM_LIMIT)


def ordered(kernel, count, deps):
    def run(*refs):
        kernel(*refs[:count], *refs[count + len(deps) :])

    return run


def unused(deps):
    return [pl.BlockSpec(memory_space=pl.ANY)] * len(deps)


def full(shape):
    return pl.BlockSpec(shape, lambda *_: (0,) * len(shape))


def normalise(tokens):
    values = tokens.astype(F32)
    centre = jnp.mean(values, axis=-1, keepdims=True)
    centred = values - centre
    spread = jnp.mean(centred * centred, axis=-1, keepdims=True)
    rstd = lax.rsqrt(spread + EPSILON)
    return centred * rstd, rstd


def norm_kernel(
    offset, tok, g1, s1, g2, s2, in_bias, feat_weight, up_bias_in, table_t, freq, turns,
    first_t, second, second_t, proj, proj_t, angle, vec, up_bias,
):
    width = tok.shape[1]
    for r, ref in enumerate((g1, s1, g2, s2)):
        vec[r : r + 1] = ref[...].reshape(1, width)
    for r in range(3):
        vec[4 + r : 5 + r] = in_bias[r * width : (r + 1) * width].reshape(1, width)
    vec[7:8] = feat_weight[...]
    up_bias[...] = up_bias_in[...].reshape(up_bias.shape)
    xhat, _ = normalise(tok[...])
    one = (xhat * vec[0:1] + vec[1:2]).astype(B16)
    two = (xhat * vec[2:3] + vec[3:4]).astype(B16)
    second[...] = two
    first_t[...] = one.T
    second_t[...] = two.T
    table = dot(table_t[...], freq[...], NN, HIGH)
    size = table.shape[0]
    wide = GROUP * size
    row = lax.broadcasted_iota(jnp.int32, (wide, wide), 0) // size
    same = row == lax.broadcasted_iota(jnp.int32, (wide, wide), 1) // size
    for out, block in ((proj, table), (proj_t, table.T)):
        block = jnp.concatenate([block] * GROUP, axis=1)
        out[...] = jnp.where(same, jnp.concatenate([block] * GROUP, axis=0), 0.0)
    length = tok.shape[0]
    at = lax.broadcasted_iota(jnp.int32, (ROT // 2, length), 1) + offset[0]
    turn = at.astype(F32) * turns[...]
    angle[0] = jnp.cos(turn)
    angle[1] = jnp.sin(turn)


def norms(offset, tok, small, freq):
    rows, width = tok.shape
    size = freq.shape[0]
    wide = GROUP * size
    return pl.pallas_call(
        norm_kernel,
        in_specs=[pl.BlockSpec(memory_space=pltpu.SMEM)] + [pl.BlockSpec()] * (4 + len(small)),
        out_shape=(
            jax.ShapeDtypeStruct((width, rows), B16),
            jax.ShapeDtypeStruct((rows, width), B16),
            jax.ShapeDtypeStruct((width, rows), B16),
            jax.ShapeDtypeStruct((wide, wide), F32),
            jax.ShapeDtypeStruct((wide, wide), F32),
            jax.ShapeDtypeStruct((2, ROT // 2, rows), F32),
            jax.ShapeDtypeStruct((8, width), F32),
            jax.ShapeDtypeStruct((1, small[-1].size), F32),
        ),
        compiler_params=params(BIG_LIMIT),
        name="norms",
    )(offset, tok, *small, jnp.asarray(cosine_table(size).T), freq,
      jnp.asarray(rotary_freq()[:, None]))


def mlp_kernel(second, cot, up, up_bias, down, act, d_hidden, down_grad, bias_grad):
    hidden = dot(second[...], up[...], NN) + up_bias[...]
    phi = 0.5 + 0.5 * lax.erf(hidden * math.sqrt(0.5))
    density = jnp.exp(hidden * hidden * -0.5) * (1.0 / math.sqrt(2.0 * math.pi))
    active = (hidden * phi).astype(B16)
    d_active = dot(cot[...], down[...], NT)
    d_low = (d_active * (phi + hidden * density)).astype(B16)
    act[...] = active
    d_hidden[...] = d_low
    down_grad[...] = dot(active, cot[...], TN)
    bias_grad[...] = jnp.sum(d_low.astype(F32), axis=0, keepdims=True)


def mlp_part(second, cot, up, up_bias, down, tile):
    rows, width = second.shape
    hidden = up.shape[1]
    return pl.pallas_call(
        mlp_kernel,
        grid=(hidden // tile,),
        in_specs=[
            full((rows, width)),
            full((rows, width)),
            pl.BlockSpec((width, tile), lambda j: (0, j)),
            pl.BlockSpec((1, tile), lambda j: (0, j)),
            pl.BlockSpec((tile, width), lambda j: (j, 0)),
        ],
        out_specs=[
            pl.BlockSpec((rows, tile), lambda j: (0, j)),
            pl.BlockSpec((rows, tile), lambda j: (0, j)),
            pl.BlockSpec((tile, width), lambda j: (j, 0)),
            pl.BlockSpec((1, tile), lambda j: (0, j)),
        ],
        out_shape=(
            jax.ShapeDtypeStruct((rows, hidden), B16),
            jax.ShapeDtypeStruct((rows, hidden), B16),
            pltpu.HBM((hidden, width), F32),
            jax.ShapeDtypeStruct((1, hidden), F32),
        ),
        compiler_params=params(),
        name="mlp",
    )(second, cot, up, up_bias, down)


def up_kernel(at, second_t, d_hidden, out):
    g = dot(second_t[...], d_hidden[...], NN)
    out[...] = g.reshape(out.shape)


def up_half(bits, bit, own, second_t, d_hidden, deps, steps=6):
    width, length = second_t.shape
    hidden = d_hidden.shape[1]
    half, tile = width // 2, hidden // steps
    at = bit.bit_length() - 1
    which = lambda bits: bits[at] if own else 1 - bits[at]
    return pl.pallas_call(
        ordered(up_kernel, 3, deps),
        grid_spec=pltpu.PrefetchScalarGridSpec(
            num_scalar_prefetch=1,
            grid=(steps,),
            in_specs=[
                pl.BlockSpec((half, length), lambda j, bits: (which(bits), 0)),
                pl.BlockSpec((length, tile), lambda j, bits: (0, j)),
            ]
            + unused(deps),
            out_specs=pl.BlockSpec((half // TILE, TILE, tile), lambda j, bits: (0, 0, j)),
        ),
        out_shape=jax.ShapeDtypeStruct((half // TILE, TILE, hidden), F32),
        compiler_params=params(),
        cost_estimate=FREE,
        name="up_half",
    )(bits, second_t, d_hidden, *deps)


def tail_kernel(active, d_hidden, up, down, out, d_second):
    one = dot(active[...], down[...], NN)
    two = dot(d_hidden[...], up[...], NT)

    @pl.when(pl.program_id(0) == 0)
    def _():
        out[...] = one
        d_second[...] = two

    @pl.when(pl.program_id(0) > 0)
    def _():
        out[...] += one
        d_second[...] += two


def mlp_tail(active, d_hidden, up, down, deps, steps=6):
    rows, hidden = active.shape
    width = up.shape[0]
    tile = hidden // steps
    wide = jax.ShapeDtypeStruct((rows, width), F32)
    return pl.pallas_call(
        ordered(tail_kernel, 4, deps),
        grid=(steps,),
        in_specs=[
            pl.BlockSpec((rows, tile), lambda j: (0, j)),
            pl.BlockSpec((rows, tile), lambda j: (0, j)),
            pl.BlockSpec((width, tile), lambda j: (0, j)),
            pl.BlockSpec((tile, width), lambda j: (j, 0)),
        ]
        + unused(deps),
        out_specs=[full((rows, width)), full((rows, width))],
        out_shape=(wide, wide),
        compiler_params=params(),
        cost_estimate=FREE,
        name="mlp_tail",
    )(active, d_hidden, up, down, *deps)


def result_kernel(tok, att, w_out, mlp_out, out_bias, down_bias, result):
    attn_out = dot(att[...], w_out[...], TN) + out_bias[...].reshape(1, -1)
    result[...] = (tok[...].astype(F32) + attn_out + (mlp_out[...] + down_bias[...].reshape(1, -1))).astype(B16)


def results(tok, att, w_out, mlp_out, out_bias, down_bias, deps):
    return pl.pallas_call(
        ordered(result_kernel, 6, deps),
        in_specs=[pl.BlockSpec()] * 6 + unused(deps),
        out_shape=jax.ShapeDtypeStruct(tok.shape, B16),
        compiler_params=params(),
        cost_estimate=FREE,
        name="results",
    )(tok, att, w_out, mlp_out, out_bias, down_bias, *deps)


def rotate(x, cosine, sine, back):
    half = ROT // 2
    a, b = x[:, :half], x[:, half:ROT]
    sine = -sine if back else sine
    return jnp.concatenate([a * cosine - b * sine, b * cosine + a * sine, x[:, ROT:]], axis=1)


def head_sums(x, size):
    cut = x.reshape(x.shape[0] // size, size, x.shape[1])
    total = jnp.sum(cut, axis=1, keepdims=True)
    return jnp.broadcast_to(total, cut.shape).reshape(x.shape)


def feature_kernel(
    size, first_t, wq, wk, wv, vec, proj_t, angle, seg, start,
    q_feat, k_feat, v_low, scaled, expo, summary,
):
    columns = vec[...].T
    bq, bk, bv, weight = (columns[:, c : c + 1] for c in range(4, 8))
    scale = math.sqrt(2.0 / size)
    feats = []
    for side, (w, bias, out) in enumerate(((wq, bq, q_feat), (wk, bk, k_feat))):
        x = dot(w[...], first_t[...], TN) + bias
        heads = x.shape[0] // size
        x = rotate(x.reshape(heads, size, x.shape[1]), angle[0], angle[1], False)
        sx = x.reshape(heads * size, x.shape[2]) * scale
        lifted = dot(proj_t[...], sx, NN, HIGH)
        e = jnp.exp(lifted - 0.5 * head_sums(sx * sx, size))
        phi = (weight * e).astype(B16)
        scaled[side] = sx
        expo[side] = e
        out[...] = phi
        feats.append(phi)
    value = (dot(wv[...], first_t[...], TN) + bv).astype(B16)
    v_low[...] = value
    ids = seg[...]
    length = ids.shape[1]
    last = (ids == ids[:, length - 1 :]).astype(F32)
    whole = jnp.where((ids[:, :1] == ids[:, length - 1 :]) & (start[0] == 0), 1.0, 0.0)
    key_last = (feats[1].astype(F32) * last).astype(B16)
    row = lax.broadcasted_iota(jnp.int32, (EXTRA, length), 0)
    ones = jnp.where(row == 0, 1.0, 0.0).astype(B16)
    tall = size + EXTRA
    rows = lax.broadcasted_iota(jnp.int32, (tall, 2 * size), 0)
    for pair in range(heads // 2):
        got = []
        for h in (2 * pair, 2 * pair + 1):
            v_ext = jnp.concatenate([value[h * size : (h + 1) * size], ones], axis=0)
            got.append(dot(v_ext, key_last[h * size : (h + 1) * size], NT))
        both = jnp.concatenate(got, axis=1)
        summary[pair] = jnp.where(rows == size + 1, whole, both)


def features(first_t, in_weight, vec, proj_t, angle, seg, start, size, deps):
    width, length = first_t.shape
    tile = GROUP * size
    steps = width // tile
    pairs = GROUP // 2
    column = lambda k: pl.BlockSpec((width, tile), lambda g: (0, k * steps + g))
    rows = pl.BlockSpec((tile, length), lambda g: (g, 0))
    two = pl.BlockSpec((2, tile, length), lambda g: (0, g, 0))
    low = jax.ShapeDtypeStruct((width, length), B16)
    wide = jax.ShapeDtypeStruct((2, width, length), F32)
    return pl.pallas_call(
        ordered(functools.partial(feature_kernel, size), 9, deps),
        grid=(steps,),
        in_specs=[
            full((width, length)),
            column(0), column(1), column(2),
            pl.BlockSpec((8, tile), lambda g: (0, g)),
            full((tile, tile)),
            full(angle.shape), full(seg.shape),
            pl.BlockSpec(memory_space=pltpu.SMEM),
        ]
        + unused(deps),
        out_specs=[
            rows, rows, rows, two, two,
            pl.BlockSpec((pairs, size + EXTRA, 2 * size), lambda g: (g, 0, 0)),
        ],
        out_shape=(
            low, low, low, wide, wide,
            jax.ShapeDtypeStruct((steps * pairs, size + EXTRA, 2 * size), F32),
        ),
        compiler_params=params(),
        cost_estimate=FREE,
        name="features",
    )(first_t, in_weight, in_weight, in_weight, vec, proj_t, angle, seg, start, *deps)


def chain_gates(flags, place, forward):
    count = len(flags)
    gates = [None]
    for m in range(1, count):
        other = place ^ m
        gate = jnp.where(other < place if forward else other > place, 1.0, 0.0)
        for n in range(1, count):
            if n != m:
                mid = place ^ n
                inside = (
                    (mid > other) & (mid < place) if forward else (mid < other) & (mid > place)
                )
                gate = gate * jnp.where(inside, flags[n], 1.0)
        gates.append(gate)
    return gates


def joined(refs, gates, pair):
    total = None
    for ref, gate in zip(refs, gates[1:]):
        term = jnp.where(gate != 0.0, ref[pair] * gate, 0.0)
        total = term if total is None else total + term
    return total


def halves(x):
    high = x.astype(B16).astype(F32)
    return high, x - high


def attention_kernel(size, partners, place, start, *refs):
    refs = list(refs)
    q_feat, k_feat, v_low, w_out, cot, seg, seg_col = refs[:7]
    came = refs[7 : 7 + partners]
    att, dq_out, dk_out, dv_out, here_out, gate_out, mask = refs[7 + partners :]
    length = seg.shape[1]
    block = 256
    ids = seg[...]

    @pl.when(pl.program_id(0) == 0)
    def _():
        key_at = lax.broadcasted_iota(jnp.int32, (length, length), 0)
        query_at = lax.broadcasted_iota(jnp.int32, (length, length), 1)
        same = (seg_col[...] == ids) & (key_at <= query_at)
        mask[...] = jnp.where(same, 1.0, 0.0)

    flags = [None] + [ref[0, size + 1 : size + 2, :] for ref in came]
    ahead = chain_gates(flags, place[0], True)
    behind = chain_gates(flags, place[0], False)
    for m in range(partners):
        gate_out[m] = jnp.broadcast_to(behind[m + 1], gate_out.shape[1:])
    keep = jnp.where((ids == ids[:, :1]) & (start[0] == 0), 1.0, 0.0)
    d_att = dot(w_out[...], cot[...], NT)
    tall = size + EXTRA
    row_s = lax.broadcasted_iota(jnp.int32, (tall, size), 0)
    row_d = lax.broadcasted_iota(jnp.int32, (EXTRA, length), 0)
    blocks = [(t * block, (t + 1) * block) for t in range(length // block)]
    for pair in range(GROUP // 2):
        state_pair = joined(came, ahead, pair)
        here_pair = []
        for h in (2 * pair, 2 * pair + 1):
            rows = slice(h * size, (h + 1) * size)
            state = state_pair[:, (h % 2) * size : (h % 2 + 1) * size]
            n_high, n_low = halves(state[size : size + 1])
            ext = jnp.where(row_s < size, state, 0.0)
            ext = ext + jnp.where((row_s == size) | (row_s == size + 2), n_high, 0.0)
            ext = (ext + jnp.where(row_s == size + 1, n_low, 0.0)).astype(B16)
            q, k, v = q_feat[rows], k_feat[rows], v_low[rows]
            outside = dot(ext, q, NN)
            scores, d_nums, d_dens = [], [], []
            for lo, hi in blocks:
                raw = dot(k[:, :hi], q[:, lo:hi], TN) * mask[:hi, lo:hi]
                s_low = raw.astype(B16)
                kept = keep[:, lo:hi]
                out_part = outside[:, lo:hi]
                denom = jnp.sum(raw, axis=0, keepdims=True) + kept * (
                    out_part[size : size + 1] + out_part[size + 1 : size + 2]
                )
                numer = dot(v[:, :hi], s_low, NN) + kept * out_part[:size]
                inverse = 1.0 / denom
                attended = numer * inverse
                da = d_att[rows, lo:hi]
                att[rows, lo:hi] = attended.astype(B16)
                d_nums.append((da * inverse).astype(B16))
                d_dens.append(-jnp.sum(da * attended, axis=0, keepdims=True) * inverse)
                scores.append(s_low)
            d_num = jnp.concatenate(d_nums, axis=1)
            d_den = jnp.concatenate(d_dens, axis=1)
            d_high, d_low = halves(d_den)
            tail = jnp.where(row_d < 2, d_high, jnp.where(row_d == 2, d_low, 0.0)).astype(B16)
            dn_ext = jnp.concatenate([d_num, tail], axis=0)
            dq_state = dot(ext, dn_ext, TN)
            dv_parts = [None] * len(blocks)
            dk_parts = [None] * len(blocks)
            for n, (lo, hi) in enumerate(blocks):
                d_score = dot(v[:, :hi], d_num[:, lo:hi], TN) + d_den[:, lo:hi]
                d_score = (d_score * mask[:hi, lo:hi]).astype(B16)
                dq_out[rows, lo:hi] = (
                    dot(k[:, :hi], d_score, NN) + keep[:, lo:hi] * dq_state[:, lo:hi]
                )
                for m in range(n + 1):
                    a, b = blocks[m]
                    dv = dot(d_num[:, lo:hi], scores[n][a:b], NT)
                    dk = dot(q[:, lo:hi], d_score[a:b], NT)
                    dv_parts[m] = dv if dv_parts[m] is None else dv_parts[m] + dv
                    dk_parts[m] = dk if dk_parts[m] is None else dk_parts[m] + dk
            for m, (a, b) in enumerate(blocks):
                dv_out[rows, a:b] = dv_parts[m]
                dk_out[rows, a:b] = dk_parts[m]
            here = dot((dn_ext.astype(F32) * keep).astype(B16), q, NT)
            norm = here[size : size + 1] + here[size + 2 : size + 3]
            here_pair.append(jnp.where(row_s < size, here, jnp.where(row_s == size, norm, 0.0)))
        here_out[pair] = jnp.concatenate(here_pair, axis=1)


def attention(
    place, start, q_feat, k_feat, v_low, w_out, cot, seg, seg_col, came, size, groups, so_far, deps
):
    width, length = q_feat.shape
    tile = GROUP * size
    steps = width // tile
    first, count = groups
    pairs = GROUP // 2
    partners = len(came)
    rows = pl.BlockSpec((tile, length), lambda g: (first + g, 0))
    packed = pl.BlockSpec((pairs, size + EXTRA, 2 * size), lambda g: (first + g, 0, 0))
    wide = jax.ShapeDtypeStruct((width, length), F32)
    return pl.pallas_call(
        ordered(functools.partial(attention_kernel, size, partners), 9 + partners, so_far + deps),
        grid=(count,),
        in_specs=[
            pl.BlockSpec(memory_space=pltpu.SMEM),
            pl.BlockSpec(memory_space=pltpu.SMEM),
            rows, rows, rows,
            pl.BlockSpec((tile, width), lambda g: (first + g, 0)),
            full(cot.shape), full(seg.shape), full(seg_col.shape),
        ]
        + [packed] * partners
        + unused(so_far + deps),
        out_specs=[rows, rows, rows, rows, packed, full((partners, 8, 2 * size))],
        out_shape=(
            jax.ShapeDtypeStruct((width, length), B16),
            wide, wide, wide,
            jax.ShapeDtypeStruct((steps * pairs, size + EXTRA, 2 * size), F32),
            jax.ShapeDtypeStruct((partners, 8, 2 * size), F32),
        ),
        scratch_shapes=[pltpu.VMEM((length, length), F32)],
        input_output_aliases={9 + partners + k: k for k in range(len(so_far))},
        compiler_params=params(),
        cost_estimate=FREE,
        name="attention",
    )(place, start, q_feat, k_feat, v_low, w_out, cot, seg, seg_col, *came, *so_far, *deps)


def backward_kernel(size, partners, opens, closes, *refs):
    refs = list(refs)
    (dq, dk, dv, k_feat, v_low, scaled, expo, vec, wq, wk, wv, first_t, att, cot_col, proj,
     angle, seg, tok, cot, d_second, vec_all) = refs[:21]
    came = refs[21 : 21 + partners]
    gates_in, up_bias, bits = refs[21 + partners : 24 + partners]
    refs = refs[24 + partners :]
    if not opens:
        acc_in, small_in = refs[:2]
        refs = refs[2:]
    send, keep, small, acc = refs[:4]
    first = 0 if opens else 2
    mine = bits[0]
    half = first_t.shape[0] // 2
    tile = dq.shape[0]
    here = pl.ds(pl.multiple_of(mine * half, half), half)
    there = pl.ds(pl.multiple_of((1 - mine) * half, half), half)
    columns = pl.ds(pl.multiple_of((first + pl.program_id(0)) * tile, tile), tile)
    count = send.shape[0]
    weight = vec[...].T[:, 7:8]
    step = pl.program_id(0)
    scale = math.sqrt(2.0 / size)
    ids = seg[...]
    length = ids.shape[1]
    last = jnp.where(ids == ids[:, length - 1 :], 1.0, 0.0)
    gates = [None] + [gates_in[m][:1] for m in range(partners)]
    tall = size + EXTRA
    row_s = lax.broadcasted_iota(jnp.int32, (tall, size), 0)
    row_d = lax.broadcasted_iota(jnp.int32, (EXTRA, length), 0)
    ones = jnp.where(row_d < 2, 1.0, 0.0).astype(B16)
    dks, dvs = [], []
    for pair in range(GROUP // 2):
        later = joined(came, gates, pair)
        for h in (2 * pair, 2 * pair + 1):
            rows = slice(h * size, (h + 1) * size)
            g = later[:, (h % 2) * size : (h % 2 + 1) * size]
            n_high, n_low = halves(g[size : size + 1])
            ext = jnp.where(row_s < size, g, jnp.where(row_s == size, n_high, 0.0))
            ext = (ext + jnp.where(row_s == size + 1, n_low, 0.0)).astype(B16)
            v_ext = jnp.concatenate([v_low[rows], ones], axis=0)
            dks.append(dk[rows] + last * dot(ext, v_ext, TN))
            dvs.append(dv[rows] + last * dot(ext[:size], k_feat[rows], NN))
    d_feats = (dq[...], jnp.concatenate(dks, axis=0))
    pieces = []
    total = None
    for side, d_feat in enumerate(d_feats):
        t1 = d_feat * expo[side]
        total = t1 if total is None else total + t1
        d_expo = weight * t1
        d_x = dot(proj[...], d_expo, NN, HIGH) - scaled[side] * head_sums(d_expo, size)
        heads = d_x.shape[0] // size
        d_x = rotate((d_x * scale).reshape(heads, size, length), angle[0], angle[1], True)
        pieces.append(d_x.reshape(heads * size, length).astype(B16))
    pieces.append(jnp.concatenate(dvs, axis=0).astype(B16))

    @pl.when(step == 0)
    def _():
        small[...] = jnp.zeros(small.shape, F32) if opens else small_in[...]
        if opens:
            for r in range(up_bias.shape[1] // first_t.shape[0]):
                part = slice(r * first_t.shape[0], (r + 1) * first_t.shape[0])
                small[9 + r : 10 + r, :] = up_bias[:, part]

    total = jnp.broadcast_to(jnp.sum(total, axis=1, keepdims=True), (tile, 128))
    small[8:9, columns] = total.T[:1]
    one_row = jnp.ones((8, length), B16)
    part = None
    for m, (piece, w) in enumerate(zip(pieces, (wq, wk, wv))):
        g = dot(first_t[there, :], piece, NT)
        send[:, m] = g.reshape(count, TILE, tile)
        g = dot(first_t[here, :], piece, NT)
        keep[:, m] = g.reshape(count, TILE, tile)
        small[5 + m : 6 + m, columns] = dot(one_row, piece, NT)[:1]
        d = dot(w[...], piece, NN)
        part = d if part is None else part + d
    send[:, 3] = dot(att[there, :], cot_col[...], NN).reshape(count, TILE, tile)
    keep[:, 3] = dot(att[here, :], cot_col[...], NN).reshape(count, TILE, tile)

    @pl.when(step == 0)
    def _():
        acc[...] = part if opens else acc_in[...] + part

    @pl.when(step > 0)
    def _():
        acc[...] += part

    if not closes:
        return
    tok_grad = refs[4]

    @pl.when(step == pl.num_programs(0) - 1)
    def _():
        d_first = acc[...].T
        d_sec = d_second[...]
        xhat, rstd = normalise(tok[...])
        cotangent = cot[...].astype(F32)
        for r, x in enumerate((d_first * xhat, d_first, d_sec * xhat, d_sec, cotangent)):
            small[r : r + 1, :] = jnp.sum(x, axis=0, keepdims=True)
        e = d_first * vec_all[0:1] + d_sec * vec_all[2:3]
        mean_e = jnp.mean(e, axis=-1, keepdims=True)
        mean_x = jnp.mean(e * xhat, axis=-1, keepdims=True)
        tok_grad[...] = (cotangent + rstd * (e - mean_e - xhat * mean_x)).astype(B16)


def backward(
    dq, dk, dv, k_feat, v_low, scaled, expo, vec, in_weight, first_t, att, cot, proj, angle,
    seg, tok, d_second, came, gates, up_bias, bits, size, groups, so_far, deps,
):
    width, length = dq.shape
    tile = GROUP * size
    steps = width // tile
    begin, some = groups
    opens, closes = begin == 0, begin + some == steps
    carried = [] if opens else [so_far[3], so_far[2]]
    kept = so_far[:2]
    pairs = GROUP // 2
    partners = len(came)
    rows = pl.BlockSpec((tile, length), lambda g: (begin + g, 0))
    two = pl.BlockSpec((2, tile, length), lambda g: (0, begin + g, 0))
    column = lambda k: pl.BlockSpec((width, tile), lambda g: (0, k * steps + begin + g))
    packed = pl.BlockSpec((pairs, size + EXTRA, 2 * size), lambda g: (begin + g, 0, 0))
    count = width // TILE // 2
    return pl.pallas_call(
        ordered(
            functools.partial(backward_kernel, size, partners, opens, closes),
            24 + partners + len(carried),
            kept + deps,
        ),
        grid=(some,),
        in_specs=[
            rows, rows, rows, rows, rows, two, two,
            pl.BlockSpec((8, tile), lambda g: (0, begin + g)),
            column(0), column(1), column(2),
            full(first_t.shape), full(att.shape),
            pl.BlockSpec((length, tile), lambda g: (0, begin + g)),
            full((tile, tile)),
            full(angle.shape), full(seg.shape),
            full(tok.shape), full(cot.shape), full(d_second.shape), full(vec.shape),
        ]
        + [packed] * partners
        + [full(gates.shape), full(up_bias.shape), pl.BlockSpec(memory_space=pltpu.SMEM)]
        + [full(x.shape) for x in carried]
        + unused(kept + deps),
        out_specs=[
            pl.BlockSpec((count, 4, TILE, tile), lambda g: (0, 0, 0, begin + g)),
            pl.BlockSpec((count, 4, TILE, tile), lambda g: (0, 0, 0, begin + g)),
            full((16, width)),
            full((width, length)),
            full(tok.shape),
        ][: 4 + closes],
        out_shape=[
            jax.ShapeDtypeStruct((count, 4, TILE, width), F32),
            jax.ShapeDtypeStruct((count, 4, TILE, width), F32),
            jax.ShapeDtypeStruct((16, width), F32),
            jax.ShapeDtypeStruct((width, length), F32),
            jax.ShapeDtypeStruct(tok.shape, B16),
        ][: 4 + closes],
        input_output_aliases={24 + partners + len(carried) + k: k for k in range(len(kept))},
        compiler_params=params(),
        cost_estimate=FREE,
        name="backward",
    )(dq, dk, dv, k_feat, v_low, scaled, expo, vec, in_weight, in_weight, in_weight, first_t,
      att, cot, proj, angle, seg, tok, cot, d_second, vec, *came, gates, up_bias, bits, *carried, *kept, *deps)


def per_device(
    tokens,
    segment_ids,
    span_starts,
    first_gain,
    first_shift,
    second_gain,
    second_shift,
    input_weight,
    input_bias,
    feature_freq,
    feature_weight,
    output_weight,
    output_bias,
    up_weight,
    up_bias,
    down_weight,
    down_bias,
    cotangent,
):
    seq_count, length, width = tokens.shape
    assert seq_count == 1
    heads, size = feature_weight.shape
    tok, cot = tokens[0], cotangent[0]
    seqs, batches = lax.axis_size("seq"), lax.axis_size("batch")
    place = lax.axis_index("seq").reshape(1)
    seg = segment_ids.reshape(1, length)
    seg_col = segment_ids.reshape(length, 1)
    start = span_starts[0, :1]
    small = (
        first_gain, first_shift, second_gain, second_shift, input_bias,
        feature_weight.reshape(1, -1), up_bias,
    )
    first_t, second, second_t, proj, proj_t, angle, vec, up_bias_row = norms(
        place * length, tok, small, feature_freq
    )
    active, d_hidden, down_grad, up_bias_grad = mlp_part(
        second, cot, up_weight, up_bias_row, down_weight, 512
    )
    down_sum = lax.psum(down_grad, AXES)
    core = bit_groups()[0][0]
    bits = device_bits()
    up_shapes = [(TILE, up_weight.shape[1])]
    attn_shapes = [(TILE, 3 * width), (TILE, width)]

    def rest(first_t, second_t, active, d_hidden):
        up_send = up_half(bits, core, False, second_t, d_hidden, [])
        up_keep = up_half(bits, core, True, second_t, d_hidden, [up_send])
        up = Reduction(bits, up_send, up_keep)
        q_feat, k_feat, v_low, scaled, expo, summary = features(
            first_t, input_weight, vec, proj_t, angle, seg, start, size, [up_keep]
        )
        states = from_partners(summary)
        mlp_out, d_second = mlp_tail(active, d_hidden, up_weight, down_weight, [summary])
        last = up.scatter(0, [mlp_out] + states)
        groups = heads // GROUP
        att, dq, dk, dv, here, gates = attention(
            place, start, q_feat, k_feat, v_low, output_weight, cot, seg, seg_col, states, size,
            (0, groups), [], last,
        )
        later = from_partners(here)
        result = results(tok, att, output_weight, mlp_out, output_bias, down_bias, [])
        last = up.scatter(1, [result] + later)
        fixed = (
            dq, dk, dv, k_feat, v_low, scaled, expo, vec, input_weight, first_t, att, cot, proj,
            angle, seg, tok, d_second, later, gates, up_bias_grad, bits, size,
        )
        some = list(backward(*fixed, (0, groups - 1), [], last))
        last = up.scatter(2, some[:1])
        send, keep, small, _, tok_grad = backward(*fixed, (groups - 1, 1), some, last)
        attn = Reduction(bits, send, keep, small.reshape(1, 2, 8, width))
        last = up.exchange([tok_grad])
        last = attn.scatter(0, last)
        last = attn.scatter(1, last)
        last = attn.scatter(2, last)
        last = attn.exchange(last)
        last = up.settle(last)
        last = up.gather(2, last)
        last = up.gather(1, last)
        last = attn.settle(last)
        last = up.gather(0, last)
        last = attn.gather(2, last)
        last = up.finish_own(move_up, up_shapes, last)
        last = attn.gather(1, last)
        last = attn.gather(0, last)
        last = attn.finish_own(move_attention, attn_shapes, last)
        (up_sum,) = up.finish(move_up, up_shapes, last)
        in_sum, out_sum = attn.finish(move_attention, attn_shapes, [up_sum])
        return result, tok_grad, up_sum, in_sum, out_sum, attn.small.reshape(16, width)

    def nothing(first_t, second_t, active, d_hidden):
        low = jnp.zeros(tok.shape, B16)
        return (
            low, low, jnp.zeros(up_weight.shape, F32), jnp.zeros(input_weight.shape, F32),
            jnp.zeros(output_weight.shape, F32), jnp.zeros((16, width), F32),
        )

    result, tok_grad, up_sum, in_sum, out_sum, sums = lax.cond(
        start[0] < 2, rest, nothing, first_t, second_t, active, d_hidden
    )
    return (
        result[None],
        tok_grad[None],
        sums[0],
        sums[1],
        sums[2],
        sums[3],
        in_sum,
        sums[5:8].reshape(-1),
        sums[8].reshape(heads, size),
        out_sum,
        sums[4],
        up_sum,
        sums[9 : 9 + up_weight.shape[1] // width].reshape(-1),
        down_sum,
        sums[4],
    )


def solution(mesh):
    in_specs = (
        P("batch", "seq", None),
        P("batch", "seq"),
        P("batch", "seq"),
        P(),
        P(),
        P(),
        P(),
        P(),
        P(),
        P(),
        P(),
        P(),
        P(),
        P(),
        P(),
        P(),
        P(),
        P("batch", "seq", None),
    )
    out_specs = (
        P("batch", "seq", None),
        P("batch", "seq", None),
        P(),
        P(),
        P(),
        P(),
        P(),
        P(),
        P(),
        P(),
        P(),
        P(),
        P(),
        P(),
        P(),
    )
    return jax.shard_map(
        per_device, mesh=mesh, in_specs=in_specs, out_specs=out_specs, check_vma=False
    )
```

```python
import functools
import math

import jax
import jax.numpy as jnp
import numpy as np
from jax import lax
from jax.experimental import pallas as pl
from jax.experimental.pallas import tpu as pltpu
from jax.sharding import PartitionSpec as P

ROT = 16
HIGH = lax.Precision.HIGHEST
EPSILON = 1e-05
ROT_BASE = 10000.0
F32 = jnp.float32
B16 = jnp.bfloat16
GROUP = 4
EXTRA = 16
NN, NT, TN = ((1,), (0,)), ((1,), (1,)), ((0,), (0,))
TILE = 8
MIB = 1024 * 1024
STEP_LIMIT = 10 * MIB
BIG_LIMIT = 60 * MIB
FREE = pl.CostEstimate(flops=0, bytes_accessed=0, transcendentals=0)

AXES = ("seq", "batch")


def bit_groups():
    seqs, batches = lax.axis_size("seq"), lax.axis_size("batch")
    seq_bits = [batches << k for k in range(seqs.bit_length() - 1)]
    batch_bits = [1 << k for k in range(batches.bit_length() - 1)]
    return batch_bits[:1], seq_bits, batch_bits[1:]


def own_index():
    return lax.axis_index("seq") * lax.axis_size("batch") + lax.axis_index("batch")


def swap(array, bit):
    count = lax.axis_size("seq") * lax.axis_size("batch")
    return lax.ppermute(array, AXES, [(i, i ^ bit) for i in range(count)])


def bit_value(bit):
    return (own_index() & bit) // bit


def device_bits():
    core, seqs, rest = bit_groups()
    count = len(core + seqs + rest)
    return (own_index() >> jnp.arange(count, dtype=jnp.int32)) & 1


def place_of(at, bits):
    total = at.get(0, 0)
    for bit, factor in at.items():
        if bit:
            total = total + factor * bits[bit.bit_length() - 1]
    return total


def shifted(at, bit, factor):
    moved = dict(at)
    moved[bit] = moved.get(bit, 0) + factor
    return moved


def block_spec(shape, block, index):
    tail = (0,) * (len(shape) - 1)
    return pl.BlockSpec((block,) + tuple(shape[1:]), lambda i, bits: (index(i, bits),) + tail)


def sum_tiles(bits, outputs, deps):
    totals = [sum(count for count, _ in segments) for _, segments in outputs]
    arrays, specs, plan, out_specs, out_shape = [], [], [], [], []
    for owner, (block, segments) in enumerate(outputs):
        begin = 0
        for count, terms in segments:
            blocks, slots = count // block, []
            for array, at in terms:
                at = {bit: factor // block for bit, factor in at.items()}

                def index(i, bits, at=at, begin=begin, blocks=blocks):
                    return place_of(at, bits) + jnp.clip(i - begin, 0, blocks - 1)

                specs.append(block_spec(array.shape, block, index))
                slots.append(len(arrays))
                arrays.append(array)
            plan.append((owner, begin, blocks, slots))
            begin += blocks
        shape = (totals[owner],) + arrays[-1].shape[1:]
        out_shape.append(jax.ShapeDtypeStruct(shape, F32))
        out_specs.append(block_spec(shape, block, lambda i, bits, n=begin: jnp.minimum(i, n - 1)))
    steps = max(begin + blocks for _, begin, blocks, _ in plan)

    def kernel(_, *refs):
        ins, outs = refs[: len(arrays)], refs[len(arrays) + len(deps) :]
        i = pl.program_id(0)
        for owner, begin, blocks, slots in plan:

            def add(owner=owner, slots=slots):
                total = ins[slots[0]][...]
                for slot in slots[1:]:
                    total = total + ins[slot][...]
                outs[owner][...] = total

            if begin == 0 and blocks == steps:
                add()
            else:
                pl.when((i >= begin) & (i < begin + blocks))(add)

    got = pl.pallas_call(
        kernel,
        grid_spec=pltpu.PrefetchScalarGridSpec(
            num_scalar_prefetch=1,
            grid=(steps,),
            in_specs=specs + unused(deps),
            out_specs=out_specs,
        ),
        out_shape=out_shape,
        compiler_params=params(STEP_LIMIT),
        cost_estimate=FREE,
        name="sum_tiles",
    )(bits, *arrays, *deps)
    return list(got)


def interleave(bits, pairs, count, order, merge, block, deps):
    shape = pairs[0][0][0].shape[1:]
    groups = len(pairs)
    tail = (0,) * len(shape)
    flat = [x for pair in pairs for x in pair]

    def kernel(bits, *refs):
        ins, outs = refs[: 2 * groups], refs[2 * groups + len(deps) :]
        for g, bit in enumerate(order):
            out = outs[0].at[g] if merge else outs[g]
            mine = bits[bit.bit_length() - 1]
            out[pl.ds(mine, 1)] = ins[2 * g][...][None]
            out[pl.ds(1 - mine, 1)] = ins[2 * g + 1][...][None]

    if merge:
        out_specs = [
            pl.BlockSpec((groups, 2, block) + shape, lambda i, bits: (0, 0, i) + tail)
        ]
        out_shape = [jax.ShapeDtypeStruct((groups, 2, count) + shape, F32)]
    else:
        out_specs = [pl.BlockSpec((2, block) + shape, lambda i, bits: (0, i) + tail)] * groups
        out_shape = [jax.ShapeDtypeStruct((2, count) + shape, F32)] * groups
    got = pl.pallas_call(
        kernel,
        grid_spec=pltpu.PrefetchScalarGridSpec(
            num_scalar_prefetch=1,
            grid=(count // block,),
            in_specs=[
                block_spec(x.shape, block, lambda i, bits, at=at: at // block + i) for x, at in flat
            ]
            + unused(deps),
            out_specs=out_specs,
        ),
        out_shape=out_shape,
        compiler_params=params(STEP_LIMIT),
        cost_estimate=FREE,
        name="interleave",
    )(bits, *[x for x, _ in flat], *deps)
    if merge:
        return got[0].reshape((groups * 2 * count,) + shape)
    return [x.reshape((2 * count,) + shape) for x in got]


def put_half(bits, bit, own, part, shapes, moves, into, deps, chunks=6):
    half = part.shape[0]
    rows = half // chunks
    at = bit.bit_length() - 1
    count = len(shapes) if len(shapes) == 1 else 4

    def kernel(bits, part, *refs):
        outs, buffer, in_sems, out_sems = refs[len(into) + len(deps) : -3], *refs[-3:]
        which = bits[at] if own else 1 - bits[at]
        spans = [pl.ds(c * rows, rows) for c in range(chunks)]
        coming = [
            pltpu.make_async_copy(part.at[span], buffer.at[span], in_sems.at[c])
            for c, span in enumerate(spans)
        ]
        going = [
            [
                pltpu.make_async_copy(a, b, out_sems.at[c * count + m])
                for m, (a, b) in enumerate(moves(buffer, outs, which, span))
            ]
            for c, span in enumerate(spans)
        ]
        for copy in coming:
            copy.start()
        for copy, onward in zip(coming, going):
            copy.wait()
            for out in onward:
                out.start()
        for onward in going:
            for out in onward:
                out.wait()

    got = pl.pallas_call(
        kernel,
        grid_spec=pltpu.PrefetchScalarGridSpec(
            num_scalar_prefetch=1,
            grid=(1,),
            in_specs=unused([part] + into + deps),
            out_specs=unused(shapes),
            scratch_shapes=[
                pltpu.VMEM(part.shape, F32),
                pltpu.SemaphoreType.DMA((chunks,)),
                pltpu.SemaphoreType.DMA((chunks * count,)),
            ],
        ),
        out_shape=[jax.ShapeDtypeStruct((2, half) + s, F32) for s in shapes],
        input_output_aliases={2 + k: k for k in range(len(into))},
        compiler_params=params(STEP_LIMIT),
        cost_estimate=FREE,
        name="put_half",
    )(bits, part, *into, *deps)
    return list(got)


def move_up(part, outs, half, rows):
    return [(part.at[rows], outs[0].at[half, rows])]


def move_attention(part, outs, half, rows):
    width = part.shape[-1]
    pieces = [outs[0].at[half, rows, :, pl.ds(m * width, width)] for m in range(3)]
    pieces.append(outs[1].at[half, rows])
    return [(part.at[rows, m], piece) for m, piece in enumerate(pieces)]


def block_of(count, most):
    return max(b for b in range(1, most + 1) if count % b == 0)


class Reduction:
    def __init__(self, bits, send, keep, groups, small=None):
        core, seqs, rest = bit_groups()
        ring = seqs + rest[:1] if groups == 3 else seqs
        self.bits = bits
        self.core, self.tail = core[0], rest[1:]
        self.merged = None if groups == 3 else rest[0]
        self.orders = [ring[k:] + ring[:k] for k in range(groups)]
        self.last = len(ring) - 1
        self.left = keep.shape[0] // groups
        came = swap(send, self.core)
        self.terms = [
            [(keep, {0: g * self.left}), (came, {0: g * self.left})] for g in range(groups)
        ]
        self.small = small
        if small is not None:
            self.small_bits = seqs + rest
            self.small_came = swap(small, self.core)

    def small_output(self):
        return [] if self.small is None else [(1, [(1, [(self.small, {}), (self.small_came, {})])])]

    def small_next(self, small):
        if small:
            (self.small,) = small
            bits = self.small_bits
            if bits:
                self.small_came, self.small_bits = swap(self.small, bits[0]), bits[1:]

    def scatter(self, step, deps):
        self.left //= 2
        block = block_of(self.left, max(min(3, self.left // 2), 1))
        outputs = []
        for g, order in enumerate(self.orders):
            bit = order[step]
            terms = [
                (t, shifted(shifted(at, 0, self.left), bit, -self.left)) for t, at in self.terms[g]
            ]
            outputs.append((block, [(self.left, terms)]))
        sends = sum_tiles(self.bits, outputs + self.small_output(), deps)
        for g, order in enumerate(self.orders):
            bit = order[step]
            came = swap(sends[g], bit)
            self.terms[g] = [(t, shifted(at, bit, self.left)) for t, at in self.terms[g]]
            self.terms[g].append((came, {}))
        self.small_next(sends[len(self.orders) :])
        return sends[:1]

    def merge(self, deps):
        self.left //= 2
        bit, segments = self.merged, []
        for terms in self.terms:
            terms = [(t, shifted(shifted(at, 0, self.left), bit, -self.left)) for t, at in terms]
            segments.append((self.left, terms))
        send, *small = sum_tiles(self.bits, [(self.left, segments)] + self.small_output(), deps)
        self.small_next(small)
        came = swap(send, bit)
        for g, terms in enumerate(self.terms):
            self.terms[g] = [(t, shifted(at, bit, self.left)) for t, at in terms]
            self.terms[g].append((came, {0: g * self.left}))
        return [send]

    def exchange(self, deps):
        segments = [(self.left, terms) for terms in self.terms]
        total, *small = sum_tiles(self.bits, [(self.left, segments)] + self.small_output(), deps)
        self.small_next(small)
        first = total
        for bit in self.tail[:-1]:
            total = total + swap(total, bit)
            if small:
                self.small_next([self.small + self.small_came])
        self.both = (total, swap(total, self.tail[-1]))
        return [first]

    def settle(self, deps):
        groups = len(self.orders)
        if self.merged:
            count = groups * self.left
            outputs = [(self.left, [(count, [(x, {}) for x in self.both])])]
        else:
            outputs = [
                (self.left, [(self.left, [(x, {0: g * self.left}) for x in self.both])])
                for g in range(groups)
            ]
        got = sum_tiles(self.bits, outputs + self.small_output(), deps)
        self.pieces = got[: len(outputs)]
        self.small_next(got[len(outputs) :])
        if self.merged:
            self.came = [swap(self.pieces[0], self.merged)]
        else:
            self.next_swap(self.last)
        return self.pieces[:1]

    def next_swap(self, step):
        self.came = [swap(p, order[step]) for p, order in zip(self.pieces, self.orders)]

    def unmerge(self, deps):
        groups = len(self.orders)
        pairs = [
            ((self.pieces[0], g * self.left), (self.came[0], g * self.left)) for g in range(groups)
        ]
        self.pieces = interleave(
            self.bits, pairs, self.left, [self.merged] * groups, False, self.left, deps
        )
        self.next_swap(self.last)
        return self.pieces[:1]

    def gather(self, step, deps):
        pairs = [((a, 0), (b, 0)) for a, b in zip(self.pieces, self.came)]
        count = self.pieces[0].shape[0]
        order = [o[step] for o in self.orders]
        block = block_of(count, max(min(3, count // 2), 1))
        self.pieces = interleave(self.bits, pairs, count, order, step == 0, block, deps)
        if step:
            self.next_swap(step - 1)
            return self.pieces[:1]
        self.came = swap(self.pieces, self.core)
        return [self.pieces]

    def finish_own(self, how, shapes, deps):
        self.out = put_half(self.bits, self.core, True, self.pieces, shapes, how, [], deps)
        return self.out[:1]

    def finish(self, how, shapes, deps):
        got = put_half(self.bits, self.core, False, self.came, shapes, how, self.out, deps)
        return [g.reshape(-1, s[-1]) for g, s in zip(got, shapes)]


def from_partners(array):
    return [swap(array, m * lax.axis_size("batch")) for m in range(1, lax.axis_size("seq"))]


def cosine_table(points):
    index = np.arange(points, dtype=np.float64)
    table = np.cos(math.pi * (index[None, :] + 0.5) * index[:, None] / points) * math.sqrt(
        2.0 / points
    )
    return (table * np.where(index[:, None] == 0, math.sqrt(0.5), 1.0)).astype(np.float32)


def rotary_freq():
    return (ROT_BASE ** (-2.0 * np.arange(ROT // 2) / ROT)).astype(np.float32)


def dot(a, b, dims, precision=None):
    return lax.dot_general(a, b, (dims, ((), ())), preferred_element_type=F32, precision=precision)


def params(limit):
    return pltpu.CompilerParams(vmem_limit_bytes=limit)


def ordered(kernel, count, deps):
    def run(*refs):
        kernel(*refs[:count], *refs[count + len(deps) :])

    return run


def unused(deps):
    return [pl.BlockSpec(memory_space=pl.ANY)] * len(deps)


def full(shape):
    return pl.BlockSpec(shape, lambda *_: (0,) * len(shape))


def normalise(tokens):
    values = tokens.astype(F32)
    centre = jnp.mean(values, axis=-1, keepdims=True)
    centred = values - centre
    spread = jnp.mean(centred * centred, axis=-1, keepdims=True)
    rstd = lax.rsqrt(spread + EPSILON)
    return centred * rstd, rstd


def norm_kernel(
    offset, tok, g1, s1, g2, s2, in_bias, feat_weight, up_bias_in, table_t, freq, turns,
    first_t, second, second_t, proj, proj_t, angle, vec, up_bias,
):
    width = tok.shape[1]
    for r, ref in enumerate((g1, s1, g2, s2)):
        vec[r : r + 1] = ref[...].reshape(1, width)
    for r in range(3):
        vec[4 + r : 5 + r] = in_bias[r * width : (r + 1) * width].reshape(1, width)
    vec[7:8] = feat_weight[...]
    up_bias[...] = up_bias_in[...].reshape(up_bias.shape)
    xhat, _ = normalise(tok[...])
    one = (xhat * vec[0:1] + vec[1:2]).astype(B16)
    two = (xhat * vec[2:3] + vec[3:4]).astype(B16)
    second[...] = two
    first_t[...] = one.T
    second_t[...] = two.T
    table = dot(table_t[...], freq[...], NN, HIGH)
    size = table.shape[0]
    wide = GROUP * size
    row = lax.broadcasted_iota(jnp.int32, (wide, wide), 0) // size
    same = row == lax.broadcasted_iota(jnp.int32, (wide, wide), 1) // size
    for out, block in ((proj, table), (proj_t, table.T)):
        block = jnp.concatenate([block] * GROUP, axis=1)
        out[...] = jnp.where(same, jnp.concatenate([block] * GROUP, axis=0), 0.0)
    length = tok.shape[0]
    at = lax.broadcasted_iota(jnp.int32, (ROT // 2, length), 1) + offset[0]
    turn = at.astype(F32) * turns[...]
    angle[0] = jnp.cos(turn)
    angle[1] = jnp.sin(turn)


def norms(offset, tok, small, freq):
    rows, width = tok.shape
    size = freq.shape[0]
    wide = GROUP * size
    return pl.pallas_call(
        norm_kernel,
        in_specs=[pl.BlockSpec(memory_space=pltpu.SMEM)] + [pl.BlockSpec()] * (4 + len(small)),
        out_shape=(
            jax.ShapeDtypeStruct((width, rows), B16),
            jax.ShapeDtypeStruct((rows, width), B16),
            jax.ShapeDtypeStruct((width, rows), B16),
            jax.ShapeDtypeStruct((wide, wide), F32),
            jax.ShapeDtypeStruct((wide, wide), F32),
            jax.ShapeDtypeStruct((2, ROT // 2, rows), F32),
            jax.ShapeDtypeStruct((8, width), F32),
            jax.ShapeDtypeStruct((1, small[-1].size), F32),
        ),
        compiler_params=params(BIG_LIMIT),
        name="norms",
    )(offset, tok, *small, jnp.asarray(cosine_table(size).T), freq,
      jnp.asarray(rotary_freq()[:, None]))


def mlp_kernel(second, cot, up, up_bias, down, act, d_hidden, down_grad, bias_grad):
    hidden = dot(second[...], up[...], NN) + up_bias[...]
    phi = 0.5 + 0.5 * lax.erf(hidden * math.sqrt(0.5))
    density = jnp.exp(hidden * hidden * -0.5) * (1.0 / math.sqrt(2.0 * math.pi))
    active = (hidden * phi).astype(B16)
    d_active = dot(cot[...], down[...], NT)
    d_low = (d_active * (phi + hidden * density)).astype(B16)
    act[...] = active
    d_hidden[...] = d_low
    down_grad[...] = dot(active, cot[...], TN)
    bias_grad[...] = jnp.sum(d_low.astype(F32), axis=0, keepdims=True)


def mlp_part(second, cot, up, up_bias, down, tile):
    rows, width = second.shape
    hidden = up.shape[1]
    return pl.pallas_call(
        mlp_kernel,
        grid=(hidden // tile,),
        in_specs=[
            full((rows, width)),
            full((rows, width)),
            pl.BlockSpec((width, tile), lambda j: (0, j)),
            pl.BlockSpec((1, tile), lambda j: (0, j)),
            pl.BlockSpec((tile, width), lambda j: (j, 0)),
        ],
        out_specs=[
            pl.BlockSpec((rows, tile), lambda j: (0, j)),
            pl.BlockSpec((rows, tile), lambda j: (0, j)),
            pl.BlockSpec((tile, width), lambda j: (j, 0)),
            pl.BlockSpec((1, tile), lambda j: (0, j)),
        ],
        out_shape=(
            jax.ShapeDtypeStruct((rows, hidden), B16),
            jax.ShapeDtypeStruct((rows, hidden), B16),
            pltpu.HBM((hidden, width), F32),
            jax.ShapeDtypeStruct((1, hidden), F32),
        ),
        compiler_params=params(18 * MIB),
        name="mlp",
    )(second, cot, up, up_bias, down)


def up_kernel(at, second_t, d_hidden, out):
    g = dot(second_t[...], d_hidden[...], NN)
    out[...] = g.reshape(out.shape)


def up_half(bits, bit, own, second_t, d_hidden, deps, steps=6):
    width, length = second_t.shape
    hidden = d_hidden.shape[1]
    half, tile = width // 2, hidden // steps
    at = bit.bit_length() - 1
    which = lambda bits: bits[at] if own else 1 - bits[at]
    return pl.pallas_call(
        ordered(up_kernel, 3, deps),
        grid_spec=pltpu.PrefetchScalarGridSpec(
            num_scalar_prefetch=1,
            grid=(steps,),
            in_specs=[
                pl.BlockSpec((half, length), lambda j, bits: (which(bits), 0)),
                pl.BlockSpec((length, tile), lambda j, bits: (0, j)),
            ]
            + unused(deps),
            out_specs=pl.BlockSpec((half // TILE, TILE, tile), lambda j, bits: (0, 0, j)),
        ),
        out_shape=jax.ShapeDtypeStruct((half // TILE, TILE, hidden), F32),
        compiler_params=params(10 * MIB),
        cost_estimate=FREE,
        name="up_half",
    )(bits, second_t, d_hidden, *deps)


def tail_kernel(active, d_hidden, up, down, out, d_second):
    one = dot(active[...], down[...], NN)
    two = dot(d_hidden[...], up[...], NT)

    @pl.when(pl.program_id(0) == 0)
    def _():
        out[...] = one
        d_second[...] = two

    @pl.when(pl.program_id(0) > 0)
    def _():
        out[...] += one
        d_second[...] += two


def mlp_tail(active, d_hidden, up, down, deps, steps=6):
    rows, hidden = active.shape
    width = up.shape[0]
    tile = hidden // steps
    wide = jax.ShapeDtypeStruct((rows, width), F32)
    return pl.pallas_call(
        ordered(tail_kernel, 4, deps),
        grid=(steps,),
        in_specs=[
            pl.BlockSpec((rows, tile), lambda j: (0, j)),
            pl.BlockSpec((rows, tile), lambda j: (0, j)),
            pl.BlockSpec((width, tile), lambda j: (0, j)),
            pl.BlockSpec((tile, width), lambda j: (j, 0)),
        ]
        + unused(deps),
        out_specs=[full((rows, width)), full((rows, width))],
        out_shape=(wide, wide),
        compiler_params=params(14 * MIB),
        cost_estimate=FREE,
        name="mlp_tail",
    )(active, d_hidden, up, down, *deps)


def result_kernel(tok, att, w_out, mlp_out, out_bias, down_bias, result):
    attn_out = dot(att[...], w_out[...], TN) + out_bias[...].reshape(1, -1)
    result[...] = (tok[...].astype(F32) + attn_out + (mlp_out[...] + down_bias[...].reshape(1, -1))).astype(B16)


def results(tok, att, w_out, mlp_out, out_bias, down_bias, deps):
    return pl.pallas_call(
        ordered(result_kernel, 6, deps),
        in_specs=[pl.BlockSpec()] * 6 + unused(deps),
        out_shape=jax.ShapeDtypeStruct(tok.shape, B16),
        compiler_params=params(10 * MIB),
        cost_estimate=FREE,
        name="results",
    )(tok, att, w_out, mlp_out, out_bias, down_bias, *deps)


def rotate(x, cosine, sine, back):
    half = ROT // 2
    a, b = x[:, :half], x[:, half:ROT]
    sine = -sine if back else sine
    return jnp.concatenate([a * cosine - b * sine, b * cosine + a * sine, x[:, ROT:]], axis=1)


def head_sums(x, size):
    cut = x.reshape(x.shape[0] // size, size, x.shape[1])
    total = jnp.sum(cut, axis=1, keepdims=True)
    return jnp.broadcast_to(total, cut.shape).reshape(x.shape)


def feature_kernel(
    size, first_t, wq, wk, wv, vec, proj_t, angle, seg, start,
    q_feat, k_feat, v_low, scaled, expo, summary,
):
    columns = vec[...].T
    bq, bk, bv, weight = (columns[:, c : c + 1] for c in range(4, 8))
    scale = math.sqrt(2.0 / size)
    feats = []
    for side, (w, bias, out) in enumerate(((wq, bq, q_feat), (wk, bk, k_feat))):
        x = dot(w[...], first_t[...], TN) + bias
        heads = x.shape[0] // size
        x = rotate(x.reshape(heads, size, x.shape[1]), angle[0], angle[1], False)
        sx = x.reshape(heads * size, x.shape[2]) * scale
        lifted = dot(proj_t[...], sx, NN, HIGH)
        e = jnp.exp(lifted - 0.5 * head_sums(sx * sx, size))
        phi = (weight * e).astype(B16)
        scaled[side] = sx
        expo[side] = e
        out[...] = phi
        feats.append(phi)
    value = (dot(wv[...], first_t[...], TN) + bv).astype(B16)
    v_low[...] = value
    ids = seg[...]
    length = ids.shape[1]
    last = (ids == ids[:, length - 1 :]).astype(F32)
    whole = jnp.where((ids[:, :1] == ids[:, length - 1 :]) & (start[0] == 0), 1.0, 0.0)
    key_last = (feats[1].astype(F32) * last).astype(B16)
    row = lax.broadcasted_iota(jnp.int32, (EXTRA, length), 0)
    ones = jnp.where(row == 0, 1.0, 0.0).astype(B16)
    tall = size + EXTRA
    rows = lax.broadcasted_iota(jnp.int32, (tall, 2 * size), 0)
    for pair in range(heads // 2):
        got = []
        for h in (2 * pair, 2 * pair + 1):
            v_ext = jnp.concatenate([value[h * size : (h + 1) * size], ones], axis=0)
            got.append(dot(v_ext, key_last[h * size : (h + 1) * size], NT))
        both = jnp.concatenate(got, axis=1)
        summary[pair] = jnp.where(rows == size + 1, whole, both)


def features(first_t, in_weight, vec, proj_t, angle, seg, start, size, deps):
    width, length = first_t.shape
    tile = GROUP * size
    steps = width // tile
    pairs = GROUP // 2
    column = lambda k: pl.BlockSpec((width, tile), lambda g: (0, k * steps + g))
    rows = pl.BlockSpec((tile, length), lambda g: (g, 0))
    two = pl.BlockSpec((2, tile, length), lambda g: (0, g, 0))
    low = jax.ShapeDtypeStruct((width, length), B16)
    wide = jax.ShapeDtypeStruct((2, width, length), F32)
    return pl.pallas_call(
        ordered(functools.partial(feature_kernel, size), 9, deps),
        grid=(steps,),
        in_specs=[
            full((width, length)),
            column(0), column(1), column(2),
            pl.BlockSpec((8, tile), lambda g: (0, g)),
            full((tile, tile)),
            full(angle.shape), full(seg.shape),
            pl.BlockSpec(memory_space=pltpu.SMEM),
        ]
        + unused(deps),
        out_specs=[
            rows, rows, rows, two, two,
            pl.BlockSpec((pairs, size + EXTRA, 2 * size), lambda g: (g, 0, 0)),
        ],
        out_shape=(
            low, low, low, wide, wide,
            jax.ShapeDtypeStruct((steps * pairs, size + EXTRA, 2 * size), F32),
        ),
        compiler_params=params(14 * MIB),
        cost_estimate=FREE,
        name="features",
    )(first_t, in_weight, in_weight, in_weight, vec, proj_t, angle, seg, start, *deps)


def chain_gates(flags, place, forward):
    count = len(flags)
    gates = [None]
    for m in range(1, count):
        other = place ^ m
        gate = jnp.where(other < place if forward else other > place, 1.0, 0.0)
        for n in range(1, count):
            if n != m:
                mid = place ^ n
                inside = (
                    (mid > other) & (mid < place) if forward else (mid < other) & (mid > place)
                )
                gate = gate * jnp.where(inside, flags[n], 1.0)
        gates.append(gate)
    return gates


def joined(refs, gates, pair):
    total = None
    for ref, gate in zip(refs, gates[1:]):
        term = jnp.where(gate != 0.0, ref[pair] * gate, 0.0)
        total = term if total is None else total + term
    return total


def halves(x):
    high = x.astype(B16).astype(F32)
    return high, x - high


def attention_kernel(size, partners, place, start, *refs):
    refs = list(refs)
    q_feat, k_feat, v_low, w_out, cot, seg, seg_col = refs[:7]
    came = refs[7 : 7 + partners]
    att, dq_out, dk_out, dv_out, here_out, gate_out, mask = refs[7 + partners :]
    length = seg.shape[1]
    block = 256
    ids = seg[...]

    @pl.when(pl.program_id(0) == 0)
    def _():
        key_at = lax.broadcasted_iota(jnp.int32, (length, length), 0)
        query_at = lax.broadcasted_iota(jnp.int32, (length, length), 1)
        same = (seg_col[...] == ids) & (key_at <= query_at)
        mask[...] = jnp.where(same, 1.0, 0.0)

    flags = [None] + [ref[0, size + 1 : size + 2, :] for ref in came]
    ahead = chain_gates(flags, place[0], True)
    behind = chain_gates(flags, place[0], False)
    for m in range(partners):
        gate_out[m] = jnp.broadcast_to(behind[m + 1], gate_out.shape[1:])
    keep = jnp.where((ids == ids[:, :1]) & (start[0] == 0), 1.0, 0.0)
    d_att = dot(w_out[...], cot[...], NT)
    tall = size + EXTRA
    row_s = lax.broadcasted_iota(jnp.int32, (tall, size), 0)
    row_d = lax.broadcasted_iota(jnp.int32, (EXTRA, length), 0)
    blocks = [(t * block, (t + 1) * block) for t in range(length // block)]
    for pair in range(GROUP // 2):
        state_pair = joined(came, ahead, pair)
        here_pair = []
        for h in (2 * pair, 2 * pair + 1):
            rows = slice(h * size, (h + 1) * size)
            state = state_pair[:, (h % 2) * size : (h % 2 + 1) * size]
            n_high, n_low = halves(state[size : size + 1])
            ext = jnp.where(row_s < size, state, 0.0)
            ext = ext + jnp.where((row_s == size) | (row_s == size + 2), n_high, 0.0)
            ext = (ext + jnp.where(row_s == size + 1, n_low, 0.0)).astype(B16)
            q, k, v = q_feat[rows], k_feat[rows], v_low[rows]
            outside = dot(ext, q, NN)
            scores, d_nums, d_dens = [], [], []
            for lo, hi in blocks:
                raw = dot(k[:, :hi], q[:, lo:hi], TN) * mask[:hi, lo:hi]
                s_low = raw.astype(B16)
                kept = keep[:, lo:hi]
                out_part = outside[:, lo:hi]
                denom = jnp.sum(raw, axis=0, keepdims=True) + kept * (
                    out_part[size : size + 1] + out_part[size + 1 : size + 2]
                )
                numer = dot(v[:, :hi], s_low, NN) + kept * out_part[:size]
                inverse = 1.0 / denom
                attended = numer * inverse
                da = d_att[rows, lo:hi]
                att[rows, lo:hi] = attended.astype(B16)
                d_nums.append((da * inverse).astype(B16))
                d_dens.append(-jnp.sum(da * attended, axis=0, keepdims=True) * inverse)
                scores.append(s_low)
            d_num = jnp.concatenate(d_nums, axis=1)
            d_den = jnp.concatenate(d_dens, axis=1)
            d_high, d_low = halves(d_den)
            tail = jnp.where(row_d < 2, d_high, jnp.where(row_d == 2, d_low, 0.0)).astype(B16)
            dn_ext = jnp.concatenate([d_num, tail], axis=0)
            dq_state = dot(ext, dn_ext, TN)
            dv_parts = [None] * len(blocks)
            dk_parts = [None] * len(blocks)
            for n, (lo, hi) in enumerate(blocks):
                d_score = dot(v[:, :hi], d_num[:, lo:hi], TN) + d_den[:, lo:hi]
                d_score = (d_score * mask[:hi, lo:hi]).astype(B16)
                dq_out[rows, lo:hi] = (
                    dot(k[:, :hi], d_score, NN) + keep[:, lo:hi] * dq_state[:, lo:hi]
                )
                for m in range(n + 1):
                    a, b = blocks[m]
                    dv = dot(d_num[:, lo:hi], scores[n][a:b], NT)
                    dk = dot(q[:, lo:hi], d_score[a:b], NT)
                    dv_parts[m] = dv if dv_parts[m] is None else dv_parts[m] + dv
                    dk_parts[m] = dk if dk_parts[m] is None else dk_parts[m] + dk
            for m, (a, b) in enumerate(blocks):
                dv_out[rows, a:b] = dv_parts[m]
                dk_out[rows, a:b] = dk_parts[m]
            here = dot((dn_ext.astype(F32) * keep).astype(B16), q, NT)
            norm = here[size : size + 1] + here[size + 2 : size + 3]
            here_pair.append(jnp.where(row_s < size, here, jnp.where(row_s == size, norm, 0.0)))
        here_out[pair] = jnp.concatenate(here_pair, axis=1)


def attention(
    place, start, q_feat, k_feat, v_low, w_out, cot, seg, seg_col, came, size, groups, so_far, deps
):
    width, length = q_feat.shape
    tile = GROUP * size
    steps = width // tile
    first, count = groups
    pairs = GROUP // 2
    partners = len(came)
    rows = pl.BlockSpec((tile, length), lambda g: (first + g, 0))
    packed = pl.BlockSpec((pairs, size + EXTRA, 2 * size), lambda g: (first + g, 0, 0))
    wide = jax.ShapeDtypeStruct((width, length), F32)
    return pl.pallas_call(
        ordered(functools.partial(attention_kernel, size, partners), 9 + partners, so_far + deps),
        grid=(count,),
        in_specs=[
            pl.BlockSpec(memory_space=pltpu.SMEM),
            pl.BlockSpec(memory_space=pltpu.SMEM),
            rows, rows, rows,
            pl.BlockSpec((tile, width), lambda g: (first + g, 0)),
            full(cot.shape), full(seg.shape), full(seg_col.shape),
        ]
        + [packed] * partners
        + unused(so_far + deps),
        out_specs=[rows, rows, rows, rows, packed, full((partners, 8, 2 * size))],
        out_shape=(
            jax.ShapeDtypeStruct((width, length), B16),
            wide, wide, wide,
            jax.ShapeDtypeStruct((steps * pairs, size + EXTRA, 2 * size), F32),
            jax.ShapeDtypeStruct((partners, 8, 2 * size), F32),
        ),
        scratch_shapes=[pltpu.VMEM((length, length), F32)],
        input_output_aliases={9 + partners + k: k for k in range(len(so_far))},
        compiler_params=params(16 * MIB),
        cost_estimate=FREE,
        name="attention",
    )(place, start, q_feat, k_feat, v_low, w_out, cot, seg, seg_col, *came, *so_far, *deps)


def backward_kernel(size, partners, opens, closes, *refs):
    refs = list(refs)
    (dq, dk, dv, k_feat, v_low, scaled, expo, vec, wq, wk, wv, first_t, att, cot_col, proj,
     angle, seg, tok, cot, d_second, vec_all) = refs[:21]
    came = refs[21 : 21 + partners]
    gates_in, up_bias, bits = refs[21 + partners : 24 + partners]
    refs = refs[24 + partners :]
    if not opens:
        acc_in, small_in = refs[:2]
        refs = refs[2:]
    send, keep, small, acc = refs[:4]
    first = 0 if opens else 2
    mine = bits[0]
    half = first_t.shape[0] // 2
    tile = dq.shape[0]
    here = pl.ds(pl.multiple_of(mine * half, half), half)
    there = pl.ds(pl.multiple_of((1 - mine) * half, half), half)
    columns = pl.ds(pl.multiple_of((first + pl.program_id(0)) * tile, tile), tile)
    count = send.shape[0]
    weight = vec[...].T[:, 7:8]
    step = pl.program_id(0)
    scale = math.sqrt(2.0 / size)
    ids = seg[...]
    length = ids.shape[1]
    last = jnp.where(ids == ids[:, length - 1 :], 1.0, 0.0)
    gates = [None] + [gates_in[m][:1] for m in range(partners)]
    tall = size + EXTRA
    row_s = lax.broadcasted_iota(jnp.int32, (tall, size), 0)
    row_d = lax.broadcasted_iota(jnp.int32, (EXTRA, length), 0)
    ones = jnp.where(row_d < 2, 1.0, 0.0).astype(B16)
    dks, dvs = [], []
    for pair in range(GROUP // 2):
        later = joined(came, gates, pair)
        for h in (2 * pair, 2 * pair + 1):
            rows = slice(h * size, (h + 1) * size)
            g = later[:, (h % 2) * size : (h % 2 + 1) * size]
            n_high, n_low = halves(g[size : size + 1])
            ext = jnp.where(row_s < size, g, jnp.where(row_s == size, n_high, 0.0))
            ext = (ext + jnp.where(row_s == size + 1, n_low, 0.0)).astype(B16)
            v_ext = jnp.concatenate([v_low[rows], ones], axis=0)
            dks.append(dk[rows] + last * dot(ext, v_ext, TN))
            dvs.append(dv[rows] + last * dot(ext[:size], k_feat[rows], NN))
    d_feats = (dq[...], jnp.concatenate(dks, axis=0))
    pieces = []
    total = None
    for side, d_feat in enumerate(d_feats):
        t1 = d_feat * expo[side]
        total = t1 if total is None else total + t1
        d_expo = weight * t1
        d_x = dot(proj[...], d_expo, NN, HIGH) - scaled[side] * head_sums(d_expo, size)
        heads = d_x.shape[0] // size
        d_x = rotate((d_x * scale).reshape(heads, size, length), angle[0], angle[1], True)
        pieces.append(d_x.reshape(heads * size, length).astype(B16))
    pieces.append(jnp.concatenate(dvs, axis=0).astype(B16))

    @pl.when(step == 0)
    def _():
        small[...] = jnp.zeros(small.shape, F32) if opens else small_in[...]
        if opens:
            for r in range(up_bias.shape[1] // first_t.shape[0]):
                part = slice(r * first_t.shape[0], (r + 1) * first_t.shape[0])
                small[9 + r : 10 + r, :] = up_bias[:, part]

    total = jnp.broadcast_to(jnp.sum(total, axis=1, keepdims=True), (tile, 128))
    small[8:9, columns] = total.T[:1]
    one_row = jnp.ones((8, length), B16)
    part = None
    for m, (piece, w) in enumerate(zip(pieces, (wq, wk, wv))):
        g = dot(first_t[there, :], piece, NT)
        send[:, m] = g.reshape(count, TILE, tile)
        g = dot(first_t[here, :], piece, NT)
        keep[:, m] = g.reshape(count, TILE, tile)
        small[5 + m : 6 + m, columns] = dot(one_row, piece, NT)[:1]
        d = dot(w[...], piece, NN)
        part = d if part is None else part + d
    send[:, 3] = dot(att[there, :], cot_col[...], NN).reshape(count, TILE, tile)
    keep[:, 3] = dot(att[here, :], cot_col[...], NN).reshape(count, TILE, tile)

    @pl.when(step == 0)
    def _():
        acc[...] = part if opens else acc_in[...] + part

    @pl.when(step > 0)
    def _():
        acc[...] += part

    if not closes:
        return
    tok_grad = refs[4]

    @pl.when(step == pl.num_programs(0) - 1)
    def _():
        d_first = acc[...].T
        d_sec = d_second[...]
        xhat, rstd = normalise(tok[...])
        cotangent = cot[...].astype(F32)
        for r, x in enumerate((d_first * xhat, d_first, d_sec * xhat, d_sec, cotangent)):
            small[r : r + 1, :] = jnp.sum(x, axis=0, keepdims=True)
        e = d_first * vec_all[0:1] + d_sec * vec_all[2:3]
        mean_e = jnp.mean(e, axis=-1, keepdims=True)
        mean_x = jnp.mean(e * xhat, axis=-1, keepdims=True)
        tok_grad[...] = (cotangent + rstd * (e - mean_e - xhat * mean_x)).astype(B16)


def backward(
    dq, dk, dv, k_feat, v_low, scaled, expo, vec, in_weight, first_t, att, cot, proj, angle,
    seg, tok, d_second, came, gates, up_bias, bits, size, groups, so_far, deps,
):
    width, length = dq.shape
    tile = GROUP * size
    steps = width // tile
    begin, some = groups
    opens, closes = begin == 0, begin + some == steps
    carried = [] if opens else [so_far[3], so_far[2]]
    kept = so_far[:2]
    pairs = GROUP // 2
    partners = len(came)
    rows = pl.BlockSpec((tile, length), lambda g: (begin + g, 0))
    two = pl.BlockSpec((2, tile, length), lambda g: (0, begin + g, 0))
    column = lambda k: pl.BlockSpec((width, tile), lambda g: (0, k * steps + begin + g))
    packed = pl.BlockSpec((pairs, size + EXTRA, 2 * size), lambda g: (begin + g, 0, 0))
    count = width // TILE // 2
    return pl.pallas_call(
        ordered(
            functools.partial(backward_kernel, size, partners, opens, closes),
            24 + partners + len(carried),
            kept + deps,
        ),
        grid=(some,),
        in_specs=[
            rows, rows, rows, rows, rows, two, two,
            pl.BlockSpec((8, tile), lambda g: (0, begin + g)),
            column(0), column(1), column(2),
            full(first_t.shape), full(att.shape),
            pl.BlockSpec((length, tile), lambda g: (0, begin + g)),
            full((tile, tile)),
            full(angle.shape), full(seg.shape),
            full(tok.shape), full(cot.shape), full(d_second.shape), full(vec.shape),
        ]
        + [packed] * partners
        + [full(gates.shape), full(up_bias.shape), pl.BlockSpec(memory_space=pltpu.SMEM)]
        + [full(x.shape) for x in carried]
        + unused(kept + deps),
        out_specs=[
            pl.BlockSpec((count, 4, TILE, tile), lambda g: (0, 0, 0, begin + g)),
            pl.BlockSpec((count, 4, TILE, tile), lambda g: (0, 0, 0, begin + g)),
            full((16, width)),
            full((width, length)),
            full(tok.shape),
        ][: 4 + closes],
        out_shape=[
            jax.ShapeDtypeStruct((count, 4, TILE, width), F32),
            jax.ShapeDtypeStruct((count, 4, TILE, width), F32),
            jax.ShapeDtypeStruct((16, width), F32),
            jax.ShapeDtypeStruct((width, length), F32),
            jax.ShapeDtypeStruct(tok.shape, B16),
        ][: 4 + closes],
        input_output_aliases={24 + partners + len(carried) + k: k for k in range(len(kept))},
        compiler_params=params(20 * MIB),
        cost_estimate=FREE,
        name="backward",
    )(dq, dk, dv, k_feat, v_low, scaled, expo, vec, in_weight, in_weight, in_weight, first_t,
      att, cot, proj, angle, seg, tok, cot, d_second, vec, *came, gates, up_bias, bits, *carried, *kept, *deps)


def per_device(
    tokens,
    segment_ids,
    span_starts,
    first_gain,
    first_shift,
    second_gain,
    second_shift,
    input_weight,
    input_bias,
    feature_freq,
    feature_weight,
    output_weight,
    output_bias,
    up_weight,
    up_bias,
    down_weight,
    down_bias,
    cotangent,
):
    seq_count, length, width = tokens.shape
    assert seq_count == 1
    heads, size = feature_weight.shape
    tok, cot = tokens[0], cotangent[0]
    seqs, batches = lax.axis_size("seq"), lax.axis_size("batch")
    place = lax.axis_index("seq").reshape(1)
    seg = segment_ids.reshape(1, length)
    seg_col = segment_ids.reshape(length, 1)
    start = span_starts[0, :1]
    small = (
        first_gain, first_shift, second_gain, second_shift, input_bias,
        feature_weight.reshape(1, -1), up_bias,
    )
    first_t, second, second_t, proj, proj_t, angle, vec, up_bias_row = norms(
        place * length, tok, small, feature_freq
    )
    active, d_hidden, down_grad, up_bias_grad = mlp_part(
        second, cot, up_weight, up_bias_row, down_weight, 512
    )
    down_sum = lax.psum(down_grad, AXES)
    core = bit_groups()[0][0]
    bits = device_bits()
    up_shapes = [(TILE, up_weight.shape[1])]
    attn_shapes = [(TILE, 3 * width), (TILE, width)]

    def rest(first_t, second_t, active, d_hidden):
        up_send = up_half(bits, core, False, second_t, d_hidden, [])
        up_keep = up_half(bits, core, True, second_t, d_hidden, [up_send])
        up = Reduction(bits, up_send, up_keep, 3)
        q_feat, k_feat, v_low, scaled, expo, summary = features(
            first_t, input_weight, vec, proj_t, angle, seg, start, size, [up_keep]
        )
        states = from_partners(summary)
        mlp_out, d_second = mlp_tail(active, d_hidden, up_weight, down_weight, [summary])
        last = up.scatter(0, [mlp_out] + states)
        groups = heads // GROUP
        att, dq, dk, dv, here, gates = attention(
            place, start, q_feat, k_feat, v_low, output_weight, cot, seg, seg_col, states, size,
            (0, groups), [], last,
        )
        later = from_partners(here)
        result = results(tok, att, output_weight, mlp_out, output_bias, down_bias, [])
        last = up.scatter(1, [result] + later)
        fixed = (
            dq, dk, dv, k_feat, v_low, scaled, expo, vec, input_weight, first_t, att, cot, proj,
            angle, seg, tok, d_second, later, gates, up_bias_grad, bits, size,
        )
        some = list(backward(*fixed, (0, groups - 1), [], last))
        last = up.scatter(2, some[:1])
        send, keep, small, _, tok_grad = backward(*fixed, (groups - 1, 1), some, last)
        attn = Reduction(bits, send, keep, 3, small.reshape(1, 2, 8, width))
        last = up.exchange([tok_grad])
        last = attn.scatter(0, last)
        last = attn.scatter(1, last)
        last = attn.scatter(2, last)
        last = attn.exchange(last)
        last = up.settle(last)
        last = up.gather(2, last)
        last = attn.settle(last)
        last = up.gather(1, last)
        last = attn.gather(2, last)
        last = up.gather(0, last)
        last = attn.gather(1, last)
        last = up.finish_own(move_up, up_shapes, last)
        last = attn.gather(0, last)
        last = attn.finish_own(move_attention, attn_shapes, last)
        (up_sum,) = up.finish(move_up, up_shapes, last)
        in_sum, out_sum = attn.finish(move_attention, attn_shapes, [up_sum])
        return result, tok_grad, up_sum, in_sum, out_sum, attn.small.reshape(16, width)

    def nothing(first_t, second_t, active, d_hidden):
        low = jnp.zeros(tok.shape, B16)
        return (
            low, low, jnp.zeros(up_weight.shape, F32), jnp.zeros(input_weight.shape, F32),
            jnp.zeros(output_weight.shape, F32), jnp.zeros((16, width), F32),
        )

    result, tok_grad, up_sum, in_sum, out_sum, sums = lax.cond(
        start[0] < 2, rest, nothing, first_t, second_t, active, d_hidden
    )
    return (
        result[None],
        tok_grad[None],
        sums[0],
        sums[1],
        sums[2],
        sums[3],
        in_sum,
        sums[5:8].reshape(-1),
        sums[8].reshape(heads, size),
        out_sum,
        sums[4],
        up_sum,
        sums[9 : 9 + up_weight.shape[1] // width].reshape(-1),
        down_sum,
        sums[4],
    )


def solution(mesh):
    in_specs = (
        P("batch", "seq", None),
        P("batch", "seq"),
        P("batch", "seq"),
        P(),
        P(),
        P(),
        P(),
        P(),
        P(),
        P(),
        P(),
        P(),
        P(),
        P(),
        P(),
        P(),
        P(),
        P("batch", "seq", None),
    )
    out_specs = (
        P("batch", "seq", None),
        P("batch", "seq", None),
        P(),
        P(),
        P(),
        P(),
        P(),
        P(),
        P(),
        P(),
        P(),
        P(),
        P(),
        P(),
        P(),
    )
    return jax.shard_map(
        per_device, mesh=mesh, in_specs=in_specs, out_specs=out_specs, check_vma=False
    )
```

```python
import functools
import math

import jax
import jax.numpy as jnp
import numpy as np
from jax import lax
from jax.experimental import pallas as pl
from jax.experimental.pallas import tpu as pltpu
from jax.sharding import PartitionSpec as P

ROT = 16
HIGH = lax.Precision.HIGHEST
EPSILON = 1e-05
ROT_BASE = 10000.0
F32 = jnp.float32
B16 = jnp.bfloat16
GROUP = 4
EXTRA = 16
NN, NT, TN = ((1,), (0,)), ((1,), (1,)), ((0,), (0,))
TILE = 8
MIB = 1024 * 1024
STEP_LIMIT = 10 * MIB
BIG_LIMIT = 60 * MIB
FREE = pl.CostEstimate(flops=0, bytes_accessed=0, transcendentals=0)

AXES = ("seq", "batch")


def bit_groups():
    seqs, batches = lax.axis_size("seq"), lax.axis_size("batch")
    seq_bits = [batches << k for k in range(seqs.bit_length() - 1)]
    batch_bits = [1 << k for k in range(batches.bit_length() - 1)]
    return batch_bits[:1], seq_bits, batch_bits[1:]


def own_index():
    return lax.axis_index("seq") * lax.axis_size("batch") + lax.axis_index("batch")


def swap(array, bit):
    count = lax.axis_size("seq") * lax.axis_size("batch")
    return lax.ppermute(array, AXES, [(i, i ^ bit) for i in range(count)])


def bit_value(bit):
    return (own_index() & bit) // bit


def device_bits():
    core, seqs, rest = bit_groups()
    count = len(core + seqs + rest)
    return (own_index() >> jnp.arange(count, dtype=jnp.int32)) & 1


def place_of(at, bits):
    total = at.get(0, 0)
    for bit, factor in at.items():
        if bit:
            total = total + factor * bits[bit.bit_length() - 1]
    return total


def shifted(at, bit, factor):
    moved = dict(at)
    moved[bit] = moved.get(bit, 0) + factor
    return moved


def block_spec(shape, block, index):
    tail = (0,) * (len(shape) - 1)
    return pl.BlockSpec((block,) + tuple(shape[1:]), lambda i, bits: (index(i, bits),) + tail)


def sum_tiles(bits, outputs, deps):
    totals = [sum(count for count, _ in segments) for _, segments in outputs]
    arrays, specs, plan, out_specs, out_shape = [], [], [], [], []
    for owner, (block, segments) in enumerate(outputs):
        begin = 0
        for count, terms in segments:
            blocks, slots = count // block, []
            for array, at in terms:
                at = {bit: factor // block for bit, factor in at.items()}

                def index(i, bits, at=at, begin=begin, blocks=blocks):
                    return place_of(at, bits) + jnp.clip(i - begin, 0, blocks - 1)

                specs.append(block_spec(array.shape, block, index))
                slots.append(len(arrays))
                arrays.append(array)
            plan.append((owner, begin, blocks, slots))
            begin += blocks
        shape = (totals[owner],) + arrays[-1].shape[1:]
        out_shape.append(jax.ShapeDtypeStruct(shape, F32))
        out_specs.append(block_spec(shape, block, lambda i, bits, n=begin: jnp.minimum(i, n - 1)))
    steps = max(begin + blocks for _, begin, blocks, _ in plan)

    def kernel(_, *refs):
        ins, outs = refs[: len(arrays)], refs[len(arrays) + len(deps) :]
        i = pl.program_id(0)
        for owner, begin, blocks, slots in plan:

            def add(owner=owner, slots=slots):
                total = ins[slots[0]][...]
                for slot in slots[1:]:
                    total = total + ins[slot][...]
                outs[owner][...] = total

            if begin == 0 and blocks == steps:
                add()
            else:
                pl.when((i >= begin) & (i < begin + blocks))(add)

    got = pl.pallas_call(
        kernel,
        grid_spec=pltpu.PrefetchScalarGridSpec(
            num_scalar_prefetch=1,
            grid=(steps,),
            in_specs=specs + unused(deps),
            out_specs=out_specs,
        ),
        out_shape=out_shape,
        compiler_params=params(STEP_LIMIT),
        cost_estimate=FREE,
        name="sum_tiles",
    )(bits, *arrays, *deps)
    return list(got)


def interleave(bits, pairs, count, order, merge, block, deps):
    shape = pairs[0][0][0].shape[1:]
    groups = len(pairs)
    tail = (0,) * len(shape)
    flat = [x for pair in pairs for x in pair]

    def kernel(bits, *refs):
        ins, outs = refs[: 2 * groups], refs[2 * groups + len(deps) :]
        for g, bit in enumerate(order):
            out = outs[0].at[g] if merge else outs[g]
            mine = bits[bit.bit_length() - 1]
            out[pl.ds(mine, 1)] = ins[2 * g][...][None]
            out[pl.ds(1 - mine, 1)] = ins[2 * g + 1][...][None]

    if merge:
        out_specs = [
            pl.BlockSpec((groups, 2, block) + shape, lambda i, bits: (0, 0, i) + tail)
        ]
        out_shape = [jax.ShapeDtypeStruct((groups, 2, count) + shape, F32)]
    else:
        out_specs = [pl.BlockSpec((2, block) + shape, lambda i, bits: (0, i) + tail)] * groups
        out_shape = [jax.ShapeDtypeStruct((2, count) + shape, F32)] * groups
    got = pl.pallas_call(
        kernel,
        grid_spec=pltpu.PrefetchScalarGridSpec(
            num_scalar_prefetch=1,
            grid=(count // block,),
            in_specs=[
                block_spec(x.shape, block, lambda i, bits, at=at: at // block + i) for x, at in flat
            ]
            + unused(deps),
            out_specs=out_specs,
        ),
        out_shape=out_shape,
        compiler_params=params(STEP_LIMIT),
        cost_estimate=FREE,
        name="interleave",
    )(bits, *[x for x, _ in flat], *deps)
    if merge:
        return got[0].reshape((groups * 2 * count,) + shape)
    return [x.reshape((2 * count,) + shape) for x in got]


def put_half(bits, bit, own, part, shapes, moves, into, deps, chunks=6):
    half = part.shape[0]
    rows = half // chunks
    at = bit.bit_length() - 1
    count = len(shapes) if len(shapes) == 1 else 4

    def kernel(bits, part, *refs):
        outs, buffer, in_sems, out_sems = refs[len(into) + len(deps) : -3], *refs[-3:]
        which = bits[at] if own else 1 - bits[at]
        spans = [pl.ds(c * rows, rows) for c in range(chunks)]
        coming = [
            pltpu.make_async_copy(part.at[span], buffer.at[span], in_sems.at[c])
            for c, span in enumerate(spans)
        ]
        going = [
            [
                pltpu.make_async_copy(a, b, out_sems.at[c * count + m])
                for m, (a, b) in enumerate(moves(buffer, outs, which, span))
            ]
            for c, span in enumerate(spans)
        ]
        for copy in coming:
            copy.start()
        for copy, onward in zip(coming, going):
            copy.wait()
            for out in onward:
                out.start()
        for onward in going:
            for out in onward:
                out.wait()

    got = pl.pallas_call(
        kernel,
        grid_spec=pltpu.PrefetchScalarGridSpec(
            num_scalar_prefetch=1,
            grid=(1,),
            in_specs=unused([part] + into + deps),
            out_specs=unused(shapes),
            scratch_shapes=[
                pltpu.VMEM(part.shape, F32),
                pltpu.SemaphoreType.DMA((chunks,)),
                pltpu.SemaphoreType.DMA((chunks * count,)),
            ],
        ),
        out_shape=[jax.ShapeDtypeStruct((2, half) + s, F32) for s in shapes],
        input_output_aliases={2 + k: k for k in range(len(into))},
        compiler_params=params(STEP_LIMIT),
        cost_estimate=FREE,
        name="put_half",
    )(bits, part, *into, *deps)
    return list(got)


def move_up(part, outs, half, rows):
    return [(part.at[rows], outs[0].at[half, rows])]


def move_attention(part, outs, half, rows):
    width = part.shape[-1]
    pieces = [outs[0].at[half, rows, :, pl.ds(m * width, width)] for m in range(3)]
    pieces.append(outs[1].at[half, rows])
    return [(part.at[rows, m], piece) for m, piece in enumerate(pieces)]


def block_of(count, most):
    return max(b for b in range(1, most + 1) if count % b == 0)


class Reduction:
    def __init__(self, bits, send, keep, groups, small=None):
        core, seqs, rest = bit_groups()
        ring = seqs + rest[:1] if groups == 3 else seqs
        self.bits = bits
        self.core, self.tail = core[0], rest[1:]
        self.merged = None if groups == 3 else rest[0]
        self.orders = [ring[k:] + ring[:k] for k in range(groups)]
        self.last = len(ring) - 1
        self.left = keep.shape[0] // groups
        came = swap(send, self.core)
        self.terms = [
            [(keep, {0: g * self.left}), (came, {0: g * self.left})] for g in range(groups)
        ]
        self.small = small
        if small is not None:
            self.small_bits = seqs + rest
            self.small_came = swap(small, self.core)

    def small_output(self):
        return [] if self.small is None else [(1, [(1, [(self.small, {}), (self.small_came, {})])])]

    def small_next(self, small):
        if small:
            (self.small,) = small
            bits = self.small_bits
            if bits:
                self.small_came, self.small_bits = swap(self.small, bits[0]), bits[1:]

    def scatter(self, step, deps):
        self.left //= 2
        block = block_of(self.left, max(min(3, self.left // 2), 1))
        outputs = []
        for g, order in enumerate(self.orders):
            bit = order[step]
            terms = [
                (t, shifted(shifted(at, 0, self.left), bit, -self.left)) for t, at in self.terms[g]
            ]
            outputs.append((block, [(self.left, terms)]))
        sends = sum_tiles(self.bits, outputs + self.small_output(), deps)
        for g, order in enumerate(self.orders):
            bit = order[step]
            came = swap(sends[g], bit)
            self.terms[g] = [(t, shifted(at, bit, self.left)) for t, at in self.terms[g]]
            self.terms[g].append((came, {}))
        self.small_next(sends[len(self.orders) :])
        return sends[:1]

    def merge(self, deps):
        self.left //= 2
        bit, segments = self.merged, []
        for terms in self.terms:
            terms = [(t, shifted(shifted(at, 0, self.left), bit, -self.left)) for t, at in terms]
            segments.append((self.left, terms))
        send, *small = sum_tiles(self.bits, [(self.left, segments)] + self.small_output(), deps)
        self.small_next(small)
        came = swap(send, bit)
        for g, terms in enumerate(self.terms):
            self.terms[g] = [(t, shifted(at, bit, self.left)) for t, at in terms]
            self.terms[g].append((came, {0: g * self.left}))
        return [send]

    def exchange(self, deps):
        segments = [(self.left, terms) for terms in self.terms]
        total, *small = sum_tiles(self.bits, [(self.left, segments)] + self.small_output(), deps)
        self.small_next(small)
        first = total
        for bit in self.tail[:-1]:
            total = total + swap(total, bit)
            if small:
                self.small_next([self.small + self.small_came])
        self.both = (total, swap(total, self.tail[-1]))
        return [first]

    def settle(self, deps):
        groups = len(self.orders)
        if self.merged:
            count = groups * self.left
            outputs = [(self.left, [(count, [(x, {}) for x in self.both])])]
        else:
            outputs = [
                (self.left, [(self.left, [(x, {0: g * self.left}) for x in self.both])])
                for g in range(groups)
            ]
        got = sum_tiles(self.bits, outputs + self.small_output(), deps)
        self.pieces = got[: len(outputs)]
        self.small_next(got[len(outputs) :])
        if self.merged:
            self.came = [swap(self.pieces[0], self.merged)]
        else:
            self.next_swap(self.last)
        return self.pieces[:1]

    def next_swap(self, step):
        self.came = [swap(p, order[step]) for p, order in zip(self.pieces, self.orders)]

    def unmerge(self, deps):
        groups = len(self.orders)
        pairs = [
            ((self.pieces[0], g * self.left), (self.came[0], g * self.left)) for g in range(groups)
        ]
        self.pieces = interleave(
            self.bits, pairs, self.left, [self.merged] * groups, False, self.left, deps
        )
        self.next_swap(self.last)
        return self.pieces[:1]

    def gather(self, step, deps):
        pairs = [((a, 0), (b, 0)) for a, b in zip(self.pieces, self.came)]
        count = self.pieces[0].shape[0]
        order = [o[step] for o in self.orders]
        block = block_of(count, max(min(3, count // 2), 1))
        self.pieces = interleave(self.bits, pairs, count, order, step == 0, block, deps)
        if step:
            self.next_swap(step - 1)
            return self.pieces[:1]
        self.came = swap(self.pieces, self.core)
        return [self.pieces]

    def finish_own(self, how, shapes, deps):
        self.out = put_half(self.bits, self.core, True, self.pieces, shapes, how, [], deps)
        return self.out[:1]

    def finish(self, how, shapes, deps):
        got = put_half(self.bits, self.core, False, self.came, shapes, how, self.out, deps)
        return [g.reshape(-1, s[-1]) for g, s in zip(got, shapes)]


def from_partners(array):
    return [swap(array, m * lax.axis_size("batch")) for m in range(1, lax.axis_size("seq"))]


def cosine_table(points):
    index = np.arange(points, dtype=np.float64)
    table = np.cos(math.pi * (index[None, :] + 0.5) * index[:, None] / points) * math.sqrt(
        2.0 / points
    )
    return (table * np.where(index[:, None] == 0, math.sqrt(0.5), 1.0)).astype(np.float32)


def rotary_freq():
    return (ROT_BASE ** (-2.0 * np.arange(ROT // 2) / ROT)).astype(np.float32)


def dot(a, b, dims, precision=None):
    return lax.dot_general(a, b, (dims, ((), ())), preferred_element_type=F32, precision=precision)


def params(limit):
    return pltpu.CompilerParams(vmem_limit_bytes=limit)


def ordered(kernel, count, deps):
    def run(*refs):
        kernel(*refs[:count], *refs[count + len(deps) :])

    return run


def unused(deps):
    return [pl.BlockSpec(memory_space=pl.ANY)] * len(deps)


def full(shape):
    return pl.BlockSpec(shape, lambda *_: (0,) * len(shape))


def normalise(tokens):
    values = tokens.astype(F32)
    centre = jnp.mean(values, axis=-1, keepdims=True)
    centred = values - centre
    spread = jnp.mean(centred * centred, axis=-1, keepdims=True)
    rstd = lax.rsqrt(spread + EPSILON)
    return centred * rstd, rstd


def norm_kernel(
    offset, tok, g1, s1, g2, s2, in_bias, feat_weight, up_bias_in, table_t, freq, turns,
    first_t, second, second_t, proj, proj_t, angle, vec, up_bias,
):
    width = tok.shape[1]
    for r, ref in enumerate((g1, s1, g2, s2)):
        vec[r : r + 1] = ref[...].reshape(1, width)
    for r in range(3):
        vec[4 + r : 5 + r] = in_bias[r * width : (r + 1) * width].reshape(1, width)
    heads = feat_weight.shape[0]
    vec[7:8] = jnp.concatenate([feat_weight[h : h + 1] for h in range(heads)], axis=1)
    up_bias[...] = up_bias_in[...].reshape(up_bias.shape)
    xhat, _ = normalise(tok[...])
    one = (xhat * vec[0:1] + vec[1:2]).astype(B16)
    two = (xhat * vec[2:3] + vec[3:4]).astype(B16)
    second[...] = two
    first_t[...] = one.T
    second_t[...] = two.T
    table = dot(table_t[...], freq[...], NN, HIGH)
    size = table.shape[0]
    wide = GROUP * size
    row = lax.broadcasted_iota(jnp.int32, (wide, wide), 0) // size
    same = row == lax.broadcasted_iota(jnp.int32, (wide, wide), 1) // size
    for out, block in ((proj, table), (proj_t, table.T)):
        block = jnp.concatenate([block] * GROUP, axis=1)
        out[...] = jnp.where(same, jnp.concatenate([block] * GROUP, axis=0), 0.0)
    length = tok.shape[0]
    at = lax.broadcasted_iota(jnp.int32, (ROT // 2, length), 1) + offset[0]
    turn = at.astype(F32) * turns[...]
    angle[0] = jnp.cos(turn)
    angle[1] = jnp.sin(turn)


def norms(offset, tok, small, freq):
    rows, width = tok.shape
    size = freq.shape[0]
    wide = GROUP * size
    return pl.pallas_call(
        norm_kernel,
        in_specs=[pl.BlockSpec(memory_space=pltpu.SMEM)] + [pl.BlockSpec()] * (4 + len(small)),
        out_shape=(
            jax.ShapeDtypeStruct((width, rows), B16),
            jax.ShapeDtypeStruct((rows, width), B16),
            jax.ShapeDtypeStruct((width, rows), B16),
            jax.ShapeDtypeStruct((wide, wide), F32),
            jax.ShapeDtypeStruct((wide, wide), F32),
            jax.ShapeDtypeStruct((2, ROT // 2, rows), F32),
            jax.ShapeDtypeStruct((8, width), F32),
            jax.ShapeDtypeStruct((1, small[-1].size), F32),
        ),
        compiler_params=params(BIG_LIMIT),
        name="norms",
    )(offset, tok, *small, jnp.asarray(cosine_table(size).T), freq,
      jnp.asarray(rotary_freq()[:, None]))


def mlp_kernel(second, cot, up, up_bias, down, act, d_hidden, down_grad, bias_grad):
    hidden = dot(second[...], up[...], NN) + up_bias[...]
    phi = 0.5 + 0.5 * lax.erf(hidden * math.sqrt(0.5))
    density = jnp.exp(hidden * hidden * -0.5) * (1.0 / math.sqrt(2.0 * math.pi))
    active = (hidden * phi).astype(B16)
    d_active = dot(cot[...], down[...], NT)
    d_low = (d_active * (phi + hidden * density)).astype(B16)
    act[...] = active
    d_hidden[...] = d_low
    down_grad[...] = dot(active, cot[...], TN)
    bias_grad[...] = jnp.sum(d_low.astype(F32), axis=0, keepdims=True)


def mlp_part(second, cot, up, up_bias, down, tile):
    rows, width = second.shape
    hidden = up.shape[1]
    return pl.pallas_call(
        mlp_kernel,
        grid=(hidden // tile,),
        in_specs=[
            full((rows, width)),
            full((rows, width)),
            pl.BlockSpec((width, tile), lambda j: (0, j)),
            pl.BlockSpec((1, tile), lambda j: (0, j)),
            pl.BlockSpec((tile, width), lambda j: (j, 0)),
        ],
        out_specs=[
            pl.BlockSpec((rows, tile), lambda j: (0, j)),
            pl.BlockSpec((rows, tile), lambda j: (0, j)),
            pl.BlockSpec((tile, width), lambda j: (j, 0)),
            pl.BlockSpec((1, tile), lambda j: (0, j)),
        ],
        out_shape=(
            jax.ShapeDtypeStruct((rows, hidden), B16),
            jax.ShapeDtypeStruct((rows, hidden), B16),
            pltpu.HBM((hidden, width), F32),
            jax.ShapeDtypeStruct((1, hidden), F32),
        ),
        compiler_params=params(18 * MIB),
        name="mlp",
    )(second, cot, up, up_bias, down)


def up_kernel(at, second_t, d_hidden, out):
    g = dot(second_t[...], d_hidden[...], NN)
    out[...] = g.reshape(out.shape)


def up_half(bits, bit, own, second_t, d_hidden, deps, steps=6):
    width, length = second_t.shape
    hidden = d_hidden.shape[1]
    half, tile = width // 2, hidden // steps
    at = bit.bit_length() - 1
    which = lambda bits: bits[at] if own else 1 - bits[at]
    return pl.pallas_call(
        ordered(up_kernel, 3, deps),
        grid_spec=pltpu.PrefetchScalarGridSpec(
            num_scalar_prefetch=1,
            grid=(steps,),
            in_specs=[
                pl.BlockSpec((half, length), lambda j, bits: (which(bits), 0)),
                pl.BlockSpec((length, tile), lambda j, bits: (0, j)),
            ]
            + unused(deps),
            out_specs=pl.BlockSpec((half // TILE, TILE, tile), lambda j, bits: (0, 0, j)),
        ),
        out_shape=jax.ShapeDtypeStruct((half // TILE, TILE, hidden), F32),
        compiler_params=params(10 * MIB),
        cost_estimate=FREE,
        name="up_half",
    )(bits, second_t, d_hidden, *deps)


def tail_kernel(active, d_hidden, up, down, out, d_second):
    one = dot(active[...], down[...], NN)
    two = dot(d_hidden[...], up[...], NT)

    @pl.when(pl.program_id(0) == 0)
    def _():
        out[...] = one
        d_second[...] = two

    @pl.when(pl.program_id(0) > 0)
    def _():
        out[...] += one
        d_second[...] += two


def mlp_tail(active, d_hidden, up, down, deps, steps=6):
    rows, hidden = active.shape
    width = up.shape[0]
    tile = hidden // steps
    wide = jax.ShapeDtypeStruct((rows, width), F32)
    return pl.pallas_call(
        ordered(tail_kernel, 4, deps),
        grid=(steps,),
        in_specs=[
            pl.BlockSpec((rows, tile), lambda j: (0, j)),
            pl.BlockSpec((rows, tile), lambda j: (0, j)),
            pl.BlockSpec((width, tile), lambda j: (0, j)),
            pl.BlockSpec((tile, width), lambda j: (j, 0)),
        ]
        + unused(deps),
        out_specs=[full((rows, width)), full((rows, width))],
        out_shape=(wide, wide),
        compiler_params=params(14 * MIB),
        cost_estimate=FREE,
        name="mlp_tail",
    )(active, d_hidden, up, down, *deps)


def result_kernel(tok, att, w_out, mlp_out, out_bias, down_bias, result):
    attn_out = dot(att[...], w_out[...], TN) + out_bias[...].reshape(1, -1)
    result[...] = (tok[...].astype(F32) + attn_out + (mlp_out[...] + down_bias[...].reshape(1, -1))).astype(B16)


def results(tok, att, w_out, mlp_out, out_bias, down_bias, deps):
    return pl.pallas_call(
        ordered(result_kernel, 6, deps),
        in_specs=[pl.BlockSpec()] * 6 + unused(deps),
        out_shape=jax.ShapeDtypeStruct(tok.shape, B16),
        compiler_params=params(10 * MIB),
        cost_estimate=FREE,
        name="results",
    )(tok, att, w_out, mlp_out, out_bias, down_bias, *deps)


def rotate(x, cosine, sine, back):
    half = ROT // 2
    a, b = x[:, :half], x[:, half:ROT]
    sine = -sine if back else sine
    return jnp.concatenate([a * cosine - b * sine, b * cosine + a * sine, x[:, ROT:]], axis=1)


def head_sums(x, size):
    cut = x.reshape(x.shape[0] // size, size, x.shape[1])
    total = jnp.sum(cut, axis=1, keepdims=True)
    return jnp.broadcast_to(total, cut.shape).reshape(x.shape)


def feature_kernel(
    size, first_t, wq, wk, wv, vec, proj_t, angle, seg, start,
    q_feat, k_feat, v_low, scaled, expo, summary,
):
    columns = vec[...].T
    bq, bk, bv, weight = (columns[:, c : c + 1] for c in range(4, 8))
    scale = math.sqrt(2.0 / size)
    feats = []
    for side, (w, bias, out) in enumerate(((wq, bq, q_feat), (wk, bk, k_feat))):
        x = dot(w[...], first_t[...], TN) + bias
        heads = x.shape[0] // size
        x = rotate(x.reshape(heads, size, x.shape[1]), angle[0], angle[1], False)
        sx = x.reshape(heads * size, x.shape[2]) * scale
        lifted = dot(proj_t[...], sx, NN, HIGH)
        e = jnp.exp(lifted - 0.5 * head_sums(sx * sx, size))
        phi = (weight * e).astype(B16)
        scaled[side] = sx
        expo[side] = e
        out[...] = phi
        feats.append(phi)
    value = (dot(wv[...], first_t[...], TN) + bv).astype(B16)
    v_low[...] = value
    ids = seg[...]
    length = ids.shape[1]
    last = (ids == ids[:, length - 1 :]).astype(F32)
    whole = jnp.where((ids[:, :1] == ids[:, length - 1 :]) & (start[0] == 0), 1.0, 0.0)
    key_last = (feats[1].astype(F32) * last).astype(B16)
    row = lax.broadcasted_iota(jnp.int32, (EXTRA, length), 0)
    ones = jnp.where(row == 0, 1.0, 0.0).astype(B16)
    tall = size + EXTRA
    rows = lax.broadcasted_iota(jnp.int32, (tall, 2 * size), 0)
    for pair in range(heads // 2):
        got = []
        for h in (2 * pair, 2 * pair + 1):
            v_ext = jnp.concatenate([value[h * size : (h + 1) * size], ones], axis=0)
            got.append(dot(v_ext, key_last[h * size : (h + 1) * size], NT))
        both = jnp.concatenate(got, axis=1)
        summary[pair] = jnp.where(rows == size + 1, whole, both)


def features(first_t, in_weight, vec, proj_t, angle, seg, start, size, deps):
    width, length = first_t.shape
    tile = GROUP * size
    steps = width // tile
    pairs = GROUP // 2
    column = lambda k: pl.BlockSpec((width, tile), lambda g: (0, k * steps + g))
    rows = pl.BlockSpec((tile, length), lambda g: (g, 0))
    two = pl.BlockSpec((2, tile, length), lambda g: (0, g, 0))
    low = jax.ShapeDtypeStruct((width, length), B16)
    wide = jax.ShapeDtypeStruct((2, width, length), F32)
    return pl.pallas_call(
        ordered(functools.partial(feature_kernel, size), 9, deps),
        grid=(steps,),
        in_specs=[
            full((width, length)),
            column(0), column(1), column(2),
            pl.BlockSpec((8, tile), lambda g: (0, g)),
            full((tile, tile)),
            full(angle.shape), full(seg.shape),
            pl.BlockSpec(memory_space=pltpu.SMEM),
        ]
        + unused(deps),
        out_specs=[
            rows, rows, rows, two, two,
            pl.BlockSpec((pairs, size + EXTRA, 2 * size), lambda g: (g, 0, 0)),
        ],
        out_shape=(
            low, low, low, wide, wide,
            jax.ShapeDtypeStruct((steps * pairs, size + EXTRA, 2 * size), F32),
        ),
        compiler_params=params(14 * MIB),
        cost_estimate=FREE,
        name="features",
    )(first_t, in_weight, in_weight, in_weight, vec, proj_t, angle, seg, start, *deps)


def chain_gates(flags, place, forward):
    count = len(flags)
    gates = [None]
    for m in range(1, count):
        other = place ^ m
        gate = jnp.where(other < place if forward else other > place, 1.0, 0.0)
        for n in range(1, count):
            if n != m:
                mid = place ^ n
                inside = (
                    (mid > other) & (mid < place) if forward else (mid < other) & (mid > place)
                )
                gate = gate * jnp.where(inside, flags[n], 1.0)
        gates.append(gate)
    return gates


def joined(refs, gates, pair):
    total = None
    for ref, gate in zip(refs, gates[1:]):
        term = jnp.where(gate != 0.0, ref[pair] * gate, 0.0)
        total = term if total is None else total + term
    return total


def halves(x):
    high = x.astype(B16).astype(F32)
    return high, x - high


def attention_kernel(size, partners, place, start, *refs):
    refs = list(refs)
    q_feat, k_feat, v_low, w_out, cot, seg, seg_col = refs[:7]
    came = refs[7 : 7 + partners]
    att, dq_out, dk_out, dv_out, here_out, gate_out, mask = refs[7 + partners :]
    length = seg.shape[1]
    block = 256
    ids = seg[...]

    @pl.when(pl.program_id(0) == 0)
    def _():
        key_at = lax.broadcasted_iota(jnp.int32, (length, length), 0)
        query_at = lax.broadcasted_iota(jnp.int32, (length, length), 1)
        same = (seg_col[...] == ids) & (key_at <= query_at)
        mask[...] = jnp.where(same, 1.0, 0.0)

    flags = [None] + [ref[0, size + 1 : size + 2, :] for ref in came]
    ahead = chain_gates(flags, place[0], True)
    behind = chain_gates(flags, place[0], False)
    for m in range(partners):
        gate_out[m] = jnp.broadcast_to(behind[m + 1], gate_out.shape[1:])
    keep = jnp.where((ids == ids[:, :1]) & (start[0] == 0), 1.0, 0.0)
    d_att = dot(w_out[...], cot[...], NT)
    tall = size + EXTRA
    row_s = lax.broadcasted_iota(jnp.int32, (tall, size), 0)
    row_d = lax.broadcasted_iota(jnp.int32, (EXTRA, length), 0)
    blocks = [(t * block, (t + 1) * block) for t in range(length // block)]
    for pair in range(GROUP // 2):
        state_pair = joined(came, ahead, pair)
        here_pair = []
        for h in (2 * pair, 2 * pair + 1):
            rows = slice(h * size, (h + 1) * size)
            state = state_pair[:, (h % 2) * size : (h % 2 + 1) * size]
            n_high, n_low = halves(state[size : size + 1])
            ext = jnp.where(row_s < size, state, 0.0)
            ext = ext + jnp.where((row_s == size) | (row_s == size + 2), n_high, 0.0)
            ext = (ext + jnp.where(row_s == size + 1, n_low, 0.0)).astype(B16)
            q, k, v = q_feat[rows], k_feat[rows], v_low[rows]
            outside = dot(ext, q, NN)
            scores, d_nums, d_dens = [], [], []
            for lo, hi in blocks:
                raw = dot(k[:, :hi], q[:, lo:hi], TN) * mask[:hi, lo:hi]
                s_low = raw.astype(B16)
                kept = keep[:, lo:hi]
                out_part = outside[:, lo:hi]
                denom = jnp.sum(raw, axis=0, keepdims=True) + kept * (
                    out_part[size : size + 1] + out_part[size + 1 : size + 2]
                )
                numer = dot(v[:, :hi], s_low, NN) + kept * out_part[:size]
                inverse = 1.0 / denom
                attended = numer * inverse
                da = d_att[rows, lo:hi]
                att[rows, lo:hi] = attended.astype(B16)
                d_nums.append((da * inverse).astype(B16))
                d_dens.append(-jnp.sum(da * attended, axis=0, keepdims=True) * inverse)
                scores.append(s_low)
            d_num = jnp.concatenate(d_nums, axis=1)
            d_den = jnp.concatenate(d_dens, axis=1)
            d_high, d_low = halves(d_den)
            tail = jnp.where(row_d < 2, d_high, jnp.where(row_d == 2, d_low, 0.0)).astype(B16)
            dn_ext = jnp.concatenate([d_num, tail], axis=0)
            dq_state = dot(ext, dn_ext, TN)
            dv_parts = [None] * len(blocks)
            dk_parts = [None] * len(blocks)
            for n, (lo, hi) in enumerate(blocks):
                d_score = dot(v[:, :hi], d_num[:, lo:hi], TN) + d_den[:, lo:hi]
                d_score = (d_score * mask[:hi, lo:hi]).astype(B16)
                dq_out[rows, lo:hi] = (
                    dot(k[:, :hi], d_score, NN) + keep[:, lo:hi] * dq_state[:, lo:hi]
                )
                for m in range(n + 1):
                    a, b = blocks[m]
                    dv = dot(d_num[:, lo:hi], scores[n][a:b], NT)
                    dk = dot(q[:, lo:hi], d_score[a:b], NT)
                    dv_parts[m] = dv if dv_parts[m] is None else dv_parts[m] + dv
                    dk_parts[m] = dk if dk_parts[m] is None else dk_parts[m] + dk
            for m, (a, b) in enumerate(blocks):
                dv_out[rows, a:b] = dv_parts[m]
                dk_out[rows, a:b] = dk_parts[m]
            here = dot((dn_ext.astype(F32) * keep).astype(B16), q, NT)
            norm = here[size : size + 1] + here[size + 2 : size + 3]
            here_pair.append(jnp.where(row_s < size, here, jnp.where(row_s == size, norm, 0.0)))
        here_out[pair] = jnp.concatenate(here_pair, axis=1)


def attention(
    place, start, q_feat, k_feat, v_low, w_out, cot, seg, seg_col, came, size, groups, so_far, deps
):
    width, length = q_feat.shape
    tile = GROUP * size
    steps = width // tile
    first, count = groups
    pairs = GROUP // 2
    partners = len(came)
    rows = pl.BlockSpec((tile, length), lambda g: (first + g, 0))
    packed = pl.BlockSpec((pairs, size + EXTRA, 2 * size), lambda g: (first + g, 0, 0))
    wide = jax.ShapeDtypeStruct((width, length), F32)
    return pl.pallas_call(
        ordered(functools.partial(attention_kernel, size, partners), 9 + partners, so_far + deps),
        grid=(count,),
        in_specs=[
            pl.BlockSpec(memory_space=pltpu.SMEM),
            pl.BlockSpec(memory_space=pltpu.SMEM),
            rows, rows, rows,
            pl.BlockSpec((tile, width), lambda g: (first + g, 0)),
            full(cot.shape), full(seg.shape), full(seg_col.shape),
        ]
        + [packed] * partners
        + unused(so_far + deps),
        out_specs=[rows, rows, rows, rows, packed, full((partners, 8, 2 * size))],
        out_shape=(
            jax.ShapeDtypeStruct((width, length), B16),
            wide, wide, wide,
            jax.ShapeDtypeStruct((steps * pairs, size + EXTRA, 2 * size), F32),
            jax.ShapeDtypeStruct((partners, 8, 2 * size), F32),
        ),
        scratch_shapes=[pltpu.VMEM((length, length), F32)],
        input_output_aliases={9 + partners + k: k for k in range(len(so_far))},
        compiler_params=params(16 * MIB),
        cost_estimate=FREE,
        name="attention",
    )(place, start, q_feat, k_feat, v_low, w_out, cot, seg, seg_col, *came, *so_far, *deps)


def backward_kernel(size, partners, opens, closes, *refs):
    refs = list(refs)
    (dq, dk, dv, k_feat, v_low, scaled, expo, vec, wq, wk, wv, first_t, att, cot_col, proj,
     angle, seg, tok, cot, d_second, vec_all) = refs[:21]
    came = refs[21 : 21 + partners]
    gates_in, up_bias, bits = refs[21 + partners : 24 + partners]
    refs = refs[24 + partners :]
    if not opens:
        acc_in, small_in = refs[:2]
        refs = refs[2:]
    send, keep, small, acc = refs[:4]
    first = 0 if opens else 2
    mine = bits[0]
    half = first_t.shape[0] // 2
    tile = dq.shape[0]
    here = pl.ds(pl.multiple_of(mine * half, half), half)
    there = pl.ds(pl.multiple_of((1 - mine) * half, half), half)
    columns = pl.ds(pl.multiple_of((first + pl.program_id(0)) * tile, tile), tile)
    count = send.shape[0]
    weight = vec[...].T[:, 7:8]
    step = pl.program_id(0)
    scale = math.sqrt(2.0 / size)
    ids = seg[...]
    length = ids.shape[1]
    last = jnp.where(ids == ids[:, length - 1 :], 1.0, 0.0)
    gates = [None] + [gates_in[m][:1] for m in range(partners)]
    tall = size + EXTRA
    row_s = lax.broadcasted_iota(jnp.int32, (tall, size), 0)
    row_d = lax.broadcasted_iota(jnp.int32, (EXTRA, length), 0)
    ones = jnp.where(row_d < 2, 1.0, 0.0).astype(B16)
    dks, dvs = [], []
    for pair in range(GROUP // 2):
        later = joined(came, gates, pair)
        for h in (2 * pair, 2 * pair + 1):
            rows = slice(h * size, (h + 1) * size)
            g = later[:, (h % 2) * size : (h % 2 + 1) * size]
            n_high, n_low = halves(g[size : size + 1])
            ext = jnp.where(row_s < size, g, jnp.where(row_s == size, n_high, 0.0))
            ext = (ext + jnp.where(row_s == size + 1, n_low, 0.0)).astype(B16)
            v_ext = jnp.concatenate([v_low[rows], ones], axis=0)
            dks.append(dk[rows] + last * dot(ext, v_ext, TN))
            dvs.append(dv[rows] + last * dot(ext[:size], k_feat[rows], NN))
    d_feats = (dq[...], jnp.concatenate(dks, axis=0))
    pieces = []
    total = None
    for side, d_feat in enumerate(d_feats):
        t1 = d_feat * expo[side]
        total = t1 if total is None else total + t1
        d_expo = weight * t1
        d_x = dot(proj[...], d_expo, NN, HIGH) - scaled[side] * head_sums(d_expo, size)
        heads = d_x.shape[0] // size
        d_x = rotate((d_x * scale).reshape(heads, size, length), angle[0], angle[1], True)
        pieces.append(d_x.reshape(heads * size, length).astype(B16))
    pieces.append(jnp.concatenate(dvs, axis=0).astype(B16))

    @pl.when(step == 0)
    def _():
        small[...] = jnp.zeros(small.shape, F32) if opens else small_in[...]
        if opens:
            for r in range(up_bias.shape[1] // first_t.shape[0]):
                part = slice(r * first_t.shape[0], (r + 1) * first_t.shape[0])
                small[9 + r : 10 + r, :] = up_bias[:, part]

    total = jnp.broadcast_to(jnp.sum(total, axis=1, keepdims=True), (tile, 128))
    small[8:9, columns] = total.T[:1]
    one_row = jnp.ones((8, length), B16)
    part = None
    for m, (piece, w) in enumerate(zip(pieces, (wq, wk, wv))):
        g = dot(first_t[there, :], piece, NT)
        send[:, m] = g.reshape(count, TILE, tile)
        g = dot(first_t[here, :], piece, NT)
        keep[:, m] = g.reshape(count, TILE, tile)
        small[5 + m : 6 + m, columns] = dot(one_row, piece, NT)[:1]
        d = dot(w[...], piece, NN)
        part = d if part is None else part + d
    send[:, 3] = dot(att[there, :], cot_col[...], NN).reshape(count, TILE, tile)
    keep[:, 3] = dot(att[here, :], cot_col[...], NN).reshape(count, TILE, tile)

    @pl.when(step == 0)
    def _():
        acc[...] = part if opens else acc_in[...] + part

    @pl.when(step > 0)
    def _():
        acc[...] += part

    if not closes:
        return
    tok_grad = refs[4]

    @pl.when(step == pl.num_programs(0) - 1)
    def _():
        d_first = acc[...].T
        d_sec = d_second[...]
        xhat, rstd = normalise(tok[...])
        cotangent = cot[...].astype(F32)
        for r, x in enumerate((d_first * xhat, d_first, d_sec * xhat, d_sec, cotangent)):
            small[r : r + 1, :] = jnp.sum(x, axis=0, keepdims=True)
        e = d_first * vec_all[0:1] + d_sec * vec_all[2:3]
        mean_e = jnp.mean(e, axis=-1, keepdims=True)
        mean_x = jnp.mean(e * xhat, axis=-1, keepdims=True)
        tok_grad[...] = (cotangent + rstd * (e - mean_e - xhat * mean_x)).astype(B16)


def backward(
    dq, dk, dv, k_feat, v_low, scaled, expo, vec, in_weight, first_t, att, cot, proj, angle,
    seg, tok, d_second, came, gates, up_bias, bits, size, groups, so_far, deps,
):
    width, length = dq.shape
    tile = GROUP * size
    steps = width // tile
    begin, some = groups
    opens, closes = begin == 0, begin + some == steps
    carried = [] if opens else [so_far[3], so_far[2]]
    kept = so_far[:2]
    pairs = GROUP // 2
    partners = len(came)
    rows = pl.BlockSpec((tile, length), lambda g: (begin + g, 0))
    two = pl.BlockSpec((2, tile, length), lambda g: (0, begin + g, 0))
    column = lambda k: pl.BlockSpec((width, tile), lambda g: (0, k * steps + begin + g))
    packed = pl.BlockSpec((pairs, size + EXTRA, 2 * size), lambda g: (begin + g, 0, 0))
    count = width // TILE // 2
    return pl.pallas_call(
        ordered(
            functools.partial(backward_kernel, size, partners, opens, closes),
            24 + partners + len(carried),
            kept + deps,
        ),
        grid=(some,),
        in_specs=[
            rows, rows, rows, rows, rows, two, two,
            pl.BlockSpec((8, tile), lambda g: (0, begin + g)),
            column(0), column(1), column(2),
            full(first_t.shape), full(att.shape),
            pl.BlockSpec((length, tile), lambda g: (0, begin + g)),
            full((tile, tile)),
            full(angle.shape), full(seg.shape),
            full(tok.shape), full(cot.shape), full(d_second.shape), full(vec.shape),
        ]
        + [packed] * partners
        + [full(gates.shape), full(up_bias.shape), pl.BlockSpec(memory_space=pltpu.SMEM)]
        + [full(x.shape) for x in carried]
        + unused(kept + deps),
        out_specs=[
            pl.BlockSpec((count, 4, TILE, tile), lambda g: (0, 0, 0, begin + g)),
            pl.BlockSpec((count, 4, TILE, tile), lambda g: (0, 0, 0, begin + g)),
            full((16, width)),
            full((width, length)),
            full(tok.shape),
        ][: 4 + closes],
        out_shape=[
            jax.ShapeDtypeStruct((count, 4, TILE, width), F32),
            jax.ShapeDtypeStruct((count, 4, TILE, width), F32),
            jax.ShapeDtypeStruct((16, width), F32),
            jax.ShapeDtypeStruct((width, length), F32),
            jax.ShapeDtypeStruct(tok.shape, B16),
        ][: 4 + closes],
        input_output_aliases={24 + partners + len(carried) + k: k for k in range(len(kept))},
        compiler_params=params(20 * MIB),
        cost_estimate=FREE,
        name="backward",
    )(dq, dk, dv, k_feat, v_low, scaled, expo, vec, in_weight, in_weight, in_weight, first_t,
      att, cot, proj, angle, seg, tok, cot, d_second, vec, *came, gates, up_bias, bits, *carried, *kept, *deps)


def per_device(
    tokens,
    segment_ids,
    span_starts,
    first_gain,
    first_shift,
    second_gain,
    second_shift,
    input_weight,
    input_bias,
    feature_freq,
    feature_weight,
    output_weight,
    output_bias,
    up_weight,
    up_bias,
    down_weight,
    down_bias,
    cotangent,
):
    seq_count, length, width = tokens.shape
    assert seq_count == 1
    heads, size = feature_weight.shape
    tok, cot = tokens[0], cotangent[0]
    seqs, batches = lax.axis_size("seq"), lax.axis_size("batch")
    place = lax.axis_index("seq").reshape(1)
    seg = segment_ids.reshape(1, length)
    seg_col = segment_ids.reshape(length, 1)
    start = span_starts[0, :1]
    small = (
        first_gain, first_shift, second_gain, second_shift, input_bias,
        feature_weight, up_bias,
    )
    first_t, second, second_t, proj, proj_t, angle, vec, up_bias_row = norms(
        place * length, tok, small, feature_freq
    )
    active, d_hidden, down_grad, up_bias_grad = mlp_part(
        second, cot, up_weight, up_bias_row, down_weight, 512
    )
    down_sum = lax.psum(down_grad, AXES)
    core = bit_groups()[0][0]
    bits = device_bits()
    up_shapes = [(TILE, up_weight.shape[1])]
    attn_shapes = [(TILE, 3 * width), (TILE, width)]

    def rest(first_t, second_t, active, d_hidden):
        up_send = up_half(bits, core, False, second_t, d_hidden, [])
        up_keep = up_half(bits, core, True, second_t, d_hidden, [up_send])
        up = Reduction(bits, up_send, up_keep, 3)
        q_feat, k_feat, v_low, scaled, expo, summary = features(
            first_t, input_weight, vec, proj_t, angle, seg, start, size, [up_keep]
        )
        states = from_partners(summary)
        mlp_out, d_second = mlp_tail(active, d_hidden, up_weight, down_weight, [summary])
        last = up.scatter(0, [mlp_out] + states)
        groups = heads // GROUP
        att, dq, dk, dv, here, gates = attention(
            place, start, q_feat, k_feat, v_low, output_weight, cot, seg, seg_col, states, size,
            (0, groups), [], last,
        )
        later = from_partners(here)
        result = results(tok, att, output_weight, mlp_out, output_bias, down_bias, [])
        last = up.scatter(1, [result] + later)
        fixed = (
            dq, dk, dv, k_feat, v_low, scaled, expo, vec, input_weight, first_t, att, cot, proj,
            angle, seg, tok, d_second, later, gates, up_bias_grad, bits, size,
        )
        some = list(backward(*fixed, (0, groups - 1), [], last))
        last = up.scatter(2, some[:1])
        send, keep, small, _, tok_grad = backward(*fixed, (groups - 1, 1), some, last)
        attn = Reduction(bits, send, keep, 3, small.reshape(1, 2, 8, width))
        last = up.exchange([tok_grad])
        last = attn.scatter(0, last)
        last = attn.scatter(1, last)
        last = attn.scatter(2, last)
        last = attn.exchange(last)
        last = up.settle(last)
        last = up.gather(2, last)
        last = attn.settle(last)
        last = up.gather(1, last)
        last = attn.gather(2, last)
        last = up.gather(0, last)
        last = attn.gather(1, last)
        last = up.finish_own(move_up, up_shapes, last)
        last = attn.gather(0, last)
        last = attn.finish_own(move_attention, attn_shapes, last)
        (up_sum,) = up.finish(move_up, up_shapes, last)
        in_sum, out_sum = attn.finish(move_attention, attn_shapes, [up_sum])
        return result, tok_grad, up_sum, in_sum, out_sum, attn.small.reshape(16, width)

    def nothing(first_t, second_t, active, d_hidden):
        low = jnp.zeros(tok.shape, B16)
        return (
            low, low, jnp.zeros(up_weight.shape, F32), jnp.zeros(input_weight.shape, F32),
            jnp.zeros(output_weight.shape, F32), jnp.zeros((16, width), F32),
        )

    result, tok_grad, up_sum, in_sum, out_sum, sums = lax.cond(
        start[0] < 2, rest, nothing, first_t, second_t, active, d_hidden
    )
    return (
        result[None],
        tok_grad[None],
        sums[0],
        sums[1],
        sums[2],
        sums[3],
        in_sum,
        sums[5:8].reshape(-1),
        sums[8].reshape(heads, size),
        out_sum,
        sums[4],
        up_sum,
        sums[9 : 9 + up_weight.shape[1] // width].reshape(-1),
        down_sum,
        sums[4],
    )


def solution(mesh):
    in_specs = (
        P("batch", "seq", None),
        P("batch", "seq"),
        P("batch", "seq"),
        P(),
        P(),
        P(),
        P(),
        P(),
        P(),
        P(),
        P(),
        P(),
        P(),
        P(),
        P(),
        P(),
        P(),
        P("batch", "seq", None),
    )
    out_specs = (
        P("batch", "seq", None),
        P("batch", "seq", None),
        P(),
        P(),
        P(),
        P(),
        P(),
        P(),
        P(),
        P(),
        P(),
        P(),
        P(),
        P(),
        P(),
    )
    return jax.shard_map(
        per_device, mesh=mesh, in_specs=in_specs, out_specs=out_specs, check_vma=False
    )
```
